32 devices in a mesh: dp: 32 (over z, y, x, core).
Axes of the slice: x: 2, y: 2, z: 4, core: 2. Of those that a mesh axis runs over, the one named last changes fastest.
Arguments:
- attention_in: float32 [768, 1152], P('dp'), may hold values from -0.3125 to 0.3125
- attention_out: float32 [768, 384], P('dp'), may hold values from -1.25 to 1.25
- hidden_in: float32 [768, 1536], P('dp'), may hold values from -0.3125 to 0.3125
- hidden_out: float32 [3072, 384], P('dp'), may hold values from -0.15625 to 0.15625
- patch_weight: float32 [768, 384], P('dp'), may hold values from -0.21875 to 0.21875
- vector_rows: float32 [202, 384], replicated
- prototypes: float32 [1024, 384], P('dp'), may hold values from -6 to 6
- first_attention_in: float32 [768, 1152], P('dp'), may hold values from -7.6293945e-06 to 7.6293945e-06
- first_attention_out: float32 [768, 384], P('dp'), may hold values from -7.6293945e-06 to 7.6293945e-06
- first_hidden_in: float32 [768, 1536], P('dp'), may hold values from -7.6293945e-06 to 7.6293945e-06
- first_hidden_out: float32 [3072, 384], P('dp'), may hold values from -7.6293945e-06 to 7.6293945e-06
- first_patch_weight: float32 [768, 384], P('dp'), may hold values from -7.6293945e-06 to 7.6293945e-06
- first_vector_rows: float32 [202, 384], replicated, may hold values from -7.6293945e-06 to 7.6293945e-06
- first_prototypes: float32 [1024, 384], P('dp'), may hold values from -7.6293945e-06 to 7.6293945e-06
- second_attention_in: float32 [768, 1152], P('dp'), may hold values from 2.3230746e-14 to 9.2922984e-14
- second_attention_out: float32 [768, 384], P('dp'), may hold values from 2.3230746e-14 to 9.2922984e-14
- second_hidden_in: float32 [768, 1536], P('dp'), may hold values from 2.3230746e-14 to 9.2922984e-14
- second_hidden_out: float32 [3072, 384], P('dp'), may hold values from 2.3230746e-14 to 9.2922984e-14
- second_patch_weight: float32 [768, 384], P('dp'), may hold values from 2.3230746e-14 to 9.2922984e-14
- second_vector_rows: float32 [202, 384], replicated, may hold values from 2.3230746e-14 to 9.2922984e-14
- second_prototypes: float32 [1024, 384], P('dp'), may hold values from 2.3230746e-14 to 9.2922984e-14
- teacher_attention_in: bfloat16 [768, 1152], P('dp'), may hold values from -0.3125 to 0.3125
- teacher_attention_out: bfloat16 [768, 384], P('dp'), may hold values from -1.25 to 1.25
- teacher_hidden_in: bfloat16 [768, 1536], P('dp'), may hold values from -0.3125 to 0.3125
- teacher_hidden_out: bfloat16 [3072, 384], P('dp'), may hold values from -0.15625 to 0.15625
- teacher_patch_weight: bfloat16 [768, 384], P('dp'), may hold values from -0.21875 to 0.21875
- teacher_vector_rows: bfloat16 [202, 384], replicated
- teacher_prototypes: bfloat16 [1024, 384], P('dp'), may hold values from -6 to 6
- anchor_patches: bfloat16 [2, 96, 196, 768], P(None, 'dp'), may hold values from -6 to 6
- target_patches: bfloat16 [2, 96, 196, 768], P(None, 'dp'), may hold values from -6 to 6
- patch_keep: int32 [2, 96, 196], P(None, 'dp'), may hold values 0 or 1
- step_count: int32 [], replicated, may hold values from 2 to 20
Outputs:
- loss: float32 [], replicated
- grad_norm: float32 [], replicated
- new_attention_in: float32 [768, 1152], P('dp')
- new_attention_out: float32 [768, 384], P('dp')
- new_hidden_in: float32 [768, 1536], P('dp')
- new_hidden_out: float32 [3072, 384], P('dp')
- new_patch_weight: float32 [768, 384], P('dp')
- new_vector_rows: float32 [202, 384], replicated
- new_prototypes: float32 [1024, 384], P('dp')
- moment_attention_in: float32 [768, 1152], P('dp')
- moment_attention_out: float32 [768, 384], P('dp')
- moment_hidden_in: float32 [768, 1536], P('dp')
- moment_hidden_out: float32 [3072, 384], P('dp')
- moment_patch_weight: float32 [768, 384], P('dp')
- moment_vector_rows: float32 [202, 384], replicated
- moment_prototypes: float32 [1024, 384], P('dp')
- square_attention_in: float32 [768, 1152], P('dp')
- square_attention_out: float32 [768, 384], P('dp')
- square_hidden_in: float32 [768, 1536], P('dp')
- square_hidden_out: float32 [3072, 384], P('dp')
- square_patch_weight: float32 [768, 384], P('dp')
- square_vector_rows: float32 [202, 384], replicated
- square_prototypes: float32 [1024, 384], P('dp')
The draws below stay inside these ranges and needn't reach their ends.
Inputs may be any that keep to these rules, and one draw needn't show every extreme that they name: `patch_keep`: 1 keeps a patch in the student's view, 0 drops it.
All inputs are finite; a program needn't handle non-finite values. No bound on the sum of `patch_keep` on one device may be relied on, other than what follows from the above.
Results may differ from the reference program's by a relative error of at most 0.014.
Values may be sent and summed in bfloat16 or wider, within the bound.
No kernel may reach another device: no remote copies, remote signals or barrier semaphores. Data moves between devices by JAX's collectives and lax.ppermute only.
A program may use at most 256 MiB of HBM per device.

```python
import math
import jax
import jax.numpy as jnp
from jax import lax

D = 384
HEADS = 6
HEAD_DIM = 64
FF = 1536
PATCHES = 196
PATCH_DIM = 768
PROTOS = 1024
LAYERS = 2
MB = 2
SEQ = 197
IMAGES_MB = 96
VROWS = 202
PARAMS = 4304640


def vector_table(key):
    rows = jnp.arange(VROWS)[:, None]
    position = 0.5 * jax.random.normal(jax.random.fold_in(key, 1), (VROWS, D), jnp.float32)
    gains = 1.0 + 0.1 * jax.random.normal(jax.random.fold_in(key, 2), (VROWS, D), jnp.float32)
    gains = jnp.clip(gains, 0.6, 1.4)
    return jnp.where(rows < SEQ, position, gains)


def draw_vector_rows(key, part):
    return vector_table(jax.random.fold_in(key, 11))


def draw_teacher_vector_rows(key, part):
    return vector_table(jax.random.fold_in(key, 23)).astype(jnp.bfloat16)


def with_ends(result, stream_key, least, top_value):
    shape = result.shape
    spot = [jax.random.randint(jax.random.fold_in(stream_key, axis), (), 0, shape[axis]) for axis in range(len(shape))]
    result = result.at[tuple(spot)].set(least)
    longest = shape.index(max(shape))
    spot[longest] = (spot[longest] + 1) % shape[longest]
    return result.at[tuple(spot)].set(top_value)


def level_of(rng, dims, split, least, largest):
    def one(dim, shards_of):
        steps = jax.random.uniform(jax.random.fold_in(jax.random.fold_in(rng, 6), dim), (shards_of,), jnp.float32, least / len(split), largest / len(split))
        return jnp.repeat(jnp.exp(steps), dims[dim] // shards_of).reshape((-1,) + (1,) * (len(dims) - dim - 1))

    loudness = one(*split[0])
    for cut in split[1:]:
        loudness = loudness * one(*cut)
    return loudness


def gaussian(stream_key, extent, scale, bound, cuts=(), kind=jnp.bfloat16):
    factor_of = level_of(stream_key, extent, cuts, -0.22, 0.18) if cuts else 1.0
    array = jax.random.normal(stream_key, extent, jnp.float32) * scale * factor_of
    return jnp.minimum(jnp.maximum(array, -bound), bound).astype(kind)


def setup_inputs(seed: int = 0) -> dict:
    key_of = jax.random.split(jax.random.key(seed), 33)
    attention_in = gaussian(key_of[0], (LAYERS * D, 3 * D), D ** -0.5, 0.3125, ((0, 32),), jnp.float32)
    attention_out = gaussian(key_of[1], (LAYERS * D, D), (D // 16) ** -0.5, 1.25, ((0, 32),), jnp.float32)
    hidden_in = gaussian(key_of[2], (LAYERS * D, FF), D ** -0.5, 0.3125, ((0, 32),), jnp.float32)
    hidden_out = gaussian(key_of[3], (LAYERS * FF, D), FF ** -0.5, 0.15625, ((0, 32),), jnp.float32)
    patch_weight = gaussian(key_of[4], (PATCH_DIM, D), PATCH_DIM ** -0.5, 0.21875, ((0, 32),), jnp.float32)
    vector_rows = draw_vector_rows(jax.random.fold_in(key_of[32], 71), 0)
    prototypes = gaussian(key_of[6], (PROTOS, D), 1.0, 6.0, ((0, 32),), jnp.float32)
    first_attention_in = gaussian(key_of[7], (LAYERS * D, 3 * D), (0.00111 / PARAMS ** 0.5), 7.62939453125e-06, ((0, 32),), jnp.float32)
    first_attention_out = gaussian(key_of[8], (LAYERS * D, D), (0.00111 / PARAMS ** 0.5), 7.62939453125e-06, ((0, 32),), jnp.float32)
    first_hidden_in = gaussian(key_of[9], (LAYERS * D, FF), (0.00111 / PARAMS ** 0.5), 7.62939453125e-06, ((0, 32),), jnp.float32)
    first_hidden_out = gaussian(key_of[10], (LAYERS * FF, D), (0.00111 / PARAMS ** 0.5), 7.62939453125e-06, ((0, 32),), jnp.float32)
    first_patch_weight = gaussian(key_of[11], (PATCH_DIM, D), (0.00111 / PARAMS ** 0.5), 7.62939453125e-06, ((0, 32),), jnp.float32)
    first_vector_rows = gaussian(key_of[12], (VROWS, D), (0.00111 / PARAMS ** 0.5), 7.62939453125e-06, (), jnp.float32)
    first_prototypes = gaussian(key_of[13], (PROTOS, D), (0.00111 / PARAMS ** 0.5), 7.62939453125e-06, ((0, 32),), jnp.float32)
    second_attention_in = jnp.clip(jnp.exp(math.log(9.29229837607487e-14) - 1.3862944 * jax.random.uniform(key_of[14], (LAYERS * D, 3 * D), jnp.float32) ** level_of(key_of[14], (LAYERS * D, 3 * D), ((0, 32),), -0.2, 0.2)), 2.3230745940187175e-14, 9.29229837607487e-14)
    second_attention_out = jnp.clip(jnp.exp(math.log(9.29229837607487e-14) - 1.3862944 * jax.random.uniform(key_of[15], (LAYERS * D, D), jnp.float32) ** level_of(key_of[15], (LAYERS * D, D), ((0, 32),), -0.2, 0.2)), 2.3230745940187175e-14, 9.29229837607487e-14)
    second_hidden_in = jnp.clip(jnp.exp(math.log(9.29229837607487e-14) - 1.3862944 * jax.random.uniform(key_of[16], (LAYERS * D, FF), jnp.float32) ** level_of(key_of[16], (LAYERS * D, FF), ((0, 32),), -0.2, 0.2)), 2.3230745940187175e-14, 9.29229837607487e-14)
    second_hidden_out = jnp.clip(jnp.exp(math.log(9.29229837607487e-14) - 1.3862944 * jax.random.uniform(key_of[17], (LAYERS * FF, D), jnp.float32) ** level_of(key_of[17], (LAYERS * FF, D), ((0, 32),), -0.2, 0.2)), 2.3230745940187175e-14, 9.29229837607487e-14)
    second_patch_weight = jnp.clip(jnp.exp(math.log(9.29229837607487e-14) - 1.3862944 * jax.random.uniform(key_of[18], (PATCH_DIM, D), jnp.float32) ** level_of(key_of[18], (PATCH_DIM, D), ((0, 32),), -0.2, 0.2)), 2.3230745940187175e-14, 9.29229837607487e-14)
    second_vector_rows = jnp.clip(jnp.exp(jax.random.uniform(key_of[19], (VROWS, D), jnp.float32, math.log(2.3230745940187175e-14), math.log(9.29229837607487e-14))), 2.3230745940187175e-14, 9.29229837607487e-14)
    second_prototypes = jnp.clip(jnp.exp(math.log(9.29229837607487e-14) - 1.3862944 * jax.random.uniform(key_of[20], (PROTOS, D), jnp.float32) ** level_of(key_of[20], (PROTOS, D), ((0, 32),), -0.2, 0.2)), 2.3230745940187175e-14, 9.29229837607487e-14)
    teacher_attention_in = gaussian(key_of[21], (LAYERS * D, 3 * D), D ** -0.5, 0.3125, ((0, 32),))
    teacher_attention_out = gaussian(key_of[22], (LAYERS * D, D), (D // 16) ** -0.5, 1.25, ((0, 32),))
    teacher_hidden_in = gaussian(key_of[23], (LAYERS * D, FF), D ** -0.5, 0.3125, ((0, 32),))
    teacher_hidden_out = gaussian(key_of[24], (LAYERS * FF, D), FF ** -0.5, 0.15625, ((0, 32),))
    teacher_patch_weight = gaussian(key_of[25], (PATCH_DIM, D), PATCH_DIM ** -0.5, 0.21875, ((0, 32),))
    teacher_vector_rows = draw_teacher_vector_rows(jax.random.fold_in(key_of[32], 71), 0)
    teacher_prototypes = gaussian(key_of[27], (PROTOS, D), 1.0, 6.0, ((0, 32),))
    anchor_patches = gaussian(key_of[28], (MB, IMAGES_MB, PATCHES, PATCH_DIM), 1.0, 6.0, ((1, 32),))
    target_patches = gaussian(key_of[29], (MB, IMAGES_MB, PATCHES, PATCH_DIM), 1.0, 6.0, ((1, 32),))
    patch_keep = with_ends((jax.random.randint(key_of[30], (MB, IMAGES_MB, PATCHES), 0, 5) < 3).astype(jnp.int32), jax.random.fold_in(key_of[30], 1), 0, 1)
    step_count = jax.random.randint(key_of[31], (), 2, 21).astype(jnp.int32)
    return {"attention_in": attention_in, "attention_out": attention_out, "hidden_in": hidden_in, "hidden_out": hidden_out, "patch_weight": patch_weight, "vector_rows": vector_rows, "prototypes": prototypes, "first_attention_in": first_attention_in, "first_attention_out": first_attention_out, "first_hidden_in": first_hidden_in, "first_hidden_out": first_hidden_out, "first_patch_weight": first_patch_weight, "first_vector_rows": first_vector_rows, "first_prototypes": first_prototypes, "second_attention_in": second_attention_in, "second_attention_out": second_attention_out, "second_hidden_in": second_hidden_in, "second_hidden_out": second_hidden_out, "second_patch_weight": second_patch_weight, "second_vector_rows": second_vector_rows, "second_prototypes": second_prototypes, "teacher_attention_in": teacher_attention_in, "teacher_attention_out": teacher_attention_out, "teacher_hidden_in": teacher_hidden_in, "teacher_hidden_out": teacher_hidden_out, "teacher_patch_weight": teacher_patch_weight, "teacher_vector_rows": teacher_vector_rows, "teacher_prototypes": teacher_prototypes, "anchor_patches": anchor_patches, "target_patches": target_patches, "patch_keep": patch_keep, "step_count": step_count}


@jax.custom_vjp
def low(v):
    return lax.optimization_barrier(v.astype(jnp.bfloat16)).astype(jnp.float32)

@jax.custom_vjp
def low_back(v):
    return v

def low_keep(v):
    return (low(v), None)

def low_pass(kept, grad):
    return (grad,)

def back_keep(v):
    return (v, None)

def back_low(kept, grad):
    return (low(grad),)
low.defvjp(low_keep, low_pass)
low_back.defvjp(back_keep, back_low)
highest = lax.Precision.HIGHEST
student_softness = 0.04
teacher_sharpness = 0.02
clip_limit = 0.01
matrix_rate = 0.05
table_rate = 0.4
decay_rate = 0.05
beta_one = 0.9
beta_two = 0.999
adam_floor = 1e-08

def layer_norm(values, gain):
    centre = values - lax.optimization_barrier(jnp.mean(values, -1, keepdims=True))
    spread = lax.optimization_barrier(jnp.mean(centre * centre, -1, keepdims=True))
    return centre * lax.rsqrt(spread + 1e-06) * gain

def unit_rows(values):
    return values * lax.rsqrt(lax.optimization_barrier(jnp.sum(values * values, -1, keepdims=True)) + 1e-06)

def encode(weights, vector_rows, patches, keep):
    attention_in, attention_out, hidden_in, hidden_out, patch_weight = weights
    count = patches.shape[0]
    pixels = patches.astype(jnp.float32)
    embedded = low_back(jnp.einsum('bpc,cd->bpd', pixels, patch_weight, precision=highest))
    head_row = jnp.broadcast_to(vector_rows[0], (count, 1, D))
    state = jnp.concatenate([head_row, embedded + vector_rows[1:SEQ]], 1)
    valid = jnp.concatenate([jnp.ones((count, 1), jnp.int32), keep], 1)[:, None, None, :] > 0
    scale = HEAD_DIM ** (-0.5)
    for layer in range(LAYERS):
        mix_weight = attention_in[layer * D:(layer + 1) * D]
        out_weight = attention_out[layer * D:(layer + 1) * D]
        up_weight = hidden_in[layer * D:(layer + 1) * D]
        down_weight = hidden_out[layer * FF:(layer + 1) * FF]
        normed = low(layer_norm(state, vector_rows[SEQ + 2 * layer]))
        mixed = low(low_back(jnp.einsum('bsd,de->bse', normed, mix_weight, precision=highest)))
        query = mixed[..., :D].reshape(count, SEQ, HEADS, HEAD_DIM)
        keys = mixed[..., D:2 * D].reshape(count, SEQ, HEADS, HEAD_DIM)
        values = mixed[..., 2 * D:].reshape(count, SEQ, HEADS, HEAD_DIM)
        scores = jnp.einsum('bqhd,bkhd->bhqk', query, keys, precision=highest) * scale
        scores = low_back(jnp.where(valid, scores, -1000000000.0))
        shares = low(jax.nn.softmax(scores, -1))
        attended = jnp.einsum('bhqk,bkhd->bqhd', shares, values, precision=highest).reshape(count, SEQ, D)
        attended = low(low_back(attended))
        state = state + low_back(jnp.einsum('bsd,de->bse', attended, out_weight, precision=highest))
        normed_two = low(layer_norm(state, vector_rows[SEQ + 2 * layer + 1]))
        expanded = low_back(jnp.einsum('bsd,df->bsf', normed_two, up_weight, precision=highest))
        activated = low(jax.nn.gelu(expanded))
        state = state + low_back(jnp.einsum('bsf,fd->bsd', activated, down_weight, precision=highest))
    return layer_norm(state[:, 0], vector_rows[SEQ + 2 * LAYERS])

def encode_all(weights, vector_rows, patches, keep):
    block = 16
    shaped_patches = patches.reshape(IMAGES_MB // block, block, PATCHES, PATCH_DIM)
    shaped_keep = keep.reshape(IMAGES_MB // block, block, PATCHES)
    run = jax.checkpoint(lambda pair: encode(weights, vector_rows, pair[0], pair[1]))
    return lax.map(run, (shaped_patches, shaped_keep)).reshape(IMAGES_MB, D)

def unscaled_logits(step_report, prototypes):
    unit_low = low(unit_rows(step_report))
    proto_low = low(unit_rows(prototypes))
    return low_back(jnp.dot(unit_low, proto_low.T, precision=highest))

def step_loss(params, targets, anchor_patches, patch_keep):
    weights = tuple((low(w) for w in params[:5]))
    vector_rows = params[5]
    prototypes = low(params[6])
    total = jnp.float32(0.0)
    for batch in range(MB):
        step_report = encode_all(weights, vector_rows, anchor_patches[batch], patch_keep[batch])
        log_probability = jax.nn.log_softmax(unscaled_logits(step_report, prototypes) / student_softness, -1)
        cross = -jnp.sum(targets[batch] * log_probability) / IMAGES_MB
        mean_share = lax.optimization_barrier(jnp.mean(jnp.exp(log_probability), 0))
        total = total + (cross + jnp.sum(mean_share * jnp.log(mean_share))) / MB
    return total

def reference(attention_in, attention_out, hidden_in, hidden_out, patch_weight, vector_rows, prototypes, first_attention_in, first_attention_out, first_hidden_in, first_hidden_out, first_patch_weight, first_vector_rows, first_prototypes, second_attention_in, second_attention_out, second_hidden_in, second_hidden_out, second_patch_weight, second_vector_rows, second_prototypes, teacher_attention_in, teacher_attention_out, teacher_hidden_in, teacher_hidden_out, teacher_patch_weight, teacher_vector_rows, teacher_prototypes, anchor_patches, target_patches, patch_keep, step_count):
    masters = (attention_in, attention_out, hidden_in, hidden_out, patch_weight, vector_rows, prototypes)
    firsts = (first_attention_in, first_attention_out, first_hidden_in, first_hidden_out, first_patch_weight, first_vector_rows, first_prototypes)
    seconds = (second_attention_in, second_attention_out, second_hidden_in, second_hidden_out, second_patch_weight, second_vector_rows, second_prototypes)
    rates = (matrix_rate, matrix_rate, matrix_rate, matrix_rate, matrix_rate, table_rate, table_rate)
    teacher = tuple((w.astype(jnp.float32) for w in (teacher_attention_in, teacher_attention_out, teacher_hidden_in, teacher_hidden_out, teacher_patch_weight)))
    teacher_rows = teacher_vector_rows.astype(jnp.float32)
    teacher_anchor_vectors = teacher_prototypes.astype(jnp.float32)
    all_keep = jnp.ones((IMAGES_MB, PATCHES), jnp.int32)
    target_entries = []
    for batch in range(MB):
        step_report = encode_all(teacher, teacher_rows, target_patches[batch], all_keep)
        target_entries.append(jax.nn.softmax(unscaled_logits(step_report, teacher_anchor_vectors) / teacher_sharpness, -1))
    targets = jnp.stack(target_entries)
    loss, pull = jax.vjp(lambda p: step_loss(p, targets, anchor_patches, patch_keep), masters)
    grads = pull(jnp.float32(1.0))[0]
    squares = jnp.float32(0.0)
    for gradient in grads:
        squares = squares + jnp.sum(gradient * gradient)
    grad_norm = jnp.sqrt(squares)
    factor = jnp.minimum(1.0, clip_limit / (grad_norm + 1e-06))
    counter = step_count.astype(jnp.float32)
    fix_one = 1.0 - beta_one ** counter
    fix_two = 1.0 - beta_two ** counter
    news, moments, squared = ([], [], [])
    for weight, first, second, gradient, rate in zip(masters, firsts, seconds, grads, rates):
        clipped = gradient * factor
        moment = beta_one * first + (1.0 - beta_one) * clipped
        square = beta_two * second + (1.0 - beta_two) * clipped * clipped
        stepped = moment / fix_one / (jnp.sqrt(square / fix_two) + adam_floor)
        news.append(weight - rate * (stepped + decay_rate * weight))
        moments.append(moment)
        squared.append(square)
    return (loss, grad_norm, news[0], news[1], news[2], news[3], news[4], news[5], news[6], moments[0], moments[1], moments[2], moments[3], moments[4], moments[5], moments[6], squared[0], squared[1], squared[2], squared[3], squared[4], squared[5], squared[6])
```

```python
import jax
import jax.numpy as jnp
from jax import lax
from jax.experimental import pallas as pl
from jax.experimental.pallas import tpu as pltpu
from jax.sharding import PartitionSpec as P

D = 384
HEADS = 6
HEAD_DIM = 64
FF = 1536
PATCHES = 196
PATCH_DIM = 768
PROTOS = 1024
SEQ = 197
VROWS = 202
ROWS = 208
CLS = 196
CR = 16
SCALE = HEAD_DIM ** (-0.5)

student_softness = 0.04
teacher_sharpness = 0.02
clip_limit = 0.01
matrix_rate = 0.05
table_rate = 0.4
decay_rate = 0.05
beta_one = 0.9
beta_two = 0.999
adam_floor = 1e-08

f32 = jnp.float32
bf16 = jnp.bfloat16
GELU_C = 0.7978845608028654
GELU_A = 0.044715


def dot(a, b):
    return lax.dot_general(a, b, (((1,), (0,)), ((), ())), preferred_element_type=f32)


def dot_bt(a, b):
    return lax.dot_general(a, b, (((1,), (1,)), ((), ())), preferred_element_type=f32)


def dot_at(a, b):
    return lax.dot_general(a, b, (((0,), (0,)), ((), ())), preferred_element_type=f32)


def normalize(x):
    centre = x - jnp.sum(x, -1, keepdims=True) * (1.0 / D)
    spread = jnp.sum(centre * centre, -1, keepdims=True) * (1.0 / D)
    inverse = lax.rsqrt(spread + 1e-06)
    return centre * inverse, inverse


def norm_back(hat, inverse, gain, upstream):
    gain_slope = jnp.sum(upstream * hat, 0, keepdims=True)
    scaled = upstream * gain
    mean_one = jnp.sum(scaled, -1, keepdims=True) * (1.0 / D)
    mean_two = jnp.sum(scaled * hat, -1, keepdims=True) * (1.0 / D)
    return inverse * (scaled - mean_one - hat * mean_two), gain_slope


def gelu_parts(x, slope):
    square = x * x
    t = jnp.tanh(x * (GELU_C + (GELU_C * GELU_A) * square))
    half = 0.5 + 0.5 * t
    act = x * half
    if not slope:
        return act, None
    inner = GELU_C + (3.0 * GELU_C * GELU_A) * square
    return act, half + act * (1.0 - t) * inner


def half_masks():
    lane = lax.broadcasted_iota(jnp.int32, (1, 128), 1)
    first = jnp.where(lane < HEAD_DIM, 1.0, 0.0)
    return first.astype(bf16), (1.0 - first).astype(bf16)


def head_mask():
    row = lax.broadcasted_iota(jnp.int32, (CR, D), 0)
    lane = lax.broadcasted_iota(jnp.int32, (CR, D), 1)
    low = row * HEAD_DIM
    return jnp.where(jnp.logical_and(lane >= low, lane < low + HEAD_DIM), 1.0, 0.0)


def forward_kernel(save, group, *refs):
    (pat, tab, bias, wp, win, wo, w1, w2, gains), refs = refs[:9], refs[9:]
    if save:
        out, first, mix, share, att, mid, act, dgelu = refs
    else:
        out, first, mix, att = refs
        share = mid = act = dgelu = None
    table = tab[...]
    for g in range(group):
        embedded = dot(pat[g], wp[...])
        first[pl.ds(g * ROWS, PATCHES), :] = embedded + table[:PATCHES]
        first[pl.ds(g * ROWS + PATCHES, ROWS - PATCHES), :] = table[PATCHES:]
    state = first[...]
    hat, _ = normalize(state)
    normed = (hat * gains[0:1, :]).astype(bf16)
    mix[...] = dot(normed, win[...]).astype(bf16)
    masks = half_masks()

    for g in range(group):
        rows = pl.ds(g * ROWS, ROWS)
        bias_row = bias[g]
        for pair in range(HEADS // 2):
            query = mix[rows, pl.ds(128 * pair, 128)] * jnp.asarray(SCALE, bf16)
            keys = mix[rows, pl.ds(D + 128 * pair, 128)]
            values = mix[rows, pl.ds(2 * D + 128 * pair, 128)]
            total = None
            for half in range(2):
                scores = dot_bt(query, keys * masks[half]) + bias_row
                top = jnp.max(scores, -1, keepdims=True)
                e = jnp.exp(scores - top)
                p = (e * (1.0 / jnp.sum(e, -1, keepdims=True))).astype(bf16)
                if save:
                    share[g, 2 * pair + half] = p
                o = dot(p, values * masks[half])
                total = o if total is None else total + o
            att[rows, pl.ds(128 * pair, 128)] = total.astype(bf16)
    middle = first[...] + dot(att[...], wo[...])
    if save:
        mid[...] = middle
    hat, _ = normalize(middle)
    normed = (hat * gains[1:2, :]).astype(bf16)
    result = middle
    for j in range(FF // D):
        cols = pl.ds(D * j, D)
        a, slope = gelu_parts(dot(normed, w1[:, cols]), save)
        a = a.astype(bf16)
        if save:
            act[:, cols] = a
            dgelu[:, cols] = slope.astype(bf16)
        result = result + dot(a, w2[cols, :])
    out[...] = result


def constant(shape, *index):
    return pl.BlockSpec(shape, lambda i: index, pipeline_mode=pl.Buffered(1))


def layer_zero(patches, table, bias, net, gains, save, group):
    count = patches.shape[0]
    weights = [net["patch"], net["mix", 0], net["out", 0], net["up", 0], net["down", 0]]
    rows = count * ROWS
    step = group * ROWS
    row_block = lambda cols: pl.BlockSpec((step, cols), lambda i: (i, 0))
    in_specs = [
        pl.BlockSpec((group, PATCHES, PATCH_DIM), lambda i: (i, 0, 0)),
        constant((ROWS, D), 0, 0),
        pl.BlockSpec((group, 1, ROWS), lambda i: (i, 0, 0)),
        *(spec for _, spec in weights),
        constant((8, D), 0, 0),
    ]
    out_shape = [jax.ShapeDtypeStruct((rows, D), f32)]
    out_specs = [row_block(D)]
    scratch = []
    if save:
        out_shape += [
            jax.ShapeDtypeStruct((rows, D), f32),
            jax.ShapeDtypeStruct((rows, 3 * D), bf16),
            jax.ShapeDtypeStruct((count, HEADS, ROWS, ROWS), bf16),
            jax.ShapeDtypeStruct((rows, D), bf16),
            jax.ShapeDtypeStruct((rows, D), f32),
            jax.ShapeDtypeStruct((rows, FF), bf16),
            jax.ShapeDtypeStruct((rows, FF), bf16),
        ]
        out_specs += [
            row_block(D),
            row_block(3 * D),
            pl.BlockSpec((group, HEADS, ROWS, ROWS), lambda i: (i, 0, 0, 0)),
            row_block(D),
            row_block(D),
            row_block(FF),
            row_block(FF),
        ]
    else:
        scratch = [
            pltpu.VMEM((step, D), f32),
            pltpu.VMEM((step, 3 * D), bf16),
            pltpu.VMEM((step, D), bf16),
        ]
    return pl.pallas_call(
        lambda *refs: forward_kernel(save, group, *refs),
        grid=(count // group,),
        in_specs=in_specs,
        out_specs=out_specs,
        out_shape=out_shape,
        scratch_shapes=scratch,
        compiler_params=pltpu.CompilerParams(
            dimension_semantics=("arbitrary",), vmem_limit_bytes=58 * 1024 * 1024
        ),
        name="student_layer_zero" if save else "teacher_layer_zero",
    )(patches, table, bias, *(w for w, _ in weights), gains)


def unit_parts(v):
    inverse = lax.rsqrt(jnp.sum(v * v, -1, keepdims=True) + 1e-06)
    return v * inverse, inverse


def class_kernel(student, count, *refs):
    (state, bias, win, wo, w1, w2, gains, protos), refs = refs[:8], refs[8:]
    if student:
        (logs, sums, kv, queries, shares, att, mid_c, expanded_out, last, cls), refs = refs[:10], refs[10:]
    else:
        (target,), (kv, att, cls) = refs[:1], refs[1:]
    hat, _ = normalize(state[...])
    normed = (hat * gains[0:1, :]).astype(bf16)
    kv[...] = dot(normed, win[:, D:]).astype(bf16)
    cls[...] = jnp.zeros((CR, D), f32)
    for g in range(count):
        cls[g : g + 1, :] = state[pl.ds(g * ROWS + CLS, 1), :]
    class_state = cls[...]
    hat, _ = normalize(class_state)
    query = dot((hat * gains[0:1, :]).astype(bf16), win[:, :D]).astype(bf16)
    if student:
        queries[...] = query
    mask = head_mask()
    for g in range(count):
        rows = pl.ds(g * ROWS, ROWS)
        spread = (jnp.broadcast_to(query[g : g + 1, :].astype(f32) * SCALE, (CR, D)) * mask).astype(bf16)
        scores = dot_bt(spread, kv[rows, pl.ds(0, D)]) + bias[g]
        e = jnp.exp(scores - jnp.max(scores, -1, keepdims=True))
        p = e * (1.0 / jnp.sum(e, -1, keepdims=True))
        if student:
            shares[g] = p
        o = dot(p.astype(bf16), kv[rows, pl.ds(D, D)])
        att[g : g + 1, :] = jnp.sum(o * mask, 0, keepdims=True)
    att[count:, :] = jnp.zeros((CR - count, D), f32)
    middle = class_state + dot(att[...].astype(bf16), wo[...])
    hat, _ = normalize(middle)
    expanded = dot((hat * gains[1:2, :]).astype(bf16), w1[...])
    act, _ = gelu_parts(expanded, False)
    result = middle + dot(act.astype(bf16), w2[...])
    if student:
        mid_c[...] = middle
        expanded_out[...] = expanded
        last[...] = result
    hat, _ = normalize(result)
    unit, _ = unit_parts(hat * gains[2:3, :])
    proto_unit, _ = unit_parts(protos[...].astype(f32))
    raw = dot_bt(unit.astype(bf16), proto_unit.astype(bf16))
    logits = raw * (1.0 / (student_softness if student else teacher_sharpness))
    logits = logits - jnp.max(logits, -1, keepdims=True)
    e = jnp.exp(logits)
    total = jnp.sum(e, -1, keepdims=True)
    if student:
        log_share = logits - jnp.log(total)
        logs[...] = log_share
        share = jnp.exp(log_share)
        row = lax.broadcasted_iota(jnp.int32, (CR, PROTOS), 0)
        sums[...] = jnp.zeros((8, PROTOS), f32)
        per = count // 2
        for m in range(2):
            inside = jnp.logical_and(row >= m * per, row < (m + 1) * per)
            sums[m : m + 1, :] = jnp.sum(jnp.where(inside, share, 0.0), 0, keepdims=True)
    else:
        target[...] = e / total


def whole():
    return pl.BlockSpec(memory_space=pltpu.VMEM)


def layer_one(state, bias, net, gains, student):
    count = bias.shape[0]
    weights = [net["mix", 1], net["out", 1], net["up", 1], net["down", 1]]
    protos, protos_spec = net["protos"]
    rows = count * ROWS
    if student:
        out_shape = [
            jax.ShapeDtypeStruct((CR, PROTOS), f32),
            jax.ShapeDtypeStruct((8, PROTOS), f32),
            jax.ShapeDtypeStruct((rows, 2 * D), bf16),
            jax.ShapeDtypeStruct((CR, D), bf16),
            jax.ShapeDtypeStruct((count, CR, ROWS), f32),
            jax.ShapeDtypeStruct((CR, D), f32),
            jax.ShapeDtypeStruct((CR, D), f32),
            jax.ShapeDtypeStruct((CR, FF), f32),
            jax.ShapeDtypeStruct((CR, D), f32),
            jax.ShapeDtypeStruct((CR, D), f32),
        ]
        scratch = []
    else:
        out_shape = [jax.ShapeDtypeStruct((CR, PROTOS), f32)]
        scratch = [
            pltpu.VMEM((rows, 2 * D), bf16),
            pltpu.VMEM((CR, D), f32),
            pltpu.VMEM((CR, D), f32),
        ]
    result = pl.pallas_call(
        lambda *refs: class_kernel(student, count, *refs),
        grid=(1,),
        in_specs=[whole()] * 2 + [spec for _, spec in weights] + [whole(), protos_spec],
        out_specs=[whole()] * len(out_shape),
        out_shape=out_shape,
        scratch_shapes=scratch,
        compiler_params=pltpu.CompilerParams(vmem_limit_bytes=58 * 1024 * 1024),
        name="student_layer_one" if student else "teacher_layer_one",
    )(state, bias, *(w for w, _ in weights), gains, protos)
    return result


def class_back_kernel(count, inverse_count, *refs):
    (logs, target, mean_sum, state, kv, queries, shares, att, mid_c, expanded, last, cls) = refs[:12]
    (win, wo, w1, w2, gains, protos) = refs[12:18]
    (delta, s_in, s_out, s_up, s_down, s_proto, s_gain, report, dkv, dq_all) = refs[18:]
    mask = head_mask()
    row = lax.broadcasted_iota(jnp.int32, (CR, 1), 0)
    live = row < count
    log_share = logs[...]
    share = jnp.exp(log_share)
    targets = target[...]
    mean_share = mean_sum[0:2, :] * (2.0 * inverse_count)
    log_mean = jnp.log(mean_share)
    cross = -jnp.sum(jnp.where(live, targets * log_share, 0.0), -1, keepdims=True)
    cross = jnp.sum(cross, 0, keepdims=True) * inverse_count
    entropy = jnp.sum(jnp.sum(mean_share * log_mean, -1, keepdims=True), 0, keepdims=True) * 0.5
    lane = lax.broadcasted_iota(jnp.int32, (8, 128), 1)
    report[...] = jnp.where(lane == 0, cross, jnp.where(lane == 1, entropy, 0.0))
    log_row = jnp.where(row < count // 2, log_mean[0:1, :], log_mean[1:2, :])
    slope = share - targets + share * (log_row - jnp.sum(share * log_row, -1, keepdims=True))
    slope = jnp.where(live, slope * (inverse_count / student_softness), 0.0).astype(bf16)
    hat_f, inv_f = normalize(last[...])
    summary = hat_f * gains[2:3, :]
    unit, inv_u = unit_parts(summary)
    proto = protos[...].astype(f32)
    proto_unit, inv_p = unit_parts(proto)
    d_unit = dot(slope, proto_unit.astype(bf16))
    d_proto = dot_at(slope, unit.astype(bf16))
    s_proto[...] = inv_p * (d_proto - proto_unit * jnp.sum(proto_unit * d_proto, -1, keepdims=True))
    d_summary = inv_u * (d_unit - unit * jnp.sum(unit * d_unit, -1, keepdims=True))
    d, gain_f = norm_back(hat_f, inv_f, gains[2:3, :], d_summary)
    s_gain[...] = jnp.zeros((8, D), f32)
    s_gain[2:3, :] = gain_f
    d_low = d.astype(bf16)
    act, gslope = gelu_parts(expanded[...], True)
    s_down[...] = dot_at(act.astype(bf16), d_low)
    d_exp = (dot_bt(d_low, w2[...]) * gslope).astype(bf16)
    hat_m, inv_m = normalize(mid_c[...])
    s_up[...] = dot_at((hat_m * gains[1:2, :]).astype(bf16), d_exp)
    d_mid, gain_two = norm_back(hat_m, inv_m, gains[1:2, :], dot_bt(d_exp, w1[...]))
    s_gain[1:2, :] = gain_two
    d_mid = d + d_mid
    d_mid_low = d_mid.astype(bf16)
    s_out[...] = dot_at(att[...].astype(bf16), d_mid_low)
    d_att = dot_bt(d_mid_low, wo[...]).astype(bf16)
    dq_all[...] = jnp.zeros((CR, D), f32)
    for g in range(count):
        rows = pl.ds(g * ROWS, ROWS)
        d_spread = (jnp.broadcast_to(d_att[g : g + 1, :].astype(f32), (CR, D)) * mask).astype(bf16)
        q_spread = (jnp.broadcast_to(queries[g : g + 1, :].astype(f32) * SCALE, (CR, D)) * mask).astype(bf16)
        p = shares[g]
        d_p = dot_bt(d_spread, kv[rows, pl.ds(D, D)])
        d_s = (p * (d_p - jnp.sum(p * d_p, -1, keepdims=True))).astype(bf16)
        dkv[rows, pl.ds(D, D)] = dot_at(p.astype(bf16), d_spread).astype(bf16)
        dkv[rows, pl.ds(0, D)] = dot_at(d_s, q_spread).astype(bf16)
        dq = dot(d_s, kv[rows, pl.ds(0, D)]) * mask
        dq_all[g : g + 1, :] = jnp.sum(dq, 0, keepdims=True) * SCALE
    dq_low = dq_all[...].astype(bf16)
    hat_c, _ = normalize(cls[...])
    s_in[:, :D] = dot_at((hat_c * gains[0:1, :]).astype(bf16), dq_low)
    hat, inv = normalize(state[...])
    s_in[:, D:] = dot_at((hat * gains[0:1, :]).astype(bf16), dkv[...])
    d_class = dot_bt(dq_low, win[:, :D])
    delta[...] = dot_bt(dkv[...], win[:, D:])
    for g in range(count):
        one = pl.ds(g * ROWS + CLS, 1)
        delta[one, :] = delta[one, :] + d_class[g : g + 1, :]
    d_state, gain_one = norm_back(hat, inv, gains[0:1, :], delta[...])
    s_gain[0:1, :] = gain_one
    delta[...] = d_state
    for g in range(count):
        one = pl.ds(g * ROWS + CLS, 1)
        delta[one, :] = delta[one, :] + d_mid[g : g + 1, :]


def layer_one_back(args, net, gains, inverse_count):
    count = args[6].shape[0]
    weights = [net["mix", 1], net["out", 1], net["up", 1], net["down", 1]]
    protos, protos_spec = net["protos"]
    rows = count * ROWS
    out_shape = [
        jax.ShapeDtypeStruct((rows, D), f32),
        jax.ShapeDtypeStruct((D, 3 * D), f32),
        jax.ShapeDtypeStruct((D, D), f32),
        jax.ShapeDtypeStruct((D, FF), f32),
        jax.ShapeDtypeStruct((FF, D), f32),
        jax.ShapeDtypeStruct((PROTOS, D), f32),
        jax.ShapeDtypeStruct((8, D), f32),
        jax.ShapeDtypeStruct((8, 128), f32),
    ]
    return pl.pallas_call(
        lambda *refs: class_back_kernel(count, inverse_count, *refs),
        grid=(1,),
        in_specs=[whole()] * 12 + [spec for _, spec in weights] + [whole(), protos_spec],
        out_specs=[whole()] * len(out_shape),
        out_shape=out_shape,
        scratch_shapes=[pltpu.VMEM((rows, 2 * D), bf16), pltpu.VMEM((CR, D), f32)],
        compiler_params=pltpu.CompilerParams(vmem_limit_bytes=58 * 1024 * 1024),
        name="layer_one_back",
    )(*args, *(w for w, _ in weights), gains, protos)


def add_to(ref, value, first):
    @pl.when(first)
    def _():
        ref[...] = value

    @pl.when(jnp.logical_not(first))
    def _():
        ref[...] = ref[...] + value


def mlp_back_kernel(group, delta, act, dgelu, mid, w1, w2, gains, d_mid, s_up, s_down, s_gain):
    first = pl.program_id(0) == 0

    @pl.when(first)
    def _():
        s_up[...] = jnp.zeros(s_up.shape, f32)
        s_down[...] = jnp.zeros(s_down.shape, f32)
        s_gain[...] = jnp.zeros(s_gain.shape, f32)

    d = delta[...]
    d_low = d.astype(bf16)
    hat, inv = normalize(mid[...])
    normed = (hat * gains[1:2, :]).astype(bf16)
    d_normed = None
    for j in range(FF // D):
        cols = pl.ds(D * j, D)
        s_down[cols, :] += dot_at(act[:, cols], d_low)
        d_exp = (dot_bt(d_low, w2[cols, :]) * dgelu[:, cols].astype(f32)).astype(bf16)
        s_up[:, cols] += dot_at(normed, d_exp)
        part = dot_bt(d_exp, w1[:, cols])
        d_normed = part if d_normed is None else d_normed + part
    back, gain = norm_back(hat, inv, gains[1:2, :], d_normed)
    s_gain[0:1, :] += gain
    d_mid[...] = d + back


def layer_zero_mlp_back(delta, act, dgelu, mid, net, gains, group):
    weights = [net["up", 0], net["down", 0]]
    rows = delta.shape[0]
    step = group * ROWS
    row_block = lambda cols: pl.BlockSpec((step, cols), lambda i: (i, 0))
    return pl.pallas_call(
        lambda *refs: mlp_back_kernel(group, *refs),
        grid=(rows // step,),
        in_specs=[
            row_block(D),
            row_block(FF),
            row_block(FF),
            row_block(D),
            *(spec for _, spec in weights),
            constant((8, D), 0, 0),
        ],
        out_specs=[
            row_block(D),
            pl.BlockSpec((D, FF), lambda i: (0, 0)),
            pl.BlockSpec((FF, D), lambda i: (0, 0)),
            pl.BlockSpec((8, D), lambda i: (0, 0)),
        ],
        out_shape=[
            jax.ShapeDtypeStruct((rows, D), f32),
            jax.ShapeDtypeStruct((D, FF), f32),
            jax.ShapeDtypeStruct((FF, D), f32),
            jax.ShapeDtypeStruct((8, D), f32),
        ],
        compiler_params=pltpu.CompilerParams(
            dimension_semantics=("arbitrary",), vmem_limit_bytes=58 * 1024 * 1024
        ),
        name="layer_zero_mlp_back",
    )(delta, act, dgelu, mid, *(w for w, _ in weights), gains)


def attention_back_kernel(group, *refs):
    (d_mid, state, mix, share, att, pat, win, wo, gains) = refs[:9]
    (s_in, s_out, s_patch, s_table, s_gain, d_att, dmix) = refs[9:]

    @pl.when(pl.program_id(0) == 0)
    def _():
        s_in[...] = jnp.zeros(s_in.shape, f32)
        s_out[...] = jnp.zeros(s_out.shape, f32)
        s_patch[...] = jnp.zeros(s_patch.shape, f32)
        s_table[...] = jnp.zeros(s_table.shape, f32)
        s_gain[...] = jnp.zeros(s_gain.shape, f32)

    d_low = d_mid[...].astype(bf16)
    s_out[...] += dot_at(att[...], d_low)
    d_att[...] = dot_bt(d_low, wo[...]).astype(bf16)
    masks = half_masks()
    for g in range(group):
        rows = pl.ds(g * ROWS, ROWS)
        for pair in range(HEADS // 2):
            lanes = [pl.ds(D * part + 128 * pair, 128) for part in range(3)]
            query = mix[rows, lanes[0]] * jnp.asarray(SCALE, bf16)
            keys = mix[rows, lanes[1]] * jnp.asarray(SCALE, bf16)
            values = mix[rows, lanes[2]]
            upstream = d_att[rows, lanes[0]]
            dq = dk = dv = None
            for half in range(2):
                p = share[g, 2 * pair + half]
                up = upstream * masks[half]
                d_p = dot_bt(up, values)
                p_wide = p.astype(f32)
                weighted = p_wide * d_p
                d_s = (weighted - p_wide * jnp.sum(weighted, -1, keepdims=True)).astype(bf16)
                parts = (
                    dot(d_s, keys * masks[half]),
                    dot_at(d_s, query * masks[half]),
                    dot_at(p, up),
                )
                dq, dk, dv = parts if dq is None else (dq + parts[0], dk + parts[1], dv + parts[2])
            dmix[rows, lanes[0]] = dq.astype(bf16)
            dmix[rows, lanes[1]] = dk.astype(bf16)
            dmix[rows, lanes[2]] = dv.astype(bf16)
    hat, inv = normalize(state[...])
    normed = (hat * gains[0:1, :]).astype(bf16)
    s_in[...] += dot_at(normed, dmix[...])
    back, gain = norm_back(hat, inv, gains[0:1, :], dot_bt(dmix[...], win[...]))
    s_gain[0:1, :] += gain
    d_state = d_mid[...] + back
    for g in range(group):
        one = d_state[g * ROWS : (g + 1) * ROWS]
        s_table[...] += one
        s_patch[...] += dot_at(pat[g], one[:PATCHES].astype(bf16))


def layer_zero_attention_back(d_mid, state, mix, share, att, patches, net, gains, group):
    weights = [net["mix", 0], net["out", 0]]
    rows = d_mid.shape[0]
    step = group * ROWS
    row_block = lambda cols: pl.BlockSpec((step, cols), lambda i: (i, 0))
    fixed = lambda *shape: pl.BlockSpec(shape, lambda i: (0, 0))
    return pl.pallas_call(
        lambda *refs: attention_back_kernel(group, *refs),
        grid=(rows // step,),
        in_specs=[
            row_block(D),
            row_block(D),
            row_block(3 * D),
            pl.BlockSpec((group, HEADS, ROWS, ROWS), lambda i: (i, 0, 0, 0)),
            row_block(D),
            pl.BlockSpec((group, PATCHES, PATCH_DIM), lambda i: (i, 0, 0)),
            *(spec for _, spec in weights),
            constant((8, D), 0, 0),
        ],
        out_specs=[fixed(D, 3 * D), fixed(D, D), fixed(PATCH_DIM, D), fixed(ROWS, D), fixed(8, D)],
        out_shape=[
            jax.ShapeDtypeStruct((D, 3 * D), f32),
            jax.ShapeDtypeStruct((D, D), f32),
            jax.ShapeDtypeStruct((PATCH_DIM, D), f32),
            jax.ShapeDtypeStruct((ROWS, D), f32),
            jax.ShapeDtypeStruct((8, D), f32),
        ],
        scratch_shapes=[pltpu.VMEM((step, D), bf16), pltpu.VMEM((step, 3 * D), bf16)],
        compiler_params=pltpu.CompilerParams(
            dimension_semantics=("arbitrary",), vmem_limit_bytes=58 * 1024 * 1024
        ),
        name="layer_zero_attention_back",
    )(d_mid, state, mix, share, att, patches, *(w for w, _ in weights), gains)


def pack_rows(shards):
    mix, out, up, down, patch, protos = shards
    r = mix.shape[0]
    down = jnp.concatenate([down[r * j : r * (j + 1)] for j in range(4)], 1)
    rest = protos[r:]
    rest = jnp.concatenate([rest[:, 128 * j : 128 * (j + 1)] for j in range(3)], 0)
    return mix, out, up, down, patch, protos[:r], rest


OFFSETS = (("up", 0, 1536), ("up", 1, 1536), ("out", 0, 384), ("mix", 0, 1152), ("mix", 1, 1152), ("out", 1, 384),
           ("patch", 0, 384), ("patch", 1, 384), ("down", 0, 1536), ("down", 1, 1536),
           ("protos", 0, 384), ("protos", 1, 384), ("rest", 0, 128), ("rest", 1, 128))


def gather_networks(student, teacher, n):
    names = ("mix", "out", "up", "down", "patch", "protos", "rest")
    packed = [dict(zip(names, pack_rows(shards))) for shards in (student, teacher)]
    whole_rows = jnp.concatenate([packed[net][name] for name, net, _ in OFFSETS], 1)
    full = lax.all_gather(whole_rows, "dp", axis=0, tiled=True)
    place, start = {}, 0
    for name, net, width in OFFSETS:
        place[name, net] = start
        start += width
    r = full.shape[0] // n
    nets = []
    for net in range(2):
        at = lambda name: place[name, net]
        down = full[:, at("down") : at("down") + FF].reshape(n, r, 4, D).transpose(0, 2, 1, 3).reshape(2 * FF, D)
        rest = full[:, at("rest") : at("rest") + 128].reshape(n, 3, r // 3, 128)
        rest = rest.transpose(0, 2, 1, 3).reshape(n, r // 3, D)
        protos = full[:, at("protos") : at("protos") + D].reshape(n, r, D)
        protos = jnp.concatenate([protos, rest], 1).reshape(PROTOS, D)
        result = {"patch": (full, constant((PATCH_DIM, D), 0, at("patch") // D)), "protos": (protos, constant((PROTOS, D), 0, 0))}
        for layer in range(2):
            result["mix", layer] = (full, constant((D, 3 * D), layer, at("mix") // (3 * D)))
            result["out", layer] = (full, constant((D, D), layer, at("out") // D))
            result["up", layer] = (full, constant((D, FF), layer, at("up") // FF))
            result["down", layer] = (down, constant((FF, D), layer, 0))
        nets.append(result)
    return nets


def small_sum(value, n):
    copies = jnp.broadcast_to(value[None], (n,) + value.shape)
    return jnp.sum(lax.all_to_all(copies, "dp", 0, 0, tiled=True), 0)


BITS = {"c": 0, "x": 1, "y": 2, "z": 3}
PATHS = (("c", "x", "y", "z"), ("c", "y", "z", "x"), ("c", "z", "x", "y"))


def pack_chunk(parts, path):
    order = PATHS[path]
    columns = parts[:, :, 128 * path : 128 * (path + 1)]
    rows = columns.shape[1]
    axes = [3 - BITS[name] for name in order]
    shaped = columns.reshape(2, 2, 2, 2, rows, 128)
    return shaped.transpose(*axes, 4, 5).reshape(16, rows, 128)


def swap(value, bit):
    size = lax.axis_size("dp")
    return lax.ppermute(value, "dp", [(i, i ^ (1 << bit)) for i in range(size)])


def scatter_chunk(arrays, me):
    arrays = list(arrays)
    for stage in range(4):
        sent, kept = [], []
        for path in range(3):
            bit = BITS[PATHS[path][stage]]
            mine = (me >> bit) & 1
            a = arrays[path]
            half = a.shape[0] // 2
            sent.append((lax.dynamic_slice_in_dim(a, (1 - mine) * half, half, 0), bit))
            kept.append(lax.dynamic_slice_in_dim(a, mine * half, half, 0))
        if stage == 0:
            joined = swap(jnp.stack([s for s, _ in sent]), 0)
            got = [joined[i] for i in range(3)]
        else:
            got = [swap(s, bit) for s, bit in sent]
        total = [k.astype(f32) + g.astype(f32) for k, g in zip(kept, got)]
        arrays = [t.astype(bf16) if stage < 3 else t for t in total]
    return [a[0] for a in arrays]


def last_stage(arrays, me, layer_rows):
    value = jnp.concatenate(arrays, 1)
    mine = me >> 4
    extra = (value.shape[0] - layer_rows) // 2
    keep = lax.dynamic_slice_in_dim(value, layer_rows + mine * extra, extra, 0)
    send = lax.dynamic_slice_in_dim(value, layer_rows + (1 - mine) * extra, extra, 0)
    if layer_rows:
        keep = jnp.concatenate([value[:layer_rows], keep], 0)
        send = jnp.concatenate([value[:layer_rows], send], 0)
    return keep + swap(send.astype(bf16), 4).astype(f32)


def blocks(value, owners):
    k, width = value.shape
    shaped = value.reshape(owners, k // owners, width // D, D).transpose(0, 2, 1, 3)
    return shaped.reshape(owners, -1, D)


def unblocks(value, width):
    rows = value.shape[0] // (width // D)
    return jnp.concatenate([value[rows * j : rows * (j + 1)] for j in range(width // D)], 1)


def wide_blocks(value):
    shaped = value.reshape(2, 16, -1, D)
    return shaped.transpose(1, 0, 2, 3).reshape(16, -1, D)


def reduce_gradients(one, zero_mlp, zero_rest, me, n):
    mix1, out1, up1, down1, protos = one
    up0, down0 = zero_mlp
    mix0, out0, patch, vectors = zero_rest
    if n != 32:
        scatter = lambda *v: lax.psum_scatter(jnp.concatenate(v, 0), "dp", scatter_dimension=0, tiled=True)
        return (scatter(mix0, mix1), scatter(out0, out1), scatter(up0, up1), scatter(down0, down1), scatter(patch), scatter(protos), scatter(vectors))
    chunks = []
    for layered, wide in (((mix1, out1, up1, down1), (protos,)), ((up0, down0), ()), ((mix0, out0), (patch, vectors))):
        layered = [blocks(v, 16) for v in layered]
        rows = sum(v.shape[1] for v in layered)
        wide = [v.reshape(2, 16, -1, D) for v in wide]
        wide = [wide_blocks(jnp.concatenate(wide, 2).reshape(-1, D))] if wide else []
        packed = jnp.concatenate(layered + wide, 1).astype(bf16)
        arrays = scatter_chunk([pack_chunk(packed, path) for path in range(3)], me)
        chunks.append(last_stage(arrays, me, rows))
    one, mlp, rest = chunks
    upper = (me >> 4) == 1
    pick = lambda a, b, width: unblocks(jnp.where(upper, a, b), width)
    mix = pick(one[0:72], rest[0:72], 3 * D)
    out = pick(one[72:96], rest[72:96], D)
    up = pick(one[96:192], mlp[0:96], FF)
    down = jnp.where(upper, one[192:288], mlp[96:192])
    return mix, out, up, down, rest[96:120], one[288:320], rest[120:128]


def local(
    attention_in, attention_out, hidden_in, hidden_out, patch_weight, vector_rows, prototypes,
    first_attention_in, first_attention_out, first_hidden_in, first_hidden_out, first_patch_weight, first_vector_rows, first_prototypes,
    second_attention_in, second_attention_out, second_hidden_in, second_hidden_out, second_patch_weight, second_vector_rows, second_prototypes,
    teacher_attention_in, teacher_attention_out, teacher_hidden_in, teacher_hidden_out, teacher_patch_weight, teacher_vector_rows, teacher_prototypes,
    anchor_patches, target_patches, patch_keep, step_count,
):
    n = lax.axis_size("dp")
    me = lax.axis_index("dp")
    groups, per = anchor_patches.shape[:2]
    count = groups * per
    inverse_count = 1.0 / (count * n)
    masters = (attention_in, attention_out, hidden_in, hidden_out, patch_weight, vector_rows, prototypes)
    firsts = (first_attention_in, first_attention_out, first_hidden_in, first_hidden_out, first_patch_weight, first_vector_rows, first_prototypes)
    seconds = (second_attention_in, second_attention_out, second_hidden_in, second_hidden_out, second_patch_weight, second_vector_rows, second_prototypes)
    student_shards = [w.astype(bf16) for w in (attention_in, attention_out, hidden_in, hidden_out, patch_weight, prototypes)]
    teacher_shards = [teacher_attention_in, teacher_attention_out, teacher_hidden_in, teacher_hidden_out, teacher_patch_weight, teacher_prototypes]
    student, teacher = gather_networks(student_shards, teacher_shards, n)

    def table_of(rows):
        return jnp.concatenate([rows[1:SEQ], rows[0:1], jnp.zeros((ROWS - SEQ, D), f32)], 0)

    def gains_of(rows):
        zeros = jnp.zeros((5, D), f32)
        first = jnp.concatenate([rows[SEQ : SEQ + 2], jnp.zeros((6, D), f32)], 0)
        second = jnp.concatenate([rows[SEQ + 2 : SEQ + 5], zeros], 0)
        return first, second

    keep = patch_keep.reshape(count, PATCHES)
    bias = jnp.where(keep == 1, 0.0, -1000000000.0).astype(f32)
    ends = jnp.where(jnp.arange(ROWS - PATCHES) == 0, 0.0, -1000000000.0).astype(f32)
    ends = jnp.broadcast_to(ends, (count, ROWS - PATCHES))
    bias = jnp.concatenate([bias, ends], 1)[:, None]
    plain = jnp.concatenate([jnp.zeros((count, PATCHES), f32), ends], 1)[:, None]
    anchor = anchor_patches.reshape(count, PATCHES, PATCH_DIM)
    target = target_patches.reshape(count, PATCHES, PATCH_DIM)
    gains0, gains1 = gains_of(vector_rows)
    teacher_rows = teacher_vector_rows.astype(f32)
    teacher_gains0, teacher_gains1 = gains_of(teacher_rows)

    state1, state0, mix, share, att, mid, act, dgelu = layer_zero(anchor, table_of(vector_rows), bias, student, gains0, True, GROUP)
    logs, sums, kv, queries, shares, att_c, mid_c, expanded, last, cls = layer_one(state1, bias, student, gains1, True)
    mean_sum = small_sum(sums, n)
    (teacher_state,) = layer_zero(target, table_of(teacher_rows), plain, teacher, teacher_gains0, False, GROUP)
    (targets,) = layer_one(teacher_state, plain, teacher, teacher_gains1, False)
    delta, mix1, out1, up1, down1, s_protos, gain1, report = layer_one_back(
        (logs, targets, mean_sum, state1, kv, queries, shares, att_c, mid_c, expanded, last, cls), student, gains1, inverse_count)
    d_mid, up0, down0, gain_two = layer_zero_mlp_back(delta, act, dgelu, mid, student, gains0, GROUP)
    mix0, out0, s_patch, s_table, gain_one = layer_zero_attention_back(d_mid, state0, mix, share, att, anchor, student, gains0, GROUP)
    vectors = jnp.concatenate([s_table, gain_one[0:1], gain_two[0:1], gain1[0:3], jnp.zeros((256 - ROWS - 5, D), f32)], 0)
    slopes = reduce_gradients((mix1, out1, up1, down1, s_protos), (up0, down0), (mix0, out0, s_patch, vectors), me, n)
    squares = sum(jnp.sum(s * s) for s in slopes)
    vector_rows_per = slopes[6].shape[0]
    line = jnp.zeros((1, D), f32).at[0, 0].set(squares).at[0, 1].set(report[0, 0])
    final = jnp.concatenate([slopes[6], line], 0)
    copies = jnp.broadcast_to(final[None], (n,) + final.shape)
    final = lax.all_to_all(copies, "dp", 0, 0, tiled=True)
    totals = jnp.sum(final[:, vector_rows_per], 0)
    vector_full = final[:, :vector_rows_per].reshape(256, D)
    vector_slope = jnp.concatenate([vector_full[CLS : CLS + 1], vector_full[:PATCHES], vector_full[ROWS : ROWS + 5]], 0)
    loss = totals[1] + report[0, 1]
    grad_norm = jnp.sqrt(totals[0])
    factor = jnp.minimum(1.0, clip_limit / (grad_norm + 1e-06))
    counter = step_count.astype(f32)
    fix_one = 1.0 - beta_one**counter
    fix_two = 1.0 - beta_two**counter
    slopes = slopes[:5] + (vector_slope, slopes[5])
    rates = (matrix_rate,) * 5 + (table_rate,) * 2
    news, moments, squared = ([], [], [])
    for weight, first, second, slope, rate in zip(masters, firsts, seconds, slopes, rates):
        clipped = slope * factor
        moment = beta_one * first + (1.0 - beta_one) * clipped
        square = beta_two * second + (1.0 - beta_two) * clipped * clipped
        stepped = moment / fix_one / (jnp.sqrt(square / fix_two) + adam_floor)
        news.append(weight - rate * (stepped + decay_rate * weight))
        moments.append(moment)
        squared.append(square)
    return (loss, grad_norm, *news, *moments, *squared)


GROUP = 2


def solution(mesh):
    rows, same, images = P("dp", None), P(), P(None, "dp", None, None)
    weights = (rows,) * 5 + (same, rows)
    return jax.shard_map(
        local,
        mesh=mesh,
        in_specs=weights * 4 + (images, images, P(None, "dp", None), same),
        out_specs=(same, same) + weights * 3,
        check_vma=False,
    )
```

```python
import jax
import jax.numpy as jnp
from jax import lax
from jax.experimental import pallas as pl
from jax.experimental.pallas import tpu as pltpu
from jax.sharding import PartitionSpec as P

D = 384
HEADS = 6
HEAD_DIM = 64
FF = 1536
PATCHES = 196
PATCH_DIM = 768
PROTOS = 1024
SEQ = 197
VROWS = 202
ROWS = 208
CLS = 196
CR = 16
SCALE = HEAD_DIM ** (-0.5)

student_softness = 0.04
teacher_sharpness = 0.02
clip_limit = 0.01
matrix_rate = 0.05
table_rate = 0.4
decay_rate = 0.05
beta_one = 0.9
beta_two = 0.999
adam_floor = 1e-08

f32 = jnp.float32
bf16 = jnp.bfloat16
GELU_C = 0.7978845608028654
GELU_A = 0.044715


def dot(a, b):
    return lax.dot_general(a, b, (((1,), (0,)), ((), ())), preferred_element_type=f32)


def dot_bt(a, b):
    return lax.dot_general(a, b, (((1,), (1,)), ((), ())), preferred_element_type=f32)


def dot_at(a, b):
    return lax.dot_general(a, b, (((0,), (0,)), ((), ())), preferred_element_type=f32)


def normalize(x):
    centre = x - jnp.sum(x, -1, keepdims=True) * (1.0 / D)
    spread = jnp.sum(centre * centre, -1, keepdims=True) * (1.0 / D)
    inverse = lax.rsqrt(spread + 1e-06)
    return centre * inverse, inverse


def norm_back(hat, inverse, gain, upstream):
    gain_slope = jnp.sum(upstream * hat, 0, keepdims=True)
    scaled = upstream * gain
    mean_one = jnp.sum(scaled, -1, keepdims=True) * (1.0 / D)
    mean_two = jnp.sum(scaled * hat, -1, keepdims=True) * (1.0 / D)
    return inverse * (scaled - mean_one - hat * mean_two), gain_slope


def gelu_parts(x, slope):
    square = x * x
    t = jnp.tanh(x * (GELU_C + (GELU_C * GELU_A) * square))
    half = 0.5 + 0.5 * t
    act = x * half
    if not slope:
        return act, None
    inner = GELU_C + (3.0 * GELU_C * GELU_A) * square
    return act, half + act * (1.0 - t) * inner


def half_masks():
    lane = lax.broadcasted_iota(jnp.int32, (1, 128), 1)
    first = jnp.where(lane < HEAD_DIM, 1.0, 0.0)
    return first.astype(bf16), (1.0 - first).astype(bf16)


def head_mask():
    row = lax.broadcasted_iota(jnp.int32, (CR, D), 0)
    lane = lax.broadcasted_iota(jnp.int32, (CR, D), 1)
    low = row * HEAD_DIM
    return jnp.where(jnp.logical_and(lane >= low, lane < low + HEAD_DIM), 1.0, 0.0)


def natural_down(ref, natural):
    for pair in range(8):
        rows = ref[pl.ds(48 * pair, 48), :].astype(f32)
        pieces = [rows[24 * b : 24 * (b + 1), D * j : D * (j + 1)] for b in range(2) for j in range(4)]
        natural[pl.ds(192 * pair, 192), :] = jnp.concatenate(pieces, 0).astype(bf16)


def natural_protos(ref, rest, natural):
    for pair in range(16):
        rows = ref[pl.ds(48 * pair, 48), :].astype(f32)
        tail = rest[pl.ds(48 * pair, 48), :].astype(f32)
        pieces = []
        for b in range(2):
            pieces.append(rows[24 * b : 24 * (b + 1)])
            pieces.append(jnp.concatenate([tail[24 * b + 8 * j : 24 * b + 8 * (j + 1)] for j in range(3)], 1))
        natural[pl.ds(64 * pair, 64), :] = jnp.concatenate(pieces, 0)


def forward_kernel(save, packed, group, *refs):
    (pat, tab, bias, wp, win, wo, w1, w2, gains), refs = refs[:9], refs[9:]
    if packed:
        refs, natural = refs[:-1], refs[-1]
        down_in = w2

        @pl.when(pl.program_id(0) == 0)
        def _():
            natural_down(down_in, natural)

        w2 = natural
    if save:
        out, first, mix, share, att, mid, act, dgelu = refs
    else:
        out, first, mix, att = refs
        share = mid = act = dgelu = None
    table = tab[...]
    for g in range(group):
        embedded = dot(pat[g], wp[...])
        first[pl.ds(g * ROWS, PATCHES), :] = embedded + table[:PATCHES]
        first[pl.ds(g * ROWS + PATCHES, ROWS - PATCHES), :] = table[PATCHES:]
    state = first[...]
    hat, _ = normalize(state)
    normed = (hat * gains[0:1, :]).astype(bf16)
    mix[...] = dot(normed, win[...]).astype(bf16)
    masks = half_masks()

    for g in range(group):
        rows = pl.ds(g * ROWS, ROWS)
        bias_row = bias[g]
        for pair in range(HEADS // 2):
            query = mix[rows, pl.ds(128 * pair, 128)] * jnp.asarray(SCALE, bf16)
            keys = mix[rows, pl.ds(D + 128 * pair, 128)]
            values = mix[rows, pl.ds(2 * D + 128 * pair, 128)]
            total = None
            for half in range(2):
                scores = dot_bt(query, keys * masks[half]) + bias_row
                top = jnp.max(scores, -1, keepdims=True)
                e = jnp.exp(scores - top)
                p = (e * (1.0 / jnp.sum(e, -1, keepdims=True))).astype(bf16)
                if save:
                    share[g, 2 * pair + half] = p
                o = dot(p, values * masks[half])
                total = o if total is None else total + o
            att[rows, pl.ds(128 * pair, 128)] = total.astype(bf16)
    middle = first[...] + dot(att[...], wo[...])
    if save:
        mid[...] = middle
    hat, _ = normalize(middle)
    normed = (hat * gains[1:2, :]).astype(bf16)
    result = middle
    for j in range(FF // D):
        cols = pl.ds(D * j, D)
        a, slope = gelu_parts(dot(normed, w1[:, cols]), save)
        a = a.astype(bf16)
        if save:
            act[:, cols] = a
            dgelu[:, cols] = slope.astype(bf16)
        result = result + dot(a, w2[cols, :])
    out[...] = result


def constant(shape, *index):
    return pl.BlockSpec(shape, lambda i: index, pipeline_mode=pl.Buffered(1))


def layer_zero(patches, table, bias, net, gains, save, group):
    count = patches.shape[0]
    weights = [net["patch"], net["mix", 0], net["out", 0], net["up", 0], net["down", 0]]
    rows = count * ROWS
    step = group * ROWS
    row_block = lambda cols: pl.BlockSpec((step, cols), lambda i: (i, 0))
    in_specs = [
        pl.BlockSpec((group, PATCHES, PATCH_DIM), lambda i: (i, 0, 0)),
        constant((ROWS, D), 0, 0),
        pl.BlockSpec((group, 1, ROWS), lambda i: (i, 0, 0)),
        *(spec for _, spec in weights),
        constant((8, D), 0, 0),
    ]
    out_shape = [jax.ShapeDtypeStruct((rows, D), f32)]
    out_specs = [row_block(D)]
    scratch = []
    if save:
        out_shape += [
            jax.ShapeDtypeStruct((rows, D), f32),
            jax.ShapeDtypeStruct((rows, 3 * D), bf16),
            jax.ShapeDtypeStruct((count, HEADS, ROWS, ROWS), bf16),
            jax.ShapeDtypeStruct((rows, D), bf16),
            jax.ShapeDtypeStruct((rows, D), f32),
            jax.ShapeDtypeStruct((rows, FF), bf16),
            jax.ShapeDtypeStruct((rows, FF), bf16),
        ]
        out_specs += [
            row_block(D),
            row_block(3 * D),
            pl.BlockSpec((group, HEADS, ROWS, ROWS), lambda i: (i, 0, 0, 0)),
            row_block(D),
            row_block(D),
            row_block(FF),
            row_block(FF),
        ]
    else:
        scratch = [
            pltpu.VMEM((step, D), f32),
            pltpu.VMEM((step, 3 * D), bf16),
            pltpu.VMEM((step, D), bf16),
        ]
    packed = net["packed"]
    if packed:
        scratch = scratch + [pltpu.VMEM((FF, D), bf16)]
    return pl.pallas_call(
        lambda *refs: forward_kernel(save, packed, group, *refs),
        grid=(count // group,),
        in_specs=in_specs,
        out_specs=out_specs,
        out_shape=out_shape,
        scratch_shapes=scratch,
        compiler_params=pltpu.CompilerParams(
            dimension_semantics=("arbitrary",), vmem_limit_bytes=58 * 1024 * 1024
        ),
        cost_estimate=cost(20),
        name="student_layer_zero" if save else "teacher_layer_zero",
    )(patches, table, bias, *(w for w, _ in weights), gains)


def unit_parts(v):
    inverse = lax.rsqrt(jnp.sum(v * v, -1, keepdims=True) + 1e-06)
    return v * inverse, inverse


def class_kernel(student, packed, count, *refs):
    if packed:
        (state, bias, win, wo, w1, down_in, gains, protos_in, rest_in), refs = refs[:9], refs[9:]
        refs, w2, protos = refs[:-2], refs[-2], refs[-1]
        natural_down(down_in, w2)
        natural_protos(protos_in, rest_in, protos)
    else:
        (state, bias, win, wo, w1, w2, gains, protos), refs = refs[:8], refs[8:]
    if student:
        (logs, sums, kv, queries, shares, att, mid_c, expanded_out, last, cls), refs = refs[:10], refs[10:]
    else:
        (target,), (kv, att, cls) = refs[:1], refs[1:]
    hat, _ = normalize(state[...])
    normed = (hat * gains[0:1, :]).astype(bf16)
    kv[...] = dot(normed, win[:, D:]).astype(bf16)
    cls[...] = jnp.zeros((CR, D), f32)
    for g in range(count):
        cls[g : g + 1, :] = state[pl.ds(g * ROWS + CLS, 1), :]
    class_state = cls[...]
    hat, _ = normalize(class_state)
    query = dot((hat * gains[0:1, :]).astype(bf16), win[:, :D]).astype(bf16)
    if student:
        queries[...] = query
    mask = head_mask()
    for g in range(count):
        rows = pl.ds(g * ROWS, ROWS)
        spread = (jnp.broadcast_to(query[g : g + 1, :].astype(f32) * SCALE, (CR, D)) * mask).astype(bf16)
        scores = dot_bt(spread, kv[rows, pl.ds(0, D)]) + bias[g]
        e = jnp.exp(scores - jnp.max(scores, -1, keepdims=True))
        p = e * (1.0 / jnp.sum(e, -1, keepdims=True))
        if student:
            shares[g] = p
        o = dot(p.astype(bf16), kv[rows, pl.ds(D, D)])
        att[g : g + 1, :] = jnp.sum(o * mask, 0, keepdims=True)
    att[count:, :] = jnp.zeros((CR - count, D), f32)
    middle = class_state + dot(att[...].astype(bf16), wo[...])
    hat, _ = normalize(middle)
    expanded = dot((hat * gains[1:2, :]).astype(bf16), w1[...])
    act, _ = gelu_parts(expanded, False)
    result = middle + dot(act.astype(bf16), w2[...])
    if student:
        mid_c[...] = middle
        expanded_out[...] = expanded
        last[...] = result
    hat, _ = normalize(result)
    unit, _ = unit_parts(hat * gains[2:3, :])
    proto_unit, _ = unit_parts(protos[...].astype(f32))
    raw = dot_bt(unit.astype(bf16), proto_unit.astype(bf16))
    logits = raw * (1.0 / (student_softness if student else teacher_sharpness))
    logits = logits - jnp.max(logits, -1, keepdims=True)
    e = jnp.exp(logits)
    total = jnp.sum(e, -1, keepdims=True)
    if student:
        log_share = logits - jnp.log(total)
        logs[...] = log_share
        share = jnp.exp(log_share)
        row = lax.broadcasted_iota(jnp.int32, (CR, PROTOS), 0)
        sums[...] = jnp.zeros((8, PROTOS), f32)
        per = count // 2
        for m in range(2):
            inside = jnp.logical_and(row >= m * per, row < (m + 1) * per)
            sums[m : m + 1, :] = jnp.sum(jnp.where(inside, share, 0.0), 0, keepdims=True)
    else:
        target[...] = e / total


def cost(micros):
    return pl.CostEstimate(flops=int(micros * 1e9), transcendentals=0, bytes_accessed=int(micros * 3e6))


def whole():
    return pl.BlockSpec(memory_space=pltpu.VMEM)


def natural_scratch(packed):
    return [pltpu.VMEM((FF, D), bf16), pltpu.VMEM((PROTOS, D), f32)] if packed else []


def layer_one(state, bias, net, gains, student):
    count = bias.shape[0]
    weights = [net["mix", 1], net["out", 1], net["up", 1], net["down", 1]]
    protos = net["protos"]
    packed = net["packed"]
    rows = count * ROWS
    if student:
        out_shape = [
            jax.ShapeDtypeStruct((CR, PROTOS), f32),
            jax.ShapeDtypeStruct((8, PROTOS), f32),
            jax.ShapeDtypeStruct((rows, 2 * D), bf16),
            jax.ShapeDtypeStruct((CR, D), bf16),
            jax.ShapeDtypeStruct((count, CR, ROWS), f32),
            jax.ShapeDtypeStruct((CR, D), f32),
            jax.ShapeDtypeStruct((CR, D), f32),
            jax.ShapeDtypeStruct((CR, FF), f32),
            jax.ShapeDtypeStruct((CR, D), f32),
            jax.ShapeDtypeStruct((CR, D), f32),
        ]
        scratch = []
    else:
        out_shape = [jax.ShapeDtypeStruct((CR, PROTOS), f32)]
        scratch = [
            pltpu.VMEM((rows, 2 * D), bf16),
            pltpu.VMEM((CR, D), f32),
            pltpu.VMEM((CR, D), f32),
        ]
    result = pl.pallas_call(
        lambda *refs: class_kernel(student, packed, count, *refs),
        grid=(1,),
        in_specs=[whole()] * 2 + [spec for _, spec in weights] + [whole()] + [spec for _, spec in protos],
        out_specs=[whole()] * len(out_shape),
        out_shape=out_shape,
        scratch_shapes=scratch + natural_scratch(packed),
        compiler_params=pltpu.CompilerParams(vmem_limit_bytes=58 * 1024 * 1024),
        cost_estimate=cost(9),
        name="student_layer_one" if student else "teacher_layer_one",
    )(state, bias, *(w for w, _ in weights), gains, *(w for w, _ in protos))
    return result


def class_back_kernel(packed, count, inverse_count, *refs):
    (logs, target, mean_sum, state, kv, queries, shares, att, mid_c, expanded, last, cls) = refs[:12]
    if packed:
        (me, win, wo, w1, w2, gains, protos), refs = refs[12:19], refs[19:]
        (delta, s_gain, report, planes, dkv, dq_all, s_in, s_out, s_up, s_down, s_proto) = refs
    else:
        (win, wo, w1, w2, gains, protos) = refs[12:18]
        (delta, s_gain, report, s_in, s_out, s_up, s_down, s_proto, dkv, dq_all) = refs[18:]
    mask = head_mask()
    row = lax.broadcasted_iota(jnp.int32, (CR, 1), 0)
    live = row < count
    log_share = logs[...]
    share = jnp.exp(log_share)
    targets = target[...]
    mean_share = mean_sum[0:2, :] * (2.0 * inverse_count)
    log_mean = jnp.log(mean_share)
    cross = -jnp.sum(jnp.where(live, targets * log_share, 0.0), -1, keepdims=True)
    cross = jnp.sum(cross, 0, keepdims=True) * inverse_count
    entropy = jnp.sum(jnp.sum(mean_share * log_mean, -1, keepdims=True), 0, keepdims=True) * 0.5
    lane = lax.broadcasted_iota(jnp.int32, (8, 128), 1)
    report[...] = jnp.where(lane == 0, cross, jnp.where(lane == 1, entropy, 0.0))
    log_row = jnp.where(row < count // 2, log_mean[0:1, :], log_mean[1:2, :])
    slope = share - targets + share * (log_row - jnp.sum(share * log_row, -1, keepdims=True))
    slope = jnp.where(live, slope * (inverse_count / student_softness), 0.0).astype(bf16)
    hat_f, inv_f = normalize(last[...])
    summary = hat_f * gains[2:3, :]
    unit, inv_u = unit_parts(summary)
    proto = protos[...].astype(f32)
    proto_unit, inv_p = unit_parts(proto)
    d_unit = dot(slope, proto_unit.astype(bf16))
    d_proto = dot_at(slope, unit.astype(bf16))
    s_proto[...] = inv_p * (d_proto - proto_unit * jnp.sum(proto_unit * d_proto, -1, keepdims=True))
    d_summary = inv_u * (d_unit - unit * jnp.sum(unit * d_unit, -1, keepdims=True))
    d, gain_f = norm_back(hat_f, inv_f, gains[2:3, :], d_summary)
    s_gain[...] = jnp.zeros((8, D), f32)
    s_gain[2:3, :] = gain_f
    d_low = d.astype(bf16)
    act, gslope = gelu_parts(expanded[...], True)
    s_down[...] = dot_at(act.astype(bf16), d_low)
    d_exp = (dot_bt(d_low, w2[...]) * gslope).astype(bf16)
    hat_m, inv_m = normalize(mid_c[...])
    s_up[...] = dot_at((hat_m * gains[1:2, :]).astype(bf16), d_exp)
    d_mid, gain_two = norm_back(hat_m, inv_m, gains[1:2, :], dot_bt(d_exp, w1[...]))
    s_gain[1:2, :] = gain_two
    d_mid = d + d_mid
    d_mid_low = d_mid.astype(bf16)
    s_out[...] = dot_at(att[...].astype(bf16), d_mid_low)
    d_att = dot_bt(d_mid_low, wo[...]).astype(bf16)
    dq_all[...] = jnp.zeros((CR, D), f32)
    for g in range(count):
        rows = pl.ds(g * ROWS, ROWS)
        d_spread = (jnp.broadcast_to(d_att[g : g + 1, :].astype(f32), (CR, D)) * mask).astype(bf16)
        q_spread = (jnp.broadcast_to(queries[g : g + 1, :].astype(f32) * SCALE, (CR, D)) * mask).astype(bf16)
        p = shares[g]
        d_p = dot_bt(d_spread, kv[rows, pl.ds(D, D)])
        d_s = (p * (d_p - jnp.sum(p * d_p, -1, keepdims=True))).astype(bf16)
        dkv[rows, pl.ds(D, D)] = dot_at(p.astype(bf16), d_spread).astype(bf16)
        dkv[rows, pl.ds(0, D)] = dot_at(d_s, q_spread).astype(bf16)
        dq = dot(d_s, kv[rows, pl.ds(0, D)]) * mask
        dq_all[g : g + 1, :] = jnp.sum(dq, 0, keepdims=True) * SCALE
    dq_low = dq_all[...].astype(bf16)
    hat_c, _ = normalize(cls[...])
    s_in[:, :D] = dot_at((hat_c * gains[0:1, :]).astype(bf16), dq_low)
    hat, inv = normalize(state[...])
    s_in[:, D:] = dot_at((hat * gains[0:1, :]).astype(bf16), dkv[...])
    d_class = dot_bt(dq_low, win[:, :D])
    delta[...] = dot_bt(dkv[...], win[:, D:])
    for g in range(count):
        one = pl.ds(g * ROWS + CLS, 1)
        delta[one, :] = delta[one, :] + d_class[g : g + 1, :]
    d_state, gain_one = norm_back(hat, inv, gains[0:1, :], delta[...])
    s_gain[0:1, :] = gain_one
    delta[...] = d_state
    for g in range(count):
        one = pl.ds(g * ROWS + CLS, 1)
        delta[one, :] = delta[one, :] + d_mid[g : g + 1, :]
    if packed:
        pack_planes(me[0], planes, [(s_in, 24), (s_out, 24), (s_up, 24), (s_down, 96)], [(s_proto, 32)])


BITS = {"c": 0, "x": 1, "y": 2, "z": 3}
PATHS = (("c", "x", "y", "z"), ("c", "y", "z", "x"), ("c", "z", "x", "y"))
LAYER_ROWS = 288
CHUNK_ROWS = (352, 192, 160)


def pack_blocks(me, keep, send, layered, wide):
    for path in range(3):
        for place in range(16):
            mask = 0
            for k in range(4):
                mask |= ((place >> (3 - k)) & 1) << BITS[PATHS[path][k]]
            owner = (me & 15) ^ mask
            pieces = []
            for ref, rows in layered:
                at = pl.ds(pl.multiple_of(owner * rows, 8), rows)
                for j in range(ref.shape[1] // D):
                    pieces.append(ref[at, pl.ds(D * j + 128 * path, 128)])
            for other in range(2):
                half = (me >> 4) ^ other
                for ref, rows in wide:
                    at = pl.ds(pl.multiple_of((half * 16 + owner) * rows, 8), rows)
                    pieces.append(ref[at, pl.ds(128 * path, 128)])
            value = jnp.concatenate(pieces, 0).astype(bf16)
            if place < 8:
                keep[path, place] = value
            else:
                send[path, place - 8] = value


def pack_planes(me, planes, layered, wide):
    for owner in range(8):
        for place in range(2):
            low = owner + 8 * (((me >> 3) & 1) ^ place)
            pieces = []
            for ref, rows in layered:
                at = pl.ds(pl.multiple_of(low * rows, 8), rows)
                for j in range(ref.shape[1] // D):
                    pieces.append(ref[at, pl.ds(D * j, D)])
            for other in range(2):
                half = (me >> 4) ^ other
                for ref, rows in wide:
                    pieces.append(ref[pl.ds(pl.multiple_of((half * 16 + low) * rows, 8), rows), :])
            planes[owner, pl.ds(352 * place, 352), :] = jnp.concatenate(pieces, 0).astype(bf16)


def chunk_shapes(chunk):
    if chunk == 0:
        return [jax.ShapeDtypeStruct((8, 704, D), bf16)]
    return [jax.ShapeDtypeStruct((3, 8, CHUNK_ROWS[chunk], 128), bf16)] * 2


def layer_one_back(args, net, gains, inverse_count, me):
    count = args[6].shape[0]
    weights = [net["mix", 1], net["out", 1], net["up", 1], net["down", 1]]
    protos = net["protos"]
    packed = net["fast"]
    rows = count * ROWS
    slopes = [(D, 3 * D), (D, D), (D, FF), (FF, D), (PROTOS, D)]
    out_shape = [
        jax.ShapeDtypeStruct((rows, D), f32),
        jax.ShapeDtypeStruct((8, D), f32),
        jax.ShapeDtypeStruct((8, 128), f32),
    ]
    scratch = [pltpu.VMEM((rows, 2 * D), bf16), pltpu.VMEM((CR, D), f32)]
    if packed:
        out_shape += chunk_shapes(0)
        scratch += [pltpu.VMEM(shape, f32) for shape in slopes]
    else:
        out_shape += [jax.ShapeDtypeStruct(shape, f32) for shape in slopes]
    scalar = [pl.BlockSpec(memory_space=pltpu.SMEM)] if packed else []
    return pl.pallas_call(
        lambda *refs: class_back_kernel(packed, count, inverse_count, *refs),
        grid=(1,),
        in_specs=[whole()] * 12 + scalar + [spec for _, spec in weights] + [whole()] + [spec for _, spec in protos],
        out_specs=[whole()] * len(out_shape),
        out_shape=out_shape,
        scratch_shapes=scratch,
        compiler_params=pltpu.CompilerParams(vmem_limit_bytes=58 * 1024 * 1024),
        cost_estimate=cost(13),
        name="layer_one_back",
    )(*args, *([me] if packed else []), *(w for w, _ in weights), gains, *(w for w, _ in protos))


def add_to(ref, value, first):
    @pl.when(first)
    def _():
        ref[...] = value

    @pl.when(jnp.logical_not(first))
    def _():
        ref[...] = ref[...] + value


def mlp_back_kernel(packed, group, *refs):
    (delta, act, dgelu, mid, w1, w2, gains), refs = refs[:7], refs[7:]
    first = pl.program_id(0) == 0
    if packed:
        me, d_mid, s_gain, keep, send, s_up, s_down = refs
    else:
        d_mid, s_gain, s_up, s_down = refs

    @pl.when(first)
    def _():
        s_up[...] = jnp.zeros(s_up.shape, f32)
        s_down[...] = jnp.zeros(s_down.shape, f32)
        s_gain[...] = jnp.zeros(s_gain.shape, f32)

    d = delta[...]
    d_low = d.astype(bf16)
    hat, inv = normalize(mid[...])
    normed = (hat * gains[1:2, :]).astype(bf16)
    d_normed = None
    for j in range(FF // D):
        cols = pl.ds(D * j, D)
        s_down[cols, :] += dot_at(act[:, cols], d_low)
        d_exp = (dot_bt(d_low, w2[cols, :]) * dgelu[:, cols].astype(f32)).astype(bf16)
        s_up[:, cols] += dot_at(normed, d_exp)
        part = dot_bt(d_exp, w1[:, cols])
        d_normed = part if d_normed is None else d_normed + part
    back, gain = norm_back(hat, inv, gains[1:2, :], d_normed)
    s_gain[0:1, :] += gain
    d_mid[...] = d + back
    if packed:

        @pl.when(pl.program_id(0) == pl.num_programs(0) - 1)
        def _():
            pack_blocks(me[0], keep, send, [(s_up, 24), (s_down, 96)], [])


def backward_shapes(packed, slopes, chunk):
    if packed:
        return chunk_shapes(chunk), [pltpu.VMEM(shape, f32) for shape in slopes]
    return [jax.ShapeDtypeStruct(shape, f32) for shape in slopes], []


def fixed_spec(shape):
    return pl.BlockSpec(shape, lambda i: (0,) * len(shape))


def layer_zero_mlp_back(delta, act, dgelu, mid, net, gains, group, me):
    packed = net["fast"]
    slopes, scratch = backward_shapes(packed, [(D, FF), (FF, D)], 1)
    scalar = [pl.BlockSpec(memory_space=pltpu.SMEM)] if packed else []
    weights = [net["up", 0], net["down", 0]]
    rows = delta.shape[0]
    step = group * ROWS
    row_block = lambda cols: pl.BlockSpec((step, cols), lambda i: (i, 0))
    return pl.pallas_call(
        lambda *refs: mlp_back_kernel(packed, group, *refs),
        grid=(rows // step,),
        in_specs=[
            row_block(D),
            row_block(FF),
            row_block(FF),
            row_block(D),
            *(spec for _, spec in weights),
            constant((8, D), 0, 0),
            *scalar,
        ],
        out_specs=[row_block(D), fixed_spec((8, D))] + [fixed_spec(v.shape) for v in slopes],
        out_shape=[jax.ShapeDtypeStruct((rows, D), f32), jax.ShapeDtypeStruct((8, D), f32)] + slopes,
        scratch_shapes=scratch,
        compiler_params=pltpu.CompilerParams(
            dimension_semantics=("arbitrary",), vmem_limit_bytes=58 * 1024 * 1024
        ),
        cost_estimate=cost(17),
        name="layer_zero_mlp_back",
    )(delta, act, dgelu, mid, *(w for w, _ in weights), gains, *([me] if packed else []))


def attention_back_kernel(packed, group, *refs):
    (d_mid, state, mix, share, att, pat, win, wo, gains, gain_two, gain_one) = refs[:11]
    if packed:
        me, keep, send, s_in, s_out, s_patch, s_vector, d_att, dmix = refs[11:]
    else:
        s_in, s_out, s_patch, s_vector, d_att, dmix = refs[11:]

    @pl.when(pl.program_id(0) == 0)
    def _():
        s_in[...] = jnp.zeros(s_in.shape, f32)
        s_out[...] = jnp.zeros(s_out.shape, f32)
        s_patch[...] = jnp.zeros(s_patch.shape, f32)
        s_vector[...] = jnp.zeros(s_vector.shape, f32)
        s_vector[ROWS + 1 : ROWS + 2, :] = gain_two[0:1, :]
        s_vector[ROWS + 2 : ROWS + 5, :] = gain_one[0:3, :]

    d_low = d_mid[...].astype(bf16)
    s_out[...] += dot_at(att[...], d_low)
    d_att[...] = dot_bt(d_low, wo[...]).astype(bf16)
    masks = half_masks()
    for g in range(group):
        rows = pl.ds(g * ROWS, ROWS)
        for pair in range(HEADS // 2):
            lanes = [pl.ds(D * part + 128 * pair, 128) for part in range(3)]
            query = mix[rows, lanes[0]] * jnp.asarray(SCALE, bf16)
            keys = mix[rows, lanes[1]] * jnp.asarray(SCALE, bf16)
            values = mix[rows, lanes[2]]
            upstream = d_att[rows, lanes[0]]
            dq = dk = dv = None
            for half in range(2):
                p = share[g, 2 * pair + half]
                up = upstream * masks[half]
                d_p = dot_bt(up, values)
                p_wide = p.astype(f32)
                weighted = p_wide * d_p
                d_s = (weighted - p_wide * jnp.sum(weighted, -1, keepdims=True)).astype(bf16)
                parts = (
                    dot(d_s, keys * masks[half]),
                    dot_at(d_s, query * masks[half]),
                    dot_at(p, up),
                )
                dq, dk, dv = parts if dq is None else (dq + parts[0], dk + parts[1], dv + parts[2])
            dmix[rows, lanes[0]] = dq.astype(bf16)
            dmix[rows, lanes[1]] = dk.astype(bf16)
            dmix[rows, lanes[2]] = dv.astype(bf16)
    hat, inv = normalize(state[...])
    normed = (hat * gains[0:1, :]).astype(bf16)
    s_in[...] += dot_at(normed, dmix[...])
    back, gain = norm_back(hat, inv, gains[0:1, :], dot_bt(dmix[...], win[...]))
    s_vector[ROWS : ROWS + 1, :] += gain
    d_state = d_mid[...] + back
    for g in range(group):
        one = d_state[g * ROWS : (g + 1) * ROWS]
        s_vector[0:ROWS, :] += one
        s_patch[...] += dot_at(pat[g], one[:PATCHES].astype(bf16))
    if packed:

        @pl.when(pl.program_id(0) == pl.num_programs(0) - 1)
        def _():
            pack_blocks(me[0], keep, send, [(s_in, 24), (s_out, 24)], [(s_patch, 24), (s_vector, 8)])


VECTORS = 256


def layer_zero_attention_back(d_mid, state, mix, share, att, patches, net, gains, gain_two, gain_one, group, me):
    packed = net["fast"]
    slopes, scratch = backward_shapes(packed, [(D, 3 * D), (D, D), (PATCH_DIM, D), (VECTORS, D)], 2)
    scalar = [pl.BlockSpec(memory_space=pltpu.SMEM)] if packed else []
    weights = [net["mix", 0], net["out", 0]]
    rows = d_mid.shape[0]
    step = group * ROWS
    row_block = lambda cols: pl.BlockSpec((step, cols), lambda i: (i, 0))
    return pl.pallas_call(
        lambda *refs: attention_back_kernel(packed, group, *refs),
        grid=(rows // step,),
        in_specs=[
            row_block(D),
            row_block(D),
            row_block(3 * D),
            pl.BlockSpec((group, HEADS, ROWS, ROWS), lambda i: (i, 0, 0, 0)),
            row_block(D),
            pl.BlockSpec((group, PATCHES, PATCH_DIM), lambda i: (i, 0, 0)),
            *(spec for _, spec in weights),
            constant((8, D), 0, 0),
            constant((8, D), 0, 0),
            constant((8, D), 0, 0),
            *scalar,
        ],
        out_specs=[fixed_spec(v.shape) for v in slopes],
        out_shape=slopes,
        scratch_shapes=scratch + [pltpu.VMEM((step, D), bf16), pltpu.VMEM((step, 3 * D), bf16)],
        compiler_params=pltpu.CompilerParams(
            dimension_semantics=("arbitrary",), vmem_limit_bytes=58 * 1024 * 1024
        ),
        cost_estimate=cost(21),
        name="layer_zero_attention_back",
    )(d_mid, state, mix, share, att, patches, *(w for w, _ in weights), gains, gain_two, gain_one, *([me] if packed else []))


NAMES = ("mix", "out", "up", "down", "patch", "protos")
WIDTHS = {"up": FF, "down": FF, "patch": D, "mix": 3 * D, "out": D, "protos": D, "rest": 128}
PLACE = {}
COLUMNS = 0
for _key in WIDTHS:
    PLACE[_key] = COLUMNS
    COLUMNS += WIDTHS[_key]


def pack_pieces(values):
    pieces = {name: values[name] for name in ("mix", "out", "up", "patch")}
    r = values["patch"].shape[0]
    down, protos = values["down"], values["protos"]
    pieces["down"] = jnp.concatenate([down[r * j : r * (j + 1)] for j in range(4)], 1)
    pieces["protos"] = protos[:r]
    pieces["rest"] = jnp.concatenate([protos[r:, 128 * j : 128 * (j + 1)] for j in range(3)], 0)
    return pieces


def pack_kernel(*refs):
    for net in range(2):
        out = refs[12 + net]
        values = {name: ref[...].astype(f32) for name, ref in zip(NAMES, refs[6 * net : 6 * net + 6])}
        for name, piece in pack_pieces(values).items():
            out[:, pl.ds(PLACE[name], WIDTHS[name])] = piece.astype(bf16)


THIRDS = ((0, 1792), (1792, 3584), (3584, 5504))


def chain_gather(mine):
    got = swap(mine, 4)
    arrays = [jnp.stack([mine[:, a:b], got[:, a:b]]) for a, b in THIRDS]
    for stage in (1, 2, 3):
        got = [swap(arrays[path], BITS[PATHS[path][stage]]) for path in range(3)]
        arrays = [jnp.concatenate([a, g], 0) for a, g in zip(arrays, got)]
    return arrays, [swap(a, 0) for a in arrays]


CHIPS_A_STEP = 2


def unpack_kernel(me, *refs):
    ins, outs = refs[: 6 * CHIPS_A_STEP], dict(zip(NAMES, refs[6 * CHIPS_A_STEP :]))
    first_core = (me[0] & 1) == 0
    pieces = {name: [] for name in NAMES}
    for chip in range(CHIPS_A_STEP):
        mine, got = ins[6 * chip : 6 * chip + 3], ins[6 * chip + 3 : 6 * chip + 6]
        own = jnp.concatenate([ref[0].astype(f32) for ref in mine], 1)
        other = jnp.concatenate([ref[0].astype(f32) for ref in got], 1)
        for rows in (jnp.where(first_core, own, other), jnp.where(first_core, other, own)):
            for name in ("mix", "out", "up", "patch"):
                pieces[name].append(rows[:, PLACE[name] : PLACE[name] + WIDTHS[name]])
            for j in range(4):
                pieces["down"].append(rows[:, PLACE["down"] + D * j : PLACE["down"] + D * (j + 1)])
            rest = rows[:, PLACE["rest"] :]
            pieces["protos"].append(rows[:, PLACE["protos"] : PLACE["protos"] + D])
            pieces["protos"].append(jnp.concatenate([rest[8 * j : 8 * (j + 1)] for j in range(3)], 1))
    for name in NAMES:
        outs[name][...] = jnp.concatenate(pieces[name], 0).astype(bf16)


def unpack_weights(arrays, got, me):
    def index(chip, path):
        def at(i, me_ref):
            other = (CHIPS_A_STEP * i + chip) ^ (me_ref[0] >> 1)
            place = (other >> 3) & 1
            for k in range(3):
                place = place + (((other >> (BITS[PATHS[path][k + 1]] - 1)) & 1) << (k + 1))
            return place, 0, 0

        return at

    in_specs, operands = [], []
    for chip in range(CHIPS_A_STEP):
        for source in (arrays, got):
            for path in range(3):
                in_specs.append(pl.BlockSpec((1,) + source[path].shape[1:], index(chip, path)))
                operands.append(source[path])
    shapes = ((2 * D, 3 * D), (2 * D, D), (2 * D, FF), (2 * FF, D), (PATCH_DIM, D), (PROTOS, D))
    steps = 16 // CHIPS_A_STEP
    return pl.pallas_call(
        unpack_kernel,
        grid_spec=pltpu.PrefetchScalarGridSpec(
            num_scalar_prefetch=1,
            grid=(steps,),
            in_specs=in_specs,
            out_specs=[pl.BlockSpec((a // steps, b), lambda i, me_ref: (i, 0)) for a, b in shapes],
        ),
        out_shape=[jax.ShapeDtypeStruct(shape, bf16) for shape in shapes],
        compiler_params=pltpu.CompilerParams(dimension_semantics=("arbitrary",), vmem_limit_bytes=58 * 1024 * 1024),
        cost_estimate=cost(9),
        name="unpack_weights",
    )(me, *operands)


def natural_net(mix, out, up, down, patch, protos, fast):
    result = {"packed": False, "fast": fast, "patch": (patch, constant((PATCH_DIM, D), 0, 0))}
    for layer in range(2):
        result["mix", layer] = (mix, constant((D, 3 * D), layer, 0))
        result["out", layer] = (out, constant((D, D), layer, 0))
        result["up", layer] = (up, constant((D, FF), layer, 0))
        result["down", layer] = (down, constant((FF, D), layer, 0))
    result["protos"] = [(protos, constant((PROTOS, D), 0, 0))]
    return result


def gathered_net(full):
    result = {"packed": True, "fast": True, "patch": (full, constant((PATCH_DIM, D), 0, PLACE["patch"] // D))}
    for layer in range(2):
        for name, height in (("mix", D), ("out", D), ("up", D), ("down", D)):
            result[name, layer] = (full, constant((height, WIDTHS[name]), layer, PLACE[name] // WIDTHS[name]))
    result["protos"] = [(full, constant((PATCH_DIM, D), 0, PLACE["protos"] // D)), (full, constant((PATCH_DIM, 128), 0, PLACE["rest"] // 128))]
    return result


def plain_net(full, n):
    r = full.shape[0] // n
    part = lambda name: full[:, PLACE[name] : PLACE[name] + WIDTHS[name]]
    down = part("down").reshape(n, r, 4, D).transpose(0, 2, 1, 3).reshape(2 * FF, D)
    rest = part("rest").reshape(n, 3, r // 3, 128).transpose(0, 2, 1, 3).reshape(n, r // 3, D)
    protos = jnp.concatenate([part("protos").reshape(n, r, D), rest], 1).reshape(PROTOS, D)
    return natural_net(part("mix"), part("out"), part("up"), down, part("patch"), protos, False)


def gather_networks(student, teacher, me, n):
    gather = lambda rows: lax.all_gather(rows, "dp", axis=0, tiled=True)
    r = student[0].shape[0]
    if n != 32:
        nets = []
        for shards in (student, teacher):
            pieces = pack_pieces(dict(zip(NAMES, shards)))
            nets.append(plain_net(gather(jnp.concatenate([pieces[name].astype(bf16) for name in WIDTHS], 1)), n))
        return nets
    student_rows, teacher_rows = pl.pallas_call(
        pack_kernel,
        in_specs=[whole()] * 12,
        out_specs=[whole()] * 2,
        out_shape=[jax.ShapeDtypeStruct((r, COLUMNS), bf16)] * 2,
        cost_estimate=cost(2),
        name="pack_weights",
    )(*student, *teacher)
    full = gather(teacher_rows)
    arrays, got = chain_gather(student_rows)
    return natural_net(*unpack_weights(arrays, got, me), True), gathered_net(full)


def small_sum(value, n):
    copies = jnp.broadcast_to(value[None], (n,) + value.shape)
    return jnp.sum(lax.all_to_all(copies, "dp", 0, 0, tiled=True), 0)


def swap(value, bit):
    size = lax.axis_size("dp")
    return lax.ppermute(value, "dp", [(i, i ^ (1 << bit)) for i in range(size)])


def core_stage(parts):
    got = [swap(send, 0) for _, send in parts]
    total = [(keep.astype(f32) + g.astype(f32)).astype(bf16) for (keep, _), g in zip(parts, got)]
    join = lambda path, rows: jnp.concatenate([t[path, rows] for t in total], 1)
    return [(join(path, slice(0, 4)), join(path, slice(4, 8))) for path in range(3)]


def axis_stage(stage, arrays):
    got = [swap(arrays[path][1], BITS[PATHS[path][stage]]) for path in range(3)]
    total = [arrays[path][0].astype(f32) + got[path].astype(f32) for path in range(3)]
    if stage == 3:
        return jnp.concatenate(total, 0)
    half = total[0].shape[0] // 2
    total = [t.astype(bf16) for t in total]
    return [(t[:half], t[half:]) for t in total]


def last_stage(total):
    send = jnp.concatenate([total[..., :LAYER_ROWS, :], total[..., LAYER_ROWS + 32 :, :]], -2)
    return total, swap(send.astype(bf16), 4)


def scatter_chunk(parts):
    arrays = core_stage(parts)
    for stage in (1, 2, 3):
        arrays = axis_stage(stage, arrays)
    return last_stage(arrays)


def scatter_planes(planes, n):
    groups = [[8 * z + i for i in range(8)] for z in range(n // 8)]
    mine = lax.psum_scatter(planes, "dp", scatter_dimension=0, axis_index_groups=groups)
    total = mine[:352].astype(f32) + swap(mine[352:], 3).astype(f32)
    return last_stage(total)


def square_sum(value):
    return jnp.sum(jnp.sum(value * value, -1, keepdims=True), 0, keepdims=True)


def three_parts(value):
    high = value.astype(bf16).astype(f32)
    middle = (value - high).astype(bf16).astype(f32)
    return high, middle, value - high - middle


def collect_kernel(*refs):
    (me, total_one, got_one, total_zero, got_zero, report) = refs[:6]
    (mix, out, up, down, patch, protos, line) = refs[6:]
    upper = (me[0] >> 4) == 1
    one = total_one[pl.ds(0, 320), :] + got_one[...].astype(f32)
    vectors = []
    for path in range(3):
        a = one[:, 128 * path : 128 * (path + 1)]
        c = total_zero[path, pl.ds(0, 320), :] + got_zero[path].astype(f32)
        lanes = pl.ds(128 * path, 128)
        for j in range(3):
            mix[:, pl.ds(D * j + 128 * path, 128)] = jnp.where(upper, a[24 * j : 24 * (j + 1)], c[192 + 24 * j : 216 + 24 * j])
        out[:, lanes] = jnp.where(upper, a[72:96], c[264:288])
        for j in range(4):
            up[:, pl.ds(D * j + 128 * path, 128)] = jnp.where(upper, a[96 + 24 * j : 120 + 24 * j], c[24 * j : 24 * (j + 1)])
        down[:, lanes] = jnp.where(upper, a[192:288], c[96:192])
        protos[:, lanes] = a[288:320]
        patch[:, lanes] = c[288:312]
        vectors.append(c[312:320])
    write_line(line, (mix, out, up, down, patch, protos), jnp.concatenate(vectors, 1), report)


def write_line(line, slopes, vectors, report):
    squares = square_sum(vectors)
    for ref in slopes:
        squares = squares + square_sum(ref[...])
    cross = report[0:1, 0:1]
    rows = vectors.shape[0]
    lane = lax.broadcasted_iota(jnp.int32, (rows, 128), 1)
    row = lax.broadcasted_iota(jnp.int32, (rows, 128), 0)
    tail = jnp.zeros((rows, 128), f32)
    for i, part in enumerate(three_parts(squares) + three_parts(cross)):
        tail = jnp.where(jnp.logical_and(lane == i, row == 0), part, tail)
    full = jnp.concatenate([vectors, tail], 1).astype(bf16)
    for d in range(line.shape[0]):
        line[d] = full


RATES = (matrix_rate,) * 5 + (table_rate,) * 2


def update_kernel(rows, *refs):
    (fixes, report, arrived), refs = refs[:3], refs[3:]
    slopes, masters, firsts, seconds = refs[:6], refs[6:13], refs[13:20], refs[20:27]
    news, moments, squares, scalars, vector = refs[27:34], refs[34:41], refs[41:48], refs[48], refs[49]
    tail = jnp.zeros((1, 128), f32)
    for d in range(arrived.shape[0]):
        tail = tail + arrived[d, 0:1, pl.ds(D, 128)].astype(f32)
    lane = lax.broadcasted_iota(jnp.int32, (1, 128), 1)
    norm = jnp.sqrt(jnp.sum(jnp.where(lane < 3, tail, 0.0), -1, keepdims=True))
    cross = jnp.sum(jnp.where(jnp.logical_and(lane >= 3, lane < 6), tail, 0.0), -1, keepdims=True)
    loss = cross + report[0:1, 1:2]
    wide = lax.broadcasted_iota(jnp.int32, (8, 128), 1)
    scalars[...] = jnp.where(wide == 0, loss, jnp.where(wide == 1, norm, 0.0))
    factor = jnp.minimum(1.0, clip_limit / (norm + 1e-06))
    per_device = arrived.shape[1]
    table = jnp.concatenate([arrived[d, :, pl.ds(0, D)].astype(f32) for d in range(arrived.shape[0])], 0)
    vector[0:1, :] = table[CLS : CLS + 1]
    vector[1:SEQ, :] = table[:PATCHES]
    vector[SEQ:VROWS, :] = table[ROWS : ROWS + 5]
    scale_one, scale_two = 1.0 / fixes[0], 1.0 / fixes[1]
    order = (0, 1, 2, 3, 4, None, 5)
    for i in range(7):
        slope = vector if order[i] is None else slopes[order[i]]
        clipped = slope[...] * factor
        moment = beta_one * firsts[i][...] + (1.0 - beta_one) * clipped
        square = beta_two * seconds[i][...] + (1.0 - beta_two) * clipped * clipped
        stepped = (moment * scale_one) / (jnp.sqrt(square * scale_two) + adam_floor)
        weight = masters[i][...]
        news[i][...] = weight - RATES[i] * (stepped + decay_rate * weight)
        moments[i][...] = moment
        squares[i][...] = square


def update_rows(slopes, arrived, report, masters, firsts, seconds, fixes):
    shapes = [jax.ShapeDtypeStruct(w.shape, f32) for w in masters]
    out_shape = shapes * 3 + [jax.ShapeDtypeStruct((8, 128), f32)]
    return pl.pallas_call(
        lambda *refs: update_kernel(None, *refs),
        in_specs=[pl.BlockSpec(memory_space=pltpu.SMEM)] + [whole()] * 29,
        out_specs=[whole()] * len(out_shape),
        out_shape=out_shape,
        scratch_shapes=[pltpu.VMEM((VROWS, D), f32)],
        compiler_params=pltpu.CompilerParams(vmem_limit_bytes=58 * 1024 * 1024),
        cost_estimate=cost(4),
        name="update_rows",
    )(fixes, report, arrived, *slopes, *masters, *firsts, *seconds)


def update_plain(slopes, arrived, report, masters, firsts, seconds, fixes):
    tail = jnp.sum(arrived[:, 0, D:].astype(f32), 0)
    table = arrived[:, :, :D].astype(f32).reshape(-1, D)
    vector = jnp.concatenate([table[CLS : CLS + 1], table[:PATCHES], table[ROWS : ROWS + 5]], 0)
    norm = jnp.sqrt(tail[0] + tail[1] + tail[2])
    loss = tail[3] + tail[4] + tail[5] + report[0, 1]
    factor = jnp.minimum(1.0, clip_limit / (norm + 1e-06))
    slopes = list(slopes[:5]) + [vector, slopes[5]]
    news, moments, squares = ([], [], [])
    for weight, first, second, slope, rate in zip(masters, firsts, seconds, slopes, RATES):
        clipped = slope * factor
        moment = beta_one * first + (1.0 - beta_one) * clipped
        square = beta_two * second + (1.0 - beta_two) * clipped * clipped
        stepped = moment / fixes[0] / (jnp.sqrt(square / fixes[1]) + adam_floor)
        news.append(weight - rate * (stepped + decay_rate * weight))
        moments.append(moment)
        squares.append(square)
    scalars = jnp.stack([loss, norm])[None]
    return (*news, *moments, *squares, scalars)


def collect(chunks, report, me, n, r):
    flat = [v for chunk in chunks for v in chunk]
    shapes = [(r, 3 * D), (r, D), (r, FF), (4 * r, D), (r, D), (4 * r // 3, D)]
    out_shape = [jax.ShapeDtypeStruct(shape, f32) for shape in shapes] + [jax.ShapeDtypeStruct((n, VECTORS // n, 512), bf16)]
    *slopes, line = pl.pallas_call(
        collect_kernel,
        in_specs=[pl.BlockSpec(memory_space=pltpu.SMEM)] + [whole()] * 5,
        out_specs=[whole()] * len(out_shape),
        out_shape=out_shape,
        compiler_params=pltpu.CompilerParams(vmem_limit_bytes=58 * 1024 * 1024),
        cost_estimate=cost(3),
        name="collect_gradients",
    )(me, *flat, report)
    return slopes, line


def collect_plain(one, mlp, rest, report, n):
    mix1, out1, up1, down1, protos = one
    up0, down0 = mlp
    mix0, out0, patch, vectors = rest
    scatter = lambda *v: lax.psum_scatter(jnp.concatenate(v, 0), "dp", scatter_dimension=0, tiled=True)
    slopes = [scatter(mix0, mix1), scatter(out0, out1), scatter(up0, up1), scatter(down0, down1), scatter(patch), scatter(protos)]
    vectors = scatter(vectors)
    squares = sum(jnp.sum(s * s) for s in slopes) + jnp.sum(vectors * vectors)
    tail = jnp.stack(three_parts(squares) + three_parts(report[0, 0]))
    tail = jnp.zeros((vectors.shape[0], 128), f32).at[0, :6].set(tail)
    line = jnp.concatenate([vectors, tail], 1).astype(bf16)
    return slopes, jnp.broadcast_to(line[None], (n,) + line.shape)


def local(
    attention_in, attention_out, hidden_in, hidden_out, patch_weight, vector_rows, prototypes,
    first_attention_in, first_attention_out, first_hidden_in, first_hidden_out, first_patch_weight, first_vector_rows, first_prototypes,
    second_attention_in, second_attention_out, second_hidden_in, second_hidden_out, second_patch_weight, second_vector_rows, second_prototypes,
    teacher_attention_in, teacher_attention_out, teacher_hidden_in, teacher_hidden_out, teacher_patch_weight, teacher_vector_rows, teacher_prototypes,
    anchor_patches, target_patches, patch_keep, step_count,
):
    n = lax.axis_size("dp")
    me = lax.axis_index("dp").astype(jnp.int32)[None]
    groups, per = anchor_patches.shape[:2]
    count = groups * per
    inverse_count = 1.0 / (count * n)
    masters = (attention_in, attention_out, hidden_in, hidden_out, patch_weight, vector_rows, prototypes)
    firsts = (first_attention_in, first_attention_out, first_hidden_in, first_hidden_out, first_patch_weight, first_vector_rows, first_prototypes)
    seconds = (second_attention_in, second_attention_out, second_hidden_in, second_hidden_out, second_patch_weight, second_vector_rows, second_prototypes)
    student, teacher = gather_networks(
        (attention_in, attention_out, hidden_in, hidden_out, patch_weight, prototypes),
        (teacher_attention_in, teacher_attention_out, teacher_hidden_in, teacher_hidden_out, teacher_patch_weight, teacher_prototypes),
        me,
        n,
    )

    def table_of(rows):
        return jnp.concatenate([rows[1:SEQ], rows[0:1], jnp.zeros((ROWS - SEQ, D), f32)], 0)

    def gains_of(rows):
        zeros = jnp.zeros((5, D), f32)
        first = jnp.concatenate([rows[SEQ : SEQ + 2], jnp.zeros((6, D), f32)], 0)
        second = jnp.concatenate([rows[SEQ + 2 : SEQ + 5], zeros], 0)
        return first, second

    keep = patch_keep.reshape(count, PATCHES)
    bias = jnp.where(keep == 1, 0.0, -1000000000.0).astype(f32)
    ends = jnp.where(jnp.arange(ROWS - PATCHES) == 0, 0.0, -1000000000.0).astype(f32)
    ends = jnp.broadcast_to(ends, (count, ROWS - PATCHES))
    bias = jnp.concatenate([bias, ends], 1)[:, None]
    plain = jnp.concatenate([jnp.zeros((count, PATCHES), f32), ends], 1)[:, None]
    anchor = anchor_patches.reshape(count, PATCHES, PATCH_DIM)
    target = target_patches.reshape(count, PATCHES, PATCH_DIM)
    gains0, gains1 = gains_of(vector_rows)
    teacher_rows = teacher_vector_rows.astype(f32)
    teacher_gains0, teacher_gains1 = gains_of(teacher_rows)
    counter = step_count.astype(f32)
    fixes = jnp.stack([1.0 - beta_one**counter, 1.0 - beta_two**counter])

    state1, state0, mix, share, att, mid, act, dgelu = layer_zero(anchor, table_of(vector_rows), bias, student, gains0, True, GROUP)
    if teacher["packed"]:
        state1, full = lax.optimization_barrier((state1, teacher["patch"][0]))
        teacher = gathered_net(full)
    logs, sums, kv, queries, shares, att_c, mid_c, expanded, last, cls = layer_one(state1, bias, student, gains1, True)
    mean_sum = small_sum(sums, n)
    (teacher_state,) = layer_zero(target, table_of(teacher_rows), plain, teacher, teacher_gains0, False, GROUP)
    (targets,) = layer_one(teacher_state, plain, teacher, teacher_gains1, False)
    delta, gain_one, report, *one = layer_one_back(
        (logs, targets, mean_sum, state1, kv, queries, shares, att_c, mid_c, expanded, last, cls), student, gains1, inverse_count, me)
    d_mid, gain_two, *mlp = layer_zero_mlp_back(delta, act, dgelu, mid, student, gains0, GROUP, me)
    rest = layer_zero_attention_back(d_mid, state0, mix, share, att, anchor, student, gains0, gain_two, gain_one, GROUP, me)
    if student["fast"]:
        chunks = [scatter_planes(*one, n), scatter_chunk([mlp, rest])]
        slopes, line = collect(chunks, report, me, n, attention_in.shape[0])
        update = update_rows
    else:
        slopes, line = collect_plain(one, mlp, rest, report, n)
        update = update_plain
    arrived = lax.all_to_all(line, "dp", 0, 0, tiled=True)
    *states, scalars = update(slopes, arrived, report, masters, firsts, seconds, fixes)
    return (scalars[0, 0], scalars[0, 1], *states)


GROUP = 2


def solution(mesh):
    rows, same, images = P("dp", None), P(), P(None, "dp", None, None)
    weights = (rows,) * 5 + (same, rows)
    return jax.shard_map(
        local,
        mesh=mesh,
        in_specs=weights * 4 + (images, images, P(None, "dp", None), same),
        out_specs=(same, same) + weights * 3,
        check_vma=False,
    )
```

```python
import jax
import jax.numpy as jnp
from jax import lax
from jax.experimental import pallas as pl
from jax.experimental.pallas import tpu as pltpu
from jax.sharding import PartitionSpec as P

D = 384
HEADS = 6
HEAD_DIM = 64
FF = 1536
PATCHES = 196
PATCH_DIM = 768
PROTOS = 1024
SEQ = 197
VROWS = 202
ROWS = 208
CLS = 196
CR = 16
SCALE = HEAD_DIM ** (-0.5)

student_softness = 0.04
teacher_sharpness = 0.02
clip_limit = 0.01
matrix_rate = 0.05
table_rate = 0.4
decay_rate = 0.05
beta_one = 0.9
beta_two = 0.999
adam_floor = 1e-08

f32 = jnp.float32
bf16 = jnp.bfloat16
GELU_C = 0.7978845608028654
GELU_A = 0.044715


def dot(a, b):
    return lax.dot_general(a, b, (((1,), (0,)), ((), ())), preferred_element_type=f32)


def dot_bt(a, b):
    return lax.dot_general(a, b, (((1,), (1,)), ((), ())), preferred_element_type=f32)


def dot_at(a, b):
    return lax.dot_general(a, b, (((0,), (0,)), ((), ())), preferred_element_type=f32)


def normalize(x):
    centre = x - jnp.sum(x, -1, keepdims=True) * (1.0 / D)
    spread = jnp.sum(centre * centre, -1, keepdims=True) * (1.0 / D)
    inverse = lax.rsqrt(spread + 1e-06)
    return centre * inverse, inverse


def norm_back(hat, inverse, gain, upstream):
    gain_slope = jnp.sum(upstream * hat, 0, keepdims=True)
    scaled = upstream * gain
    mean_one = jnp.sum(scaled, -1, keepdims=True) * (1.0 / D)
    mean_two = jnp.sum(scaled * hat, -1, keepdims=True) * (1.0 / D)
    return inverse * (scaled - mean_one - hat * mean_two), gain_slope


def gelu_parts(x, slope):
    square = x * x
    t = jnp.tanh(x * (GELU_C + (GELU_C * GELU_A) * square))
    half = 0.5 + 0.5 * t
    act = x * half
    if not slope:
        return act, None
    inner = GELU_C + (3.0 * GELU_C * GELU_A) * square
    return act, half + act * (1.0 - t) * inner


def half_masks():
    lane = lax.broadcasted_iota(jnp.int32, (1, 128), 1)
    first = jnp.where(lane < HEAD_DIM, 1.0, 0.0)
    return first.astype(bf16), (1.0 - first).astype(bf16)


def spot_masks():
    lane = lax.broadcasted_iota(jnp.int32, (1, 128), 1)
    return jnp.where(lane == HEAD_DIM, 1.0, 0.0).astype(bf16), jnp.where(lane == 0, 1.0, 0.0).astype(bf16)


def head_mask():
    row = lax.broadcasted_iota(jnp.int32, (CR, D), 0)
    lane = lax.broadcasted_iota(jnp.int32, (CR, D), 1)
    low = row * HEAD_DIM
    return jnp.where(jnp.logical_and(lane >= low, lane < low + HEAD_DIM), 1.0, 0.0)


def natural_down(ref, natural):
    for pair in range(8):
        rows = ref[pl.ds(48 * pair, 48), :].astype(f32)
        pieces = [rows[24 * b : 24 * (b + 1), D * j : D * (j + 1)] for b in range(2) for j in range(4)]
        natural[pl.ds(192 * pair, 192), :] = jnp.concatenate(pieces, 0).astype(bf16)


def natural_protos(ref, rest, natural):
    for pair in range(16):
        rows = ref[pl.ds(48 * pair, 48), :].astype(f32)
        tail = rest[pl.ds(48 * pair, 48), :].astype(f32)
        pieces = []
        for b in range(2):
            pieces.append(rows[24 * b : 24 * (b + 1)])
            pieces.append(jnp.concatenate([tail[24 * b + 8 * j : 24 * b + 8 * (j + 1)] for j in range(3)], 1))
        natural[pl.ds(64 * pair, 64), :] = jnp.concatenate(pieces, 0).astype(bf16)


def step_rows(ref, height):
    return ref.at[pl.ds(pl.multiple_of(pl.program_id(0) * height, 16), height)]


def layer_views(weights, packed, layer):
    if packed:
        (full,) = weights
        at = lambda name: full.at[pl.ds(D * layer, D), pl.ds(PLACE[name], WIDTHS[name])]
        return tuple(at(name) for name in ("mix", "out", "up", "down"))
    mix, out, up, down = weights[:4]
    rows = pl.ds(D * layer, D)
    return mix.at[rows], out.at[rows], up.at[rows], down.at[pl.ds(FF * layer, FF)]


def forward_kernel(save, packed, count, *refs):
    (pats, tab, bias_all, key_bias_all, gains, gains_one), refs = refs[:6], refs[6:]
    weights, refs = refs[: 1 if packed else 6], refs[1 if packed else 6 :]
    step = pl.program_id(0)
    group = pats.shape[1]
    height = group * ROWS
    pat = pats.at[pl.ds(step, 1)]
    if save:
        states, class_refs, naturals = refs[0], refs[8:18], refs[18:]
        out, first, mix, share, att, mid, act, dgelu = (step_rows(ref, height) if i != 3 else ref.at[pl.ds(step * group, group)] for i, ref in enumerate(refs[:8]))
    else:
        share = mid = act = dgelu = None
        (target, first, mix, att, kv, att_c, cls, states) = refs[:8]
        class_refs = (target, kv, att_c, cls)
        out = step_rows(states, height)
    win, wo, w1, w2 = layer_views(weights, packed, 0)
    if packed:
        down, down_one, protos = naturals
        wp = weights[0].at[:, pl.ds(PLACE["patch"], D)]

        @pl.when(step == 0)
        def _():
            natural_down(w2, down)

    else:
        wp, down = weights[4], w2
    group = pat.shape[1]
    table = tab[...]
    for g in range(group):
        embedded = dot(pat[0, g], wp[...])
        first[pl.ds(g * ROWS, PATCHES), :] = embedded + table[:PATCHES]
        first[pl.ds(g * ROWS + PATCHES, ROWS - PATCHES), :] = table[PATCHES:]
    state = first[...]
    hat, _ = normalize(state)
    normed = (hat * gains[0:1, :]).astype(bf16)
    mix[...] = dot(normed, win[...]).astype(bf16)
    masks, spots = half_masks(), spot_masks()

    for g in range(group):
        rows = pl.ds(g * ROWS, ROWS)
        key_bias = key_bias_all[step * group + g]
        for pair in range(HEADS // 2):
            query = mix[rows, pl.ds(128 * pair, 128)] * jnp.asarray(SCALE, bf16)
            keys = mix[rows, pl.ds(D + 128 * pair, 128)]
            values = mix[rows, pl.ds(2 * D + 128 * pair, 128)]
            total = None
            for half in range(2):
                scores = dot_bt(keys * masks[half] + key_bias * spots[half], query * masks[half] + spots[half])
                e = jnp.exp(scores - jnp.max(scores, 0, keepdims=True))
                p = (e * (1.0 / jnp.sum(e, 0, keepdims=True))).astype(bf16)
                if save:
                    share[g, 2 * pair + half] = p
                o = dot_at(p, values * masks[half])
                total = o if total is None else total + o
            att[rows, pl.ds(128 * pair, 128)] = total.astype(bf16)
    middle = first[...] + dot(att[...], wo[...])
    if save:
        mid[...] = middle
    hat, _ = normalize(middle)
    normed = (hat * gains[1:2, :]).astype(bf16)
    result = middle
    for j in range(FF // D):
        cols = pl.ds(D * j, D)
        a, slope = gelu_parts(dot(normed, w1[:, cols]), save)
        a = a.astype(bf16)
        if save:
            act[:, cols] = a
            dgelu[:, cols] = slope.astype(bf16)
        result = result + dot(a, down[cols, :])
    out[...] = result

    @pl.when(step == pl.num_programs(0) - 1)
    def _():
        win, wo, w1, w2 = layer_views(weights, packed, 1)
        if packed:
            natural_down(w2, down_one)
            natural_protos(weights[0].at[:, pl.ds(PLACE["protos"], D)], weights[0].at[:, pl.ds(PLACE["rest"], 128)], protos)
            late = (win, wo, w1, down_one, protos)
        else:
            late = (win, wo, w1, w2, weights[5])
        class_forward(save, count, states, bias_all, late, gains_one, class_refs)


def class_forward(student, count, state, bias, weights, gains, refs):
    win, wo, w1, w2, protos = weights
    if student:
        (logs, sums, kv, queries, shares, att, mid_c, expanded_out, last, cls) = refs
    else:
        (target, kv, att, cls) = refs
    hat, _ = normalize(state[...])
    normed = (hat * gains[0:1, :]).astype(bf16)
    kv[...] = dot(normed, win[:, D:]).astype(bf16)
    cls[...] = jnp.zeros((CR, D), f32)
    for g in range(count):
        cls[g : g + 1, :] = state[pl.ds(g * ROWS + CLS, 1), :]
    class_state = cls[...]
    hat, _ = normalize(class_state)
    query = dot((hat * gains[0:1, :]).astype(bf16), win[:, :D]).astype(bf16)
    if student:
        queries[...] = query
    mask = head_mask()
    for g in range(count):
        rows = pl.ds(g * ROWS, ROWS)
        spread = (jnp.broadcast_to(query[g : g + 1, :].astype(f32) * SCALE, (CR, D)) * mask).astype(bf16)
        scores = dot_bt(spread, kv[rows, pl.ds(0, D)]) + bias[g]
        e = jnp.exp(scores - jnp.max(scores, -1, keepdims=True))
        p = e * (1.0 / jnp.sum(e, -1, keepdims=True))
        if student:
            shares[g] = p
        o = dot(p.astype(bf16), kv[rows, pl.ds(D, D)])
        att[g : g + 1, :] = jnp.sum(o * mask, 0, keepdims=True)
    att[count:, :] = jnp.zeros((CR - count, D), f32)
    middle = class_state + dot(att[...].astype(bf16), wo[...])
    hat, _ = normalize(middle)
    expanded = dot((hat * gains[1:2, :]).astype(bf16), w1[...])
    act, _ = gelu_parts(expanded, False)
    result = middle + dot(act.astype(bf16), w2[...])
    if student:
        mid_c[...] = middle
        expanded_out[...] = expanded
        last[...] = result
    hat, _ = normalize(result)
    unit, _ = unit_parts(hat * gains[2:3, :])
    proto_unit, _ = unit_parts(protos[...].astype(f32))
    raw = dot_bt(unit.astype(bf16), proto_unit.astype(bf16))
    logits = raw * (1.0 / (student_softness if student else teacher_sharpness))
    logits = logits - jnp.max(logits, -1, keepdims=True)
    e = jnp.exp(logits)
    total = jnp.sum(e, -1, keepdims=True)
    if student:
        log_share = logits - jnp.log(total)
        logs[...] = log_share
        share = jnp.exp(log_share)
        row = lax.broadcasted_iota(jnp.int32, (CR, PROTOS), 0)
        per = count // 2
        lines = []
        for m in range(2):
            inside = jnp.logical_and(row >= m * per, row < (m + 1) * per)
            line = jnp.sum(jnp.where(inside, share, 0.0), 0, keepdims=True)
            lines += [line[:, 128 * k : 128 * (k + 1)] for k in range(PROTOS // 128)]
        lines = jnp.concatenate(lines, 0)
        for d in range(sums.shape[0]):
            sums[d] = lines.astype(bf16)
    else:
        target[...] = e / total


def forward(patches, table, bias, net, gains, gains_one, save, n):
    groups, group = patches.shape[:2]
    count = groups * group
    rows = count * ROWS
    step = group * ROWS
    packed = net["packed"]
    if save:
        out_shape = [
            jax.ShapeDtypeStruct((rows, D), f32),
            jax.ShapeDtypeStruct((rows, D), f32),
            jax.ShapeDtypeStruct((rows, 3 * D), bf16),
            jax.ShapeDtypeStruct((count, HEADS, ROWS, ROWS), bf16),
            jax.ShapeDtypeStruct((rows, D), bf16),
            jax.ShapeDtypeStruct((rows, D), f32),
            jax.ShapeDtypeStruct((rows, FF), bf16),
            jax.ShapeDtypeStruct((rows, FF), bf16),
            jax.ShapeDtypeStruct((CR, PROTOS), f32),
            jax.ShapeDtypeStruct((n, 16, 128), bf16),
            jax.ShapeDtypeStruct((rows, 2 * D), bf16),
            jax.ShapeDtypeStruct((CR, D), bf16),
            jax.ShapeDtypeStruct((count, CR, ROWS), f32),
            jax.ShapeDtypeStruct((CR, D), f32),
            jax.ShapeDtypeStruct((CR, D), f32),
            jax.ShapeDtypeStruct((CR, FF), f32),
            jax.ShapeDtypeStruct((CR, D), f32),
            jax.ShapeDtypeStruct((CR, D), f32),
        ]
        scratch = []
    else:
        out_shape = [jax.ShapeDtypeStruct((CR, PROTOS), f32)]
        scratch = [
            pltpu.VMEM((step, D), f32),
            pltpu.VMEM((step, 3 * D), bf16),
            pltpu.VMEM((step, D), bf16),
            pltpu.VMEM((rows, 2 * D), bf16),
            pltpu.VMEM((CR, D), f32),
            pltpu.VMEM((CR, D), f32),
            pltpu.VMEM((rows, D), f32),
        ]
    if packed:
        out_shape += [jax.ShapeDtypeStruct(shape, bf16) for shape in ((FF, D), (FF, D), (PROTOS, D))]
    key_bias = jnp.broadcast_to(bias.reshape(count, ROWS, 1).astype(bf16), (count, ROWS, 128))
    operands = (patches, table, bias, key_bias, gains, gains_one, *net["arrays"])
    return pl.pallas_call(
        lambda *refs: forward_kernel(save, packed, count, *refs),
        grid=(groups,),
        in_specs=[whole()] * len(operands),
        out_specs=[whole()] * len(out_shape),
        out_shape=out_shape,
        scratch_shapes=scratch,
        compiler_params=pltpu.CompilerParams(dimension_semantics=("arbitrary",), vmem_limit_bytes=megabytes(LIMITS[0 if save else 1])),
        cost_estimate=cost(30),
        name="student_forward" if save else "teacher_forward",
    )(*operands)


LIMITS = [12, 18, 20, 14, 14, 10]


def megabytes(count):
    return count * 1024 * 1024


def cost(micros):
    return pl.CostEstimate(flops=int(micros * 1e9), transcendentals=0, bytes_accessed=int(micros * 3e6))


def unit_parts(v):
    inverse = lax.rsqrt(jnp.sum(v * v, -1, keepdims=True) + 1e-06)
    return v * inverse, inverse


def whole():
    return pl.BlockSpec(memory_space=pltpu.VMEM)


def class_back_kernel(packed, count, inverse_count, *refs):
    (logs, target, mean_sum, state, kv, queries, shares, att, mid_c, expanded, last, cls) = refs[:12]
    if packed:
        (me, gains, full, w2, protos), refs = refs[12:17], refs[17:]
        (delta, s_gain, report, keep, send, dkv, dq_all, s_up, s_down) = refs
        s_proto, s_in, s_out = s_down.at[pl.ds(0, PROTOS)], s_up.at[:, pl.ds(0, 3 * D)], s_up.at[:, pl.ds(3 * D, D)]
        win, wo, w1, _ = layer_views((full,), True, 1)
    else:
        gains, weights = refs[12], refs[13:19]
        (delta, s_gain, report, s_in, s_out, s_up, s_down, s_proto, dkv, dq_all) = refs[19:]
        (win, wo, w1, w2), protos = layer_views(weights, False, 1), weights[5]
    mask = head_mask()
    row = lax.broadcasted_iota(jnp.int32, (CR, 1), 0)
    live = row < count
    log_share = logs[...]
    share = jnp.exp(log_share)
    targets = target[...]
    total = mean_sum[0].astype(f32)
    for device in range(1, mean_sum.shape[0]):
        total = total + mean_sum[device].astype(f32)
    lines = [jnp.concatenate([total[8 * m + k : 8 * m + k + 1] for k in range(PROTOS // 128)], 1) for m in range(2)]
    mean_share = jnp.concatenate(lines, 0) * (2.0 * inverse_count)
    log_mean = jnp.log(mean_share)
    cross = -jnp.sum(jnp.where(live, targets * log_share, 0.0), -1, keepdims=True)
    cross = jnp.sum(cross, 0, keepdims=True) * inverse_count
    entropy = jnp.sum(jnp.sum(mean_share * log_mean, -1, keepdims=True), 0, keepdims=True) * 0.5
    lane = lax.broadcasted_iota(jnp.int32, (8, 128), 1)
    report[...] = jnp.where(lane == 0, cross, jnp.where(lane == 1, entropy, 0.0))
    log_row = jnp.where(row < count // 2, log_mean[0:1, :], log_mean[1:2, :])
    slope = share - targets + share * (log_row - jnp.sum(share * log_row, -1, keepdims=True))
    slope = jnp.where(live, slope * (inverse_count / student_softness), 0.0).astype(bf16)
    hat_f, inv_f = normalize(last[...])
    summary = hat_f * gains[2:3, :]
    unit, inv_u = unit_parts(summary)
    proto = protos[...].astype(f32)
    proto_unit, inv_p = unit_parts(proto)
    d_unit = dot(slope, proto_unit.astype(bf16))
    d_proto = dot_at(slope, unit.astype(bf16))
    s_proto[...] = inv_p * (d_proto - proto_unit * jnp.sum(proto_unit * d_proto, -1, keepdims=True))
    if packed:
        pack_blocks(me[0], keep, send, [], [(s_proto, 32)], 288)
    d_summary = inv_u * (d_unit - unit * jnp.sum(unit * d_unit, -1, keepdims=True))
    d, gain_f = norm_back(hat_f, inv_f, gains[2:3, :], d_summary)
    s_gain[...] = jnp.zeros((8, D), f32)
    s_gain[2:3, :] = gain_f
    d_low = d.astype(bf16)
    act, gslope = gelu_parts(expanded[...], True)
    s_down[...] = dot_at(act.astype(bf16), d_low)
    d_exp = (dot_bt(d_low, w2[...]) * gslope).astype(bf16)
    if packed:
        pack_blocks(me[0], keep, send, [(s_down, 96)], [], 192)
    hat_m, inv_m = normalize(mid_c[...])
    s_up[...] = dot_at((hat_m * gains[1:2, :]).astype(bf16), d_exp)
    d_mid, gain_two = norm_back(hat_m, inv_m, gains[1:2, :], dot_bt(d_exp, w1[...]))
    s_gain[1:2, :] = gain_two
    if packed:
        pack_blocks(me[0], keep, send, [(s_up, 24)], [], 96)
    d_mid = d + d_mid
    d_mid_low = d_mid.astype(bf16)
    s_out[...] = dot_at(att[...].astype(bf16), d_mid_low)
    d_att = dot_bt(d_mid_low, wo[...]).astype(bf16)
    dq_all[...] = jnp.zeros((CR, D), f32)
    for g in range(count):
        rows = pl.ds(g * ROWS, ROWS)
        d_spread = (jnp.broadcast_to(d_att[g : g + 1, :].astype(f32), (CR, D)) * mask).astype(bf16)
        q_spread = (jnp.broadcast_to(queries[g : g + 1, :].astype(f32) * SCALE, (CR, D)) * mask).astype(bf16)
        p = shares[g]
        d_p = dot_bt(d_spread, kv[rows, pl.ds(D, D)])
        d_s = (p * (d_p - jnp.sum(p * d_p, -1, keepdims=True))).astype(bf16)
        dkv[rows, pl.ds(D, D)] = dot_at(p.astype(bf16), d_spread).astype(bf16)
        dkv[rows, pl.ds(0, D)] = dot_at(d_s, q_spread).astype(bf16)
        dq = dot(d_s, kv[rows, pl.ds(0, D)]) * mask
        dq_all[g : g + 1, :] = jnp.sum(dq, 0, keepdims=True) * SCALE
    dq_low = dq_all[...].astype(bf16)
    hat_c, _ = normalize(cls[...])
    s_in[:, :D] = dot_at((hat_c * gains[0:1, :]).astype(bf16), dq_low)
    hat, inv = normalize(state[...])
    s_in[:, D:] = dot_at((hat * gains[0:1, :]).astype(bf16), dkv[...])
    d_class = dot_bt(dq_low, win[:, :D])
    delta[...] = dot_bt(dkv[...], win[:, D:])
    for g in range(count):
        one = pl.ds(g * ROWS + CLS, 1)
        delta[one, :] = delta[one, :] + d_class[g : g + 1, :]
    d_state, gain_one = norm_back(hat, inv, gains[0:1, :], delta[...])
    s_gain[0:1, :] = gain_one
    delta[...] = d_state
    for g in range(count):
        one = pl.ds(g * ROWS + CLS, 1)
        delta[one, :] = delta[one, :] + d_mid[g : g + 1, :]
    if packed:
        pack_blocks(me[0], keep, send, [(s_up, 24)], [], 0)


BITS = {"c": 0, "x": 1, "y": 2, "z": 3}
PATHS = (("c", "x", "y", "z"), ("c", "y", "z", "x"), ("c", "z", "x", "y"))
LAYER_ROWS = 288
CHUNK_ROWS = (352, 192, 160)


def pack_blocks(me, keep, send, layered, wide, start=0):
    for path in range(3):
        for place in range(16):
            mask = 0
            for k in range(4):
                mask |= ((place >> (3 - k)) & 1) << BITS[PATHS[path][k]]
            owner = (me & 15) ^ mask
            pieces = []
            for ref, rows in layered:
                at = pl.ds(pl.multiple_of(owner * rows, 8), rows)
                for j in range(ref.shape[1] // D):
                    pieces.append(ref[at, pl.ds(D * j + 128 * path, 128)])
            for other in range(2):
                half = (me >> 4) ^ other
                for ref, rows in wide:
                    at = pl.ds(pl.multiple_of((half * 16 + owner) * rows, 8), rows)
                    pieces.append(ref[at, pl.ds(128 * path, 128)])
            value = jnp.concatenate(pieces, 0).astype(bf16)
            target, at = (keep, place) if place < 8 else (send, place - 8)
            target[path, at, pl.ds(start, value.shape[0]), :] = value


def chunk_shapes(chunk):
    return [jax.ShapeDtypeStruct((3, 8, CHUNK_ROWS[chunk], 128), bf16)] * 2


def layer_one_back(args, net, gains, inverse_count, me):
    count = args[6].shape[0]
    packed = net["fast"]
    weights = (net["arrays"][0], *net["natural"][1:]) if packed else net["arrays"]
    rows = count * ROWS
    slopes = [(D, 3 * D), (D, D), (D, FF), (FF, D), (PROTOS, D)]
    out_shape = [
        jax.ShapeDtypeStruct((rows, D), f32),
        jax.ShapeDtypeStruct((8, D), f32),
        jax.ShapeDtypeStruct((8, 128), f32),
    ]
    scratch = [pltpu.VMEM((rows, 2 * D), bf16), pltpu.VMEM((CR, D), f32)]
    if packed:
        out_shape += chunk_shapes(0)
        scratch += [pltpu.VMEM(shape, f32) for shape in ((D, FF), (FF, D))]
    else:
        out_shape += [jax.ShapeDtypeStruct(shape, f32) for shape in slopes]
    scalar = [pl.BlockSpec(memory_space=pltpu.SMEM)] if packed else []
    return pl.pallas_call(
        lambda *refs: class_back_kernel(packed, count, inverse_count, *refs),
        in_specs=[whole()] * 12 + scalar + [whole()] * (1 + len(weights)),
        out_specs=[whole()] * len(out_shape),
        out_shape=out_shape,
        scratch_shapes=scratch,
        compiler_params=pltpu.CompilerParams(vmem_limit_bytes=megabytes(LIMITS[2])),
        cost_estimate=cost(13),
        name="layer_one_back",
    )(*args, *([me] if packed else []), gains, *weights)


def mlp_back_kernel(packed, group, *refs):
    (delta, act, dgelu, mid), (gains, ups, downs), refs = (step_rows(ref, group * ROWS) for ref in refs[:4]), refs[4:7], refs[7:]
    w1 = layer_views((ups,), True, 0)[2] if packed else ups.at[pl.ds(0, D)]
    w2 = downs.at[pl.ds(0, FF)]
    first = pl.program_id(0) == 0
    if packed:
        me, d_mid, s_gain, keep, send, s_up, s_down = refs
    else:
        d_mid, s_gain, s_up, s_down = refs
    d_mid = step_rows(d_mid, group * ROWS)

    @pl.when(first)
    def _():
        s_up[...] = jnp.zeros(s_up.shape, f32)
        s_down[...] = jnp.zeros(s_down.shape, f32)
        s_gain[...] = jnp.zeros(s_gain.shape, f32)

    d = delta[...]
    d_low = d.astype(bf16)
    hat, inv = normalize(mid[...])
    normed = (hat * gains[1:2, :]).astype(bf16)
    d_normed = None
    for j in range(FF // D):
        cols = pl.ds(D * j, D)
        s_down[cols, :] += dot_at(act[:, cols], d_low)
        d_exp = (dot_bt(d_low, w2[cols, :]) * dgelu[:, cols].astype(f32)).astype(bf16)
        s_up[:, cols] += dot_at(normed, d_exp)
        part = dot_bt(d_exp, w1[:, cols])
        d_normed = part if d_normed is None else d_normed + part
    back, gain = norm_back(hat, inv, gains[1:2, :], d_normed)
    s_gain[0:1, :] += gain
    d_mid[...] = d + back
    if packed:

        @pl.when(pl.program_id(0) == pl.num_programs(0) - 1)
        def _():
            pack_blocks(me[0], keep, send, [(s_up, 24), (s_down, 96)], [])


def backward_shapes(packed, slopes, chunk):
    if packed:
        return chunk_shapes(chunk), [pltpu.VMEM(shape, f32) for shape in slopes]
    return [jax.ShapeDtypeStruct(shape, f32) for shape in slopes], []


def layer_zero_mlp_back(delta, act, dgelu, mid, net, gains, group, me):
    packed = net["fast"]
    weights = (net["arrays"][0], net["natural"][0]) if packed else net["arrays"][2:4]
    slopes, scratch = backward_shapes(packed, [(D, FF), (FF, D)], 1)
    scalar = [pl.BlockSpec(memory_space=pltpu.SMEM)] if packed else []
    rows = delta.shape[0]
    step = group * ROWS
    return pl.pallas_call(
        lambda *refs: mlp_back_kernel(packed, group, *refs),
        grid=(rows // step,),
        in_specs=[whole()] * 7 + scalar,
        out_specs=[whole()] * (2 + len(slopes)),
        out_shape=[jax.ShapeDtypeStruct((rows, D), f32), jax.ShapeDtypeStruct((8, D), f32)] + slopes,
        scratch_shapes=scratch,
        compiler_params=pltpu.CompilerParams(dimension_semantics=("arbitrary",), vmem_limit_bytes=megabytes(LIMITS[3])),
        cost_estimate=cost(17),
        name="layer_zero_mlp_back",
    )(delta, act, dgelu, mid, gains, *weights, *([me] if packed else []))


def attention_back_kernel(packed, group, *refs):
    (d_mid, state, mix, att) = (step_rows(ref, group * ROWS) for ref in refs[:4])
    if packed:
        (shares, pats, mixes, gains, gain_two, gain_one), refs = refs[4:10], refs[10:]
    else:
        (shares, pats, mixes, outs, gains, gain_two, gain_one), refs = refs[4:11], refs[11:]
    base = pl.program_id(0) * group
    share = shares.at[pl.ds(base, group)]
    win, wo = layer_views((mixes,), True, 0)[:2] if packed else (mixes.at[pl.ds(0, D)], outs.at[pl.ds(0, D)])
    if packed:
        me, keep, send, s_in, s_out, s_patch, s_vector, d_att, dmix = refs
    else:
        s_in, s_out, s_patch, s_vector, d_att, dmix = refs

    @pl.when(pl.program_id(0) == 0)
    def _():
        s_in[...] = jnp.zeros(s_in.shape, f32)
        s_out[...] = jnp.zeros(s_out.shape, f32)
        s_patch[...] = jnp.zeros(s_patch.shape, f32)
        s_vector[...] = jnp.zeros(s_vector.shape, f32)
        s_vector[ROWS + 1 : ROWS + 2, :] = gain_two[0:1, :]
        s_vector[ROWS + 2 : ROWS + 5, :] = gain_one[0:3, :]

    d_low = d_mid[...].astype(bf16)
    s_out[...] += dot_at(att[...], d_low)
    d_att[...] = dot_bt(d_low, wo[...]).astype(bf16)
    masks = half_masks()
    for g in range(group):
        rows = pl.ds(g * ROWS, ROWS)
        for pair in range(HEADS // 2):
            lanes = [pl.ds(D * part + 128 * pair, 128) for part in range(3)]
            query = mix[rows, lanes[0]] * jnp.asarray(SCALE, bf16)
            keys = mix[rows, lanes[1]] * jnp.asarray(SCALE, bf16)
            values = mix[rows, lanes[2]]
            upstream = d_att[rows, lanes[0]]
            dq = dk = dv = None
            for half in range(2):
                p = share[g, 2 * pair + half]
                up = upstream * masks[half]
                d_p = dot_bt(values, up)
                p_wide = p.astype(f32)
                weighted = p_wide * d_p
                d_s = (weighted - p_wide * jnp.sum(weighted, 0, keepdims=True)).astype(bf16)
                parts = (
                    dot_at(d_s, keys * masks[half]),
                    dot(d_s, query * masks[half]),
                    dot(p, up),
                )
                dq, dk, dv = parts if dq is None else (dq + parts[0], dk + parts[1], dv + parts[2])
            dmix[rows, lanes[0]] = dq.astype(bf16)
            dmix[rows, lanes[1]] = dk.astype(bf16)
            dmix[rows, lanes[2]] = dv.astype(bf16)
    hat, inv = normalize(state[...])
    normed = (hat * gains[0:1, :]).astype(bf16)
    s_in[...] += dot_at(normed, dmix[...])
    back, gain = norm_back(hat, inv, gains[0:1, :], dot_bt(dmix[...], win[...]))
    s_vector[ROWS : ROWS + 1, :] += gain
    d_state = d_mid[...] + back
    for g in range(group):
        one = d_state[g * ROWS : (g + 1) * ROWS]
        s_vector[0:ROWS, :] += one
        image = base + g
        s_patch[...] += dot_at(pats[image // pats.shape[1], image % pats.shape[1]], one[:PATCHES].astype(bf16))
    if packed:

        @pl.when(pl.program_id(0) == pl.num_programs(0) - 1)
        def _():
            pack_blocks(me[0], keep, send, [(s_in, 24), (s_out, 24)], [(s_patch, 24), (s_vector, 8)])


VECTORS = 256


def layer_zero_attention_back(d_mid, state, mix, share, att, patches, net, gains, gain_two, gain_one, group, me):
    packed = net["fast"]
    weights = net["arrays"][:1] if packed else net["arrays"][:2]
    slopes, scratch = backward_shapes(packed, [(D, 3 * D), (D, D), (PATCH_DIM, D), (VECTORS, D)], 2)
    scalar = [pl.BlockSpec(memory_space=pltpu.SMEM)] if packed else []
    rows = d_mid.shape[0]
    step = group * ROWS
    return pl.pallas_call(
        lambda *refs: attention_back_kernel(packed, group, *refs),
        grid=(rows // step,),
        in_specs=[whole()] * (9 + len(weights)) + scalar,
        out_specs=[whole()] * len(slopes),
        out_shape=slopes,
        scratch_shapes=scratch + [pltpu.VMEM((step, D), bf16), pltpu.VMEM((step, 3 * D), bf16)],
        compiler_params=pltpu.CompilerParams(dimension_semantics=("arbitrary",), vmem_limit_bytes=megabytes(LIMITS[4])),
        cost_estimate=cost(21),
        name="layer_zero_attention_back",
    )(d_mid, state, mix, att, share, patches, *weights, gains, gain_two, gain_one, *([me] if packed else []))


NAMES = ("mix", "out", "up", "down", "patch", "protos")
WIDTHS = {"up": FF, "down": FF, "patch": D, "mix": 3 * D, "out": D, "protos": D, "rest": 128}
PLACE = {}
COLUMNS = 0
for _key in WIDTHS:
    PLACE[_key] = COLUMNS
    COLUMNS += WIDTHS[_key]


def pack_pieces(values):
    pieces = {name: values[name] for name in ("mix", "out", "up", "patch")}
    r = values["patch"].shape[0]
    down, protos = values["down"], values["protos"]
    pieces["down"] = jnp.concatenate([down[r * j : r * (j + 1)] for j in range(4)], 1)
    pieces["protos"] = protos[:r]
    pieces["rest"] = jnp.concatenate([protos[r:, 128 * j : 128 * (j + 1)] for j in range(3)], 0)
    return pieces


def pack_kernel(*refs):
    for net in range(2):
        out = refs[12 + net]
        values = {name: ref[...].astype(f32) for name, ref in zip(NAMES, refs[6 * net : 6 * net + 6])}
        for name, piece in pack_pieces(values).items():
            out[:, pl.ds(PLACE[name], WIDTHS[name])] = piece.astype(bf16)


THIRDS = ((0, 1792), (1792, 3584), (3584, 5504))


def chain_gather(mine):
    got = swap(mine, 4)
    arrays = [jnp.stack([mine[:, a:b], got[:, a:b]]) for a, b in THIRDS]
    for stage in (1, 2, 3):
        got = [swap(arrays[path], BITS[PATHS[path][stage]]) for path in range(3)]
        arrays = [jnp.concatenate([a, g], 0) for a, g in zip(arrays, got)]
    return arrays, [swap(a, 0) for a in arrays]


CHIPS_A_STEP = 4


def unpack_kernel(me, *refs):
    ins, outs = refs[: 6 * CHIPS_A_STEP], dict(zip(NAMES, refs[6 * CHIPS_A_STEP :]))
    first_core = (me[0] & 1) == 0
    pieces = {name: [] for name in NAMES}
    for chip in range(CHIPS_A_STEP):
        mine, got = ins[6 * chip : 6 * chip + 3], ins[6 * chip + 3 : 6 * chip + 6]
        own = jnp.concatenate([ref[0].astype(f32) for ref in mine], 1)
        other = jnp.concatenate([ref[0].astype(f32) for ref in got], 1)
        for rows in (jnp.where(first_core, own, other), jnp.where(first_core, other, own)):
            for name in ("mix", "out", "up", "patch"):
                pieces[name].append(rows[:, PLACE[name] : PLACE[name] + WIDTHS[name]])
            for j in range(4):
                pieces["down"].append(rows[:, PLACE["down"] + D * j : PLACE["down"] + D * (j + 1)])
            rest = rows[:, PLACE["rest"] :]
            pieces["protos"].append(rows[:, PLACE["protos"] : PLACE["protos"] + D])
            pieces["protos"].append(jnp.concatenate([rest[8 * j : 8 * (j + 1)] for j in range(3)], 1))
    for name in NAMES:
        outs[name][...] = jnp.concatenate(pieces[name], 0).astype(bf16)


def unpack_weights(arrays, got, me):
    def index(chip, path):
        def at(i, me_ref):
            other = (CHIPS_A_STEP * i + chip) ^ (me_ref[0] >> 1)
            place = (other >> 3) & 1
            for k in range(3):
                place = place + (((other >> (BITS[PATHS[path][k + 1]] - 1)) & 1) << (k + 1))
            return place, 0, 0

        return at

    in_specs, operands = [], []
    for chip in range(CHIPS_A_STEP):
        for source in (arrays, got):
            for path in range(3):
                in_specs.append(pl.BlockSpec((1,) + source[path].shape[1:], index(chip, path)))
                operands.append(source[path])
    shapes = ((2 * D, 3 * D), (2 * D, D), (2 * D, FF), (2 * FF, D), (PATCH_DIM, D), (PROTOS, D))
    steps = 16 // CHIPS_A_STEP
    return pl.pallas_call(
        unpack_kernel,
        grid_spec=pltpu.PrefetchScalarGridSpec(
            num_scalar_prefetch=1,
            grid=(steps,),
            in_specs=in_specs,
            out_specs=[pl.BlockSpec((a // steps, b), lambda i, me_ref: (i, 0)) for a, b in shapes],
        ),
        out_shape=[jax.ShapeDtypeStruct(shape, bf16) for shape in shapes],
        compiler_params=pltpu.CompilerParams(dimension_semantics=("arbitrary",), vmem_limit_bytes=megabytes(LIMITS[5])),
        cost_estimate=cost(9),
        name="unpack_weights",
    )(me, *operands)


def natural_net(mix, out, up, down, patch, protos, fast):
    return {"packed": False, "fast": fast, "arrays": (mix, out, up, down, patch, protos)}


def gathered_net(full):
    return {"packed": True, "fast": True, "arrays": (full,)}


def plain_net(full, n):
    r = full.shape[0] // n
    part = lambda name: full[:, PLACE[name] : PLACE[name] + WIDTHS[name]]
    down = part("down").reshape(n, r, 4, D).transpose(0, 2, 1, 3).reshape(2 * FF, D)
    rest = part("rest").reshape(n, 3, r // 3, 128).transpose(0, 2, 1, 3).reshape(n, r // 3, D)
    protos = jnp.concatenate([part("protos").reshape(n, r, D), rest], 1).reshape(PROTOS, D)
    return natural_net(part("mix"), part("out"), part("up"), down, part("patch"), protos, False)


def gather_networks(student, teacher, me, n):
    gather = lambda rows: lax.all_gather(rows, "dp", axis=0, tiled=True)
    r = student[0].shape[0]
    if n != 32:
        nets = []
        for shards in (student, teacher):
            pieces = pack_pieces(dict(zip(NAMES, shards)))
            nets.append(plain_net(gather(jnp.concatenate([pieces[name].astype(bf16) for name in WIDTHS], 1)), n))
        return nets
    student_rows, teacher_rows = pl.pallas_call(
        pack_kernel,
        in_specs=[whole()] * 12,
        out_specs=[whole()] * 2,
        out_shape=[jax.ShapeDtypeStruct((r, COLUMNS), bf16)] * 2,
        cost_estimate=cost(2),
        name="pack_weights",
    )(*student, *teacher)
    full = gather(student_rows)
    arrays, got = chain_gather(teacher_rows)
    return gathered_net(full), natural_net(*unpack_weights(arrays, got, me), True)


def swap(value, bit):
    size = lax.axis_size("dp")
    return lax.ppermute(value, "dp", [(i, i ^ (1 << bit)) for i in range(size)])


def core_stage(parts):
    got = [swap(send, 0) for _, send in parts]
    one, mlp, rest = [(keep.astype(f32) + g.astype(f32)).astype(bf16) for (keep, _), g in zip(parts, got)]

    def join(path, places):
        a, b, c = one[path, places], mlp[path, places], rest[path, places]
        return jnp.concatenate([a[:, :288], c[:, :96], b, a[:, 288:320], c[:, 96:128], a[:, 320:], c[:, 128:]], 1)

    return [(join(path, slice(0, 4)), join(path, slice(4, 8))) for path in range(3)]


def axis_stage(stage, arrays):
    got = [swap(arrays[path][1], BITS[PATHS[path][stage]]) for path in range(3)]
    total = [arrays[path][0].astype(f32) + got[path].astype(f32) for path in range(3)]
    if stage == 3:
        return jnp.concatenate(total, 0)
    half = total[0].shape[0] // 2
    total = [t.astype(bf16) for t in total]
    return [(t[:half], t[half:]) for t in total]


def scatter_gradients(parts, me):
    arrays = core_stage(parts)
    for stage in (1, 2, 3):
        arrays = axis_stage(stage, arrays)
    upper = (me[0] >> 4) == 1
    one, zero = arrays[:, :288], arrays[:, 288:576]
    keep = jnp.concatenate([jnp.where(upper, one, zero), arrays[:, 576:640]], 1)
    send = jnp.concatenate([jnp.where(upper, zero, one), arrays[:, 640:]], 1)
    return keep, swap(send.astype(bf16), 4)


def square_sum(value):
    return jnp.sum(jnp.sum(value * value, -1, keepdims=True), 0, keepdims=True)


def three_parts(value):
    high = value.astype(bf16).astype(f32)
    middle = (value - high).astype(bf16).astype(f32)
    return high, middle, value - high - middle


def collect_kernel(*refs):
    (keep, got, report) = refs[:3]
    (mix, out, up, down, patch, protos, line) = refs[3:]
    vectors = []
    for path in range(3):
        a = keep[path] + got[path].astype(f32)
        lanes = pl.ds(128 * path, 128)
        for j in range(3):
            mix[:, pl.ds(D * j + 128 * path, 128)] = a[24 * j : 24 * (j + 1)]
        out[:, lanes] = a[72:96]
        for j in range(4):
            up[:, pl.ds(D * j + 128 * path, 128)] = a[96 + 24 * j : 120 + 24 * j]
        down[:, lanes] = a[192:288]
        protos[:, lanes] = a[288:320]
        patch[:, lanes] = a[320:344]
        vectors.append(a[344:352])
    write_line(line, (mix, out, up, down, patch, protos), jnp.concatenate(vectors, 1), report)


def write_line(line, slopes, vectors, report):
    squares = square_sum(vectors)
    for ref in slopes:
        squares = squares + square_sum(ref[...])
    cross = report[0:1, 0:1]
    rows = vectors.shape[0]
    lane = lax.broadcasted_iota(jnp.int32, (rows, 128), 1)
    row = lax.broadcasted_iota(jnp.int32, (rows, 128), 0)
    tail = jnp.zeros((rows, 128), f32)
    for i, part in enumerate(three_parts(squares) + three_parts(cross)):
        tail = jnp.where(jnp.logical_and(lane == i, row == 0), part, tail)
    full = jnp.concatenate([vectors, tail], 1).astype(bf16)
    for d in range(line.shape[0]):
        line[d] = full


RATES = (matrix_rate,) * 5 + (table_rate,) * 2


def update_kernel(rows, *refs):
    (fixes, report, arrived), refs = refs[:3], refs[3:]
    slopes, masters, firsts, seconds = refs[:6], refs[6:13], refs[13:20], refs[20:27]
    news, moments, squares, scalars, vector = refs[27:34], refs[34:41], refs[41:48], refs[48:50], refs[50]
    tail = jnp.zeros((1, 128), f32)
    for d in range(arrived.shape[0]):
        tail = tail + arrived[d, 0:1, pl.ds(D, 128)].astype(f32)
    lane = lax.broadcasted_iota(jnp.int32, (1, 128), 1)
    norm = jnp.sqrt(jnp.sum(jnp.where(lane < 3, tail, 0.0), -1, keepdims=True))
    cross = jnp.sum(jnp.where(jnp.logical_and(lane >= 3, lane < 6), tail, 0.0), -1, keepdims=True)
    loss = cross + report[0:1, 1:2]
    scalars[0][...] = loss
    scalars[1][...] = norm
    factor = jnp.minimum(1.0, clip_limit / (norm + 1e-06))
    per_device = arrived.shape[1]
    table = jnp.concatenate([arrived[d, :, pl.ds(0, D)].astype(f32) for d in range(arrived.shape[0])], 0)
    vector[0:1, :] = table[CLS : CLS + 1]
    vector[1:SEQ, :] = table[:PATCHES]
    vector[SEQ:VROWS, :] = table[ROWS : ROWS + 5]
    scale_one, scale_two = 1.0 / fixes[0], 1.0 / fixes[1]
    order = (0, 1, 2, 3, 4, None, 5)
    for i in range(7):
        slope = vector if order[i] is None else slopes[order[i]]
        clipped = slope[...] * factor
        moment = beta_one * firsts[i][...] + (1.0 - beta_one) * clipped
        square = beta_two * seconds[i][...] + (1.0 - beta_two) * clipped * clipped
        stepped = (moment * scale_one) / (jnp.sqrt(square * scale_two) + adam_floor)
        weight = masters[i][...]
        news[i][...] = weight - RATES[i] * (stepped + decay_rate * weight)
        moments[i][...] = moment
        squares[i][...] = square


def update_rows(slopes, arrived, report, masters, firsts, seconds, fixes):
    shapes = [jax.ShapeDtypeStruct(w.shape, f32) for w in masters]
    out_shape = shapes * 3 + [jax.ShapeDtypeStruct((1, 1), f32)] * 2
    return pl.pallas_call(
        lambda *refs: update_kernel(None, *refs),
        in_specs=[pl.BlockSpec(memory_space=pltpu.SMEM)] + [whole()] * 29,
        out_specs=[whole()] * len(out_shape),
        out_shape=out_shape,
        scratch_shapes=[pltpu.VMEM((VROWS, D), f32)],
        compiler_params=pltpu.CompilerParams(vmem_limit_bytes=megabytes(LIMITS[5])),
        cost_estimate=cost(4),
        name="update_rows",
    )(fixes, report, arrived, *slopes, *masters, *firsts, *seconds)


def update_plain(slopes, arrived, report, masters, firsts, seconds, fixes):
    tail = jnp.sum(arrived[:, 0, D:].astype(f32), 0)
    table = arrived[:, :, :D].astype(f32).reshape(-1, D)
    vector = jnp.concatenate([table[CLS : CLS + 1], table[:PATCHES], table[ROWS : ROWS + 5]], 0)
    norm = jnp.sqrt(tail[0] + tail[1] + tail[2])
    loss = tail[3] + tail[4] + tail[5] + report[0, 1]
    factor = jnp.minimum(1.0, clip_limit / (norm + 1e-06))
    slopes = list(slopes[:5]) + [vector, slopes[5]]
    news, moments, squares = ([], [], [])
    for weight, first, second, slope, rate in zip(masters, firsts, seconds, slopes, RATES):
        clipped = slope * factor
        moment = beta_one * first + (1.0 - beta_one) * clipped
        square = beta_two * second + (1.0 - beta_two) * clipped * clipped
        stepped = moment / fixes[0] / (jnp.sqrt(square / fixes[1]) + adam_floor)
        news.append(weight - rate * (stepped + decay_rate * weight))
        moments.append(moment)
        squares.append(square)
    return (*news, *moments, *squares, loss[None, None], norm[None, None])


def collect(keep, got, report, n, r):
    shapes = [(r, 3 * D), (r, D), (r, FF), (4 * r, D), (r, D), (4 * r // 3, D)]
    out_shape = [jax.ShapeDtypeStruct(shape, f32) for shape in shapes] + [jax.ShapeDtypeStruct((n, VECTORS // n, 512), bf16)]
    *slopes, line = pl.pallas_call(
        collect_kernel,
        in_specs=[whole()] * 3,
        out_specs=[whole()] * len(out_shape),
        out_shape=out_shape,
        compiler_params=pltpu.CompilerParams(vmem_limit_bytes=megabytes(LIMITS[5])),
        cost_estimate=cost(3),
        name="collect_gradients",
    )(keep, got, report)
    return slopes, line


def collect_plain(one, mlp, rest, report, n):
    mix1, out1, up1, down1, protos = one
    up0, down0 = mlp
    mix0, out0, patch, vectors = rest
    scatter = lambda *v: lax.psum_scatter(jnp.concatenate(v, 0), "dp", scatter_dimension=0, tiled=True)
    slopes = [scatter(mix0, mix1), scatter(out0, out1), scatter(up0, up1), scatter(down0, down1), scatter(patch), scatter(protos)]
    vectors = scatter(vectors)
    squares = sum(jnp.sum(s * s) for s in slopes) + jnp.sum(vectors * vectors)
    tail = jnp.stack(three_parts(squares) + three_parts(report[0, 0]))
    tail = jnp.zeros((vectors.shape[0], 128), f32).at[0, :6].set(tail)
    line = jnp.concatenate([vectors, tail], 1).astype(bf16)
    return slopes, jnp.broadcast_to(line[None], (n,) + line.shape)


def local(
    attention_in, attention_out, hidden_in, hidden_out, patch_weight, vector_rows, prototypes,
    first_attention_in, first_attention_out, first_hidden_in, first_hidden_out, first_patch_weight, first_vector_rows, first_prototypes,
    second_attention_in, second_attention_out, second_hidden_in, second_hidden_out, second_patch_weight, second_vector_rows, second_prototypes,
    teacher_attention_in, teacher_attention_out, teacher_hidden_in, teacher_hidden_out, teacher_patch_weight, teacher_vector_rows, teacher_prototypes,
    anchor_patches, target_patches, patch_keep, step_count,
):
    n = lax.axis_size("dp")
    me = lax.axis_index("dp").astype(jnp.int32)[None]
    groups, per = anchor_patches.shape[:2]
    count = groups * per
    inverse_count = 1.0 / (count * n)
    masters = (attention_in, attention_out, hidden_in, hidden_out, patch_weight, vector_rows, prototypes)
    firsts = (first_attention_in, first_attention_out, first_hidden_in, first_hidden_out, first_patch_weight, first_vector_rows, first_prototypes)
    seconds = (second_attention_in, second_attention_out, second_hidden_in, second_hidden_out, second_patch_weight, second_vector_rows, second_prototypes)
    student, teacher = gather_networks(
        (attention_in, attention_out, hidden_in, hidden_out, patch_weight, prototypes),
        (teacher_attention_in, teacher_attention_out, teacher_hidden_in, teacher_hidden_out, teacher_patch_weight, teacher_prototypes),
        me,
        n,
    )

    def table_of(rows):
        return jnp.concatenate([rows[1:SEQ], rows[0:1], jnp.zeros((ROWS - SEQ, D), f32)], 0)

    def gains_of(rows):
        zeros = jnp.zeros((5, D), f32)
        first = jnp.concatenate([rows[SEQ : SEQ + 2], jnp.zeros((6, D), f32)], 0)
        second = jnp.concatenate([rows[SEQ + 2 : SEQ + 5], zeros], 0)
        return first, second

    keep = patch_keep.reshape(count, PATCHES)
    bias = jnp.where(keep == 1, 0.0, -1000000000.0).astype(f32)
    ends = jnp.where(jnp.arange(ROWS - PATCHES) == 0, 0.0, -1000000000.0).astype(f32)
    ends = jnp.broadcast_to(ends, (count, ROWS - PATCHES))
    bias = jnp.concatenate([bias, ends], 1)[:, None]
    plain = jnp.concatenate([jnp.zeros((count, PATCHES), f32), ends], 1)[:, None]
    gains0, gains1 = gains_of(vector_rows)
    teacher_rows = teacher_vector_rows.astype(f32)
    teacher_gains0, teacher_gains1 = gains_of(teacher_rows)
    counter = step_count.astype(f32)
    fixes = jnp.stack([1.0 - beta_one**counter, 1.0 - beta_two**counter])

    (targets,) = forward(target_patches, table_of(teacher_rows), plain, teacher, teacher_gains0, teacher_gains1, False, n)
    if student["fast"]:
        targets, bias = lax.optimization_barrier((targets, bias))
    state1, state0, mix, share, att, mid, act, dgelu, logs, sums, kv, queries, shares, att_c, mid_c, expanded, last, cls, *natural = forward(
        anchor_patches, table_of(vector_rows), bias, student, gains0, gains1, True, n)
    student["natural"] = natural
    mean_sum = lax.all_to_all(sums, "dp", 0, 0, tiled=True)
    delta, gain_one, report, *one = layer_one_back(
        (logs, targets, mean_sum, state1, kv, queries, shares, att_c, mid_c, expanded, last, cls), student, gains1, inverse_count, me)
    d_mid, gain_two, *mlp = layer_zero_mlp_back(delta, act, dgelu, mid, student, gains0, GROUP, me)
    rest = layer_zero_attention_back(d_mid, state0, mix, share, att, anchor_patches, student, gains0, gain_two, gain_one, GROUP, me)
    if student["fast"]:
        slopes, line = collect(*scatter_gradients([one, mlp, rest], me), report, n, attention_in.shape[0])
        update = update_rows
    else:
        slopes, line = collect_plain(one, mlp, rest, report, n)
        update = update_plain
    arrived = lax.all_to_all(line, "dp", 0, 0, tiled=True)
    *states, loss, norm = update(slopes, arrived, report, masters, firsts, seconds, fixes)
    return (loss[0, 0], norm[0, 0], *states)


GROUP = 3


def solution(mesh):
    rows, same, images = P("dp", None), P(), P(None, "dp", None, None)
    weights = (rows,) * 5 + (same, rows)
    return jax.shard_map(
        local,
        mesh=mesh,
        in_specs=weights * 4 + (images, images, P(None, "dp", None), same),
        out_specs=(same, same) + weights * 3,
        check_vma=False,
    )
```

```python
import jax
import jax.numpy as jnp
from jax import lax
from jax.experimental import pallas as pl
from jax.experimental.pallas import tpu as pltpu
from jax.sharding import PartitionSpec as P

D = 384
HEADS = 6
HEAD_DIM = 64
FF = 1536
PATCHES = 196
PATCH_DIM = 768
PROTOS = 1024
SEQ = 197
VROWS = 202
ROWS = 208
CLS = 196
WIDE = 512
CR = 16
SCALE = HEAD_DIM ** (-0.5)

student_softness = 0.04
teacher_sharpness = 0.02
clip_limit = 0.01
matrix_rate = 0.05
table_rate = 0.4
decay_rate = 0.05
beta_one = 0.9
beta_two = 0.999
adam_floor = 1e-08

f32 = jnp.float32
bf16 = jnp.bfloat16
GELU_C = 0.7978845608028654
GELU_A = 0.044715


def dot(a, b):
    return lax.dot_general(a, b, (((1,), (0,)), ((), ())), preferred_element_type=f32)


def dot_bt(a, b):
    return lax.dot_general(a, b, (((1,), (1,)), ((), ())), preferred_element_type=f32)


def dot_at(a, b):
    return lax.dot_general(a, b, (((0,), (0,)), ((), ())), preferred_element_type=f32)


def normalize(x):
    centre = x - jnp.sum(x, -1, keepdims=True) * (1.0 / D)
    spread = jnp.sum(centre * centre, -1, keepdims=True) * (1.0 / D)
    inverse = lax.rsqrt(spread + 1e-06)
    return centre * inverse, inverse


def norm_back(hat, inverse, gain, upstream):
    gain_slope = jnp.sum(upstream * hat, 0, keepdims=True)
    scaled = upstream * gain
    mean_one = jnp.sum(scaled, -1, keepdims=True) * (1.0 / D)
    mean_two = jnp.sum(scaled * hat, -1, keepdims=True) * (1.0 / D)
    return inverse * (scaled - mean_one - hat * mean_two), gain_slope


def gelu_parts(x, slope):
    square = x * x
    t = jnp.tanh(x * (GELU_C + (GELU_C * GELU_A) * square))
    half = 0.5 + 0.5 * t
    act = x * half
    if not slope:
        return act, None
    inner = GELU_C + (3.0 * GELU_C * GELU_A) * square
    return act, half + act * (1.0 - t) * inner


def half_masks():
    lane = lax.broadcasted_iota(jnp.int32, (1, 128), 1)
    first = jnp.where(lane < HEAD_DIM, 1.0, 0.0)
    return first.astype(bf16), (1.0 - first).astype(bf16)


def spot_masks():
    lane = lax.broadcasted_iota(jnp.int32, (1, 128), 1)
    return jnp.where(lane == HEAD_DIM, 1.0, 0.0).astype(bf16), jnp.where(lane == 0, 1.0, 0.0).astype(bf16)


def head_mask():
    row = lax.broadcasted_iota(jnp.int32, (CR, D), 0)
    lane = lax.broadcasted_iota(jnp.int32, (CR, D), 1)
    low = row * HEAD_DIM
    return jnp.where(jnp.logical_and(lane >= low, lane < low + HEAD_DIM), 1.0, 0.0)


def natural_down(ref, natural):
    for pair in range(8):
        rows = ref[pl.ds(48 * pair, 48), :].astype(f32)
        pieces = [rows[24 * b : 24 * (b + 1), D * j : D * (j + 1)] for b in range(2) for j in range(4)]
        natural[pl.ds(192 * pair, 192), :] = jnp.concatenate(pieces, 0).astype(bf16)


def natural_protos(ref, rest, natural):
    for pair in range(16):
        rows = ref[pl.ds(48 * pair, 48), :].astype(f32)
        tail = rest[pl.ds(48 * pair, 48), :].astype(f32)
        pieces = []
        for b in range(2):
            pieces.append(rows[24 * b : 24 * (b + 1)])
            pieces.append(jnp.concatenate([tail[24 * b + 8 * j : 24 * b + 8 * (j + 1)] for j in range(3)], 1))
        natural[pl.ds(64 * pair, 64), :] = jnp.concatenate(pieces, 0).astype(bf16)


def layer_views(weights, packed, layer):
    if packed:
        (full,) = weights
        at = lambda name: full.at[pl.ds(D * layer, D), pl.ds(PLACE[name], WIDTHS[name])]
        return tuple(at(name) for name in ("mix", "out", "up", "down"))
    mix, out, up, down = weights[:4]
    rows = pl.ds(D * layer, D)
    return mix.at[rows], out.at[rows], up.at[rows], down.at[pl.ds(FF * layer, FF)]


def forward_kernel(save, packed, count, *refs):
    (pats, tab, bias_all, key_bias_all, gains, gains_one), refs = refs[:6], refs[6:]
    weights, refs = refs[: 1 if packed else 6], refs[1 if packed else 6 :]
    group = count
    per = pats.shape[1]
    if save:
        out, first, mix, share, att, mid = refs[:6]
        class_refs, naturals = refs[6:16], refs[16:]
    else:
        share = mid = None
        (target, first, mix, att, kv, att_c, cls, out) = refs[:8]
        class_refs = (target, kv, att_c, cls)
    win, wo, w1, w2 = layer_views(weights, packed, 0)
    if packed:
        down, down_one, protos = naturals
        wp = weights[0].at[:, pl.ds(PLACE["patch"], D)]
        natural_down(w2, down)
    else:
        wp, down = weights[4], w2
    table = tab[...]
    for g in range(group):
        embedded = dot(pats[g // per, g % per], wp[...])
        first[pl.ds(g * ROWS, PATCHES), :] = embedded + table[:PATCHES]
        first[pl.ds(g * ROWS + PATCHES, ROWS - PATCHES), :] = table[PATCHES:]
    state = first[...]
    hat, _ = normalize(state)
    normed = (hat * gains[0:1, :]).astype(bf16)
    mix[...] = dot(normed, win[...]).astype(bf16)
    masks, spots = half_masks(), spot_masks()

    for g in range(group):
        rows = pl.ds(g * ROWS, ROWS)
        key_bias = key_bias_all[g]
        for pair in range(HEADS // 2):
            query = mix[rows, pl.ds(128 * pair, 128)] * jnp.asarray(SCALE, bf16)
            keys = mix[rows, pl.ds(D + 128 * pair, 128)]
            values = mix[rows, pl.ds(2 * D + 128 * pair, 128)]
            total = None
            for half in range(2):
                scores = dot_bt(keys * masks[half] + key_bias * spots[half], query * masks[half] + spots[half])
                e = jnp.exp(scores - jnp.max(scores, 0, keepdims=True))
                p = (e * (1.0 / jnp.sum(e, 0, keepdims=True))).astype(bf16)
                if save:
                    share[g, 2 * pair + half] = p
                o = dot_at(p, values * masks[half])
                total = o if total is None else total + o
            att[rows, pl.ds(128 * pair, 128)] = total.astype(bf16)
    middle = first[...] + dot(att[...], wo[...])
    if save:
        mid[...] = middle
    hat, _ = normalize(middle)
    normed = (hat * gains[1:2, :]).astype(bf16)
    result = middle
    for j in range(FF // WIDE):
        cols = pl.ds(WIDE * j, WIDE)
        a, _ = gelu_parts(dot(normed, w1[:, cols]), False)
        result = result + dot(a.astype(bf16), down[cols, :])
    out[...] = result
    win, wo, w1, w2 = layer_views(weights, packed, 1)
    if packed:
        natural_down(w2, down_one)
        natural_protos(weights[0].at[:, pl.ds(PLACE["protos"], D)], weights[0].at[:, pl.ds(PLACE["rest"], 128)], protos)
        late = (win, wo, w1, down_one, protos)
    else:
        late = (win, wo, w1, w2, weights[5])
    class_forward(save, count, out, bias_all, late, gains_one, class_refs)


def class_forward(student, count, state, bias, weights, gains, refs):
    win, wo, w1, w2, protos = weights
    if student:
        (logs, sums, kv, queries, shares, att, mid_c, expanded_out, last, cls) = refs
    else:
        (target, kv, att, cls) = refs
    hat, _ = normalize(state[...])
    normed = (hat * gains[0:1, :]).astype(bf16)
    kv[...] = dot(normed, win[:, D:]).astype(bf16)
    cls[...] = jnp.zeros((CR, D), f32)
    for g in range(count):
        cls[g : g + 1, :] = state[pl.ds(g * ROWS + CLS, 1), :]
    class_state = cls[...]
    hat, _ = normalize(class_state)
    query = dot((hat * gains[0:1, :]).astype(bf16), win[:, :D]).astype(bf16)
    if student:
        queries[...] = query
    mask = head_mask()
    for g in range(count):
        rows = pl.ds(g * ROWS, ROWS)
        spread = (jnp.broadcast_to(query[g : g + 1, :].astype(f32) * SCALE, (CR, D)) * mask).astype(bf16)
        scores = dot_bt(spread, kv[rows, pl.ds(0, D)]) + bias[g]
        e = jnp.exp(scores - jnp.max(scores, -1, keepdims=True))
        p = e * (1.0 / jnp.sum(e, -1, keepdims=True))
        if student:
            shares[g] = p
        o = dot(p.astype(bf16), kv[rows, pl.ds(D, D)])
        att[g : g + 1, :] = jnp.sum(o * mask, 0, keepdims=True)
    att[count:, :] = jnp.zeros((CR - count, D), f32)
    middle = class_state + dot(att[...].astype(bf16), wo[...])
    hat, _ = normalize(middle)
    expanded = dot((hat * gains[1:2, :]).astype(bf16), w1[...])
    act, _ = gelu_parts(expanded, False)
    result = middle + dot(act.astype(bf16), w2[...])
    if student:
        mid_c[...] = middle
        expanded_out[...] = expanded
        last[...] = result
    hat, _ = normalize(result)
    unit, _ = unit_parts(hat * gains[2:3, :])
    proto_unit, _ = unit_parts(protos[...].astype(f32))
    raw = dot_bt(unit.astype(bf16), proto_unit.astype(bf16))
    logits = raw * (1.0 / (student_softness if student else teacher_sharpness))
    logits = logits - jnp.max(logits, -1, keepdims=True)
    e = jnp.exp(logits)
    total = jnp.sum(e, -1, keepdims=True)
    if student:
        log_share = logits - jnp.log(total)
        logs[...] = log_share
        share = jnp.exp(log_share)
        row = lax.broadcasted_iota(jnp.int32, (CR, PROTOS), 0)
        per = count // 2
        lines = []
        for m in range(2):
            inside = jnp.logical_and(row >= m * per, row < (m + 1) * per)
            line = jnp.sum(jnp.where(inside, share, 0.0), 0, keepdims=True)
            lines += [line[:, 128 * k : 128 * (k + 1)] for k in range(PROTOS // 128)]
        lines = jnp.concatenate(lines, 0)
        for d in range(sums.shape[0]):
            sums[d] = lines.astype(bf16)
    else:
        target[...] = e / total


def forward(patches, table, bias, net, gains, gains_one, save, n):
    groups, group = patches.shape[:2]
    count = groups * group
    rows = count * ROWS
    packed = net["packed"]
    if save:
        out_shape = [
            jax.ShapeDtypeStruct((rows, D), f32),
            jax.ShapeDtypeStruct((rows, D), f32),
            jax.ShapeDtypeStruct((rows, 3 * D), bf16),
            jax.ShapeDtypeStruct((count, HEADS, ROWS, ROWS), bf16),
            jax.ShapeDtypeStruct((rows, D), bf16),
            jax.ShapeDtypeStruct((rows, D), f32),
            jax.ShapeDtypeStruct((CR, PROTOS), f32),
            jax.ShapeDtypeStruct((n, 16, 128), bf16),
            jax.ShapeDtypeStruct((rows, 2 * D), bf16),
            jax.ShapeDtypeStruct((CR, D), bf16),
            jax.ShapeDtypeStruct((count, CR, ROWS), f32),
            jax.ShapeDtypeStruct((CR, D), f32),
            jax.ShapeDtypeStruct((CR, D), f32),
            jax.ShapeDtypeStruct((CR, FF), f32),
            jax.ShapeDtypeStruct((CR, D), f32),
            jax.ShapeDtypeStruct((CR, D), f32),
        ]
        scratch = []
    else:
        out_shape = [jax.ShapeDtypeStruct((CR, PROTOS), f32)]
        scratch = [
            pltpu.VMEM((rows, D), f32),
            pltpu.VMEM((rows, 3 * D), bf16),
            pltpu.VMEM((rows, D), bf16),
            pltpu.VMEM((rows, 2 * D), bf16),
            pltpu.VMEM((CR, D), f32),
            pltpu.VMEM((CR, D), f32),
            pltpu.VMEM((rows, D), f32),
        ]
    if packed:
        out_shape += [jax.ShapeDtypeStruct(shape, bf16) for shape in ((FF, D), (FF, D), (PROTOS, D))]
    key_bias = jnp.broadcast_to(bias.reshape(count, ROWS, 1).astype(bf16), (count, ROWS, 128))
    operands = (patches, table, bias, key_bias, gains, gains_one, *net["arrays"])
    return pl.pallas_call(
        lambda *refs: forward_kernel(save, packed, count, *refs),
        in_specs=[whole()] * len(operands),
        out_specs=[whole()] * len(out_shape),
        out_shape=out_shape,
        scratch_shapes=scratch,
        compiler_params=pltpu.CompilerParams(vmem_limit_bytes=megabytes(LIMITS[0 if save else 1])),
        cost_estimate=cost(30),
        name="student_forward" if save else "teacher_forward",
    )(*operands)


LIMITS = [18, 18, 18, 18, 18, 10, 18]


def megabytes(count):
    return count * 1024 * 1024


def cost(micros):
    return pl.CostEstimate(flops=int(micros * 1e9), transcendentals=0, bytes_accessed=int(micros * 3e6))


def unit_parts(v):
    inverse = lax.rsqrt(jnp.sum(v * v, -1, keepdims=True) + 1e-06)
    return v * inverse, inverse


def whole():
    return pl.BlockSpec(memory_space=pltpu.VMEM)


def class_back_kernel(packed, count, inverse_count, *refs):
    (logs, target, mean_sum, state, kv, queries, shares, att, mid_c, expanded, last, cls) = refs[:12]
    if packed:
        (me, gains, full, w2, protos), refs = refs[12:17], refs[17:]
        (delta, s_gain, report, keep, send, dkv, dq_all, s_up, s_down) = refs
        s_proto, s_in, s_out = s_down.at[pl.ds(0, PROTOS)], s_up.at[:, pl.ds(0, 3 * D)], s_up.at[:, pl.ds(3 * D, D)]
        win, wo, w1, _ = layer_views((full,), True, 1)
    else:
        gains, weights = refs[12], refs[13:19]
        (delta, s_gain, report, s_in, s_out, s_up, s_down, s_proto, dkv, dq_all) = refs[19:]
        (win, wo, w1, w2), protos = layer_views(weights, False, 1), weights[5]
    mask = head_mask()
    row = lax.broadcasted_iota(jnp.int32, (CR, 1), 0)
    live = row < count
    log_share = logs[...]
    share = jnp.exp(log_share)
    targets = target[...]
    total = mean_sum[0].astype(f32)
    for device in range(1, mean_sum.shape[0]):
        total = total + mean_sum[device].astype(f32)
    lines = [jnp.concatenate([total[8 * m + k : 8 * m + k + 1] for k in range(PROTOS // 128)], 1) for m in range(2)]
    mean_share = jnp.concatenate(lines, 0) * (2.0 * inverse_count)
    log_mean = jnp.log(mean_share)
    cross = -jnp.sum(jnp.where(live, targets * log_share, 0.0), -1, keepdims=True)
    cross = jnp.sum(cross, 0, keepdims=True) * inverse_count
    entropy = jnp.sum(jnp.sum(mean_share * log_mean, -1, keepdims=True), 0, keepdims=True) * 0.5
    lane = lax.broadcasted_iota(jnp.int32, (8, 128), 1)
    report[...] = jnp.where(lane == 0, cross, jnp.where(lane == 1, entropy, 0.0))
    log_row = jnp.where(row < count // 2, log_mean[0:1, :], log_mean[1:2, :])
    slope = share - targets + share * (log_row - jnp.sum(share * log_row, -1, keepdims=True))
    slope = jnp.where(live, slope * (inverse_count / student_softness), 0.0).astype(bf16)
    hat_f, inv_f = normalize(last[...])
    summary = hat_f * gains[2:3, :]
    unit, inv_u = unit_parts(summary)
    proto = protos[...].astype(f32)
    proto_unit, inv_p = unit_parts(proto)
    d_unit = dot(slope, proto_unit.astype(bf16))
    d_proto = dot_at(slope, unit.astype(bf16))
    s_proto[...] = inv_p * (d_proto - proto_unit * jnp.sum(proto_unit * d_proto, -1, keepdims=True))
    if packed:
        pack_blocks(me[0], keep, send, [], [(s_proto, 32)], 288)
    d_summary = inv_u * (d_unit - unit * jnp.sum(unit * d_unit, -1, keepdims=True))
    d, gain_f = norm_back(hat_f, inv_f, gains[2:3, :], d_summary)
    s_gain[...] = jnp.zeros((8, D), f32)
    s_gain[2:3, :] = gain_f
    d_low = d.astype(bf16)
    act, gslope = gelu_parts(expanded[...], True)
    s_down[...] = dot_at(act.astype(bf16), d_low)
    d_exp = (dot_bt(d_low, w2[...]) * gslope).astype(bf16)
    if packed:
        pack_blocks(me[0], keep, send, [(s_down, 96)], [], 192)
    hat_m, inv_m = normalize(mid_c[...])
    s_up[...] = dot_at((hat_m * gains[1:2, :]).astype(bf16), d_exp)
    d_mid, gain_two = norm_back(hat_m, inv_m, gains[1:2, :], dot_bt(d_exp, w1[...]))
    s_gain[1:2, :] = gain_two
    if packed:
        pack_blocks(me[0], keep, send, [(s_up, 24)], [], 96)
    d_mid = d + d_mid
    d_mid_low = d_mid.astype(bf16)
    s_out[...] = dot_at(att[...].astype(bf16), d_mid_low)
    d_att = dot_bt(d_mid_low, wo[...]).astype(bf16)
    dq_all[...] = jnp.zeros((CR, D), f32)
    for g in range(count):
        rows = pl.ds(g * ROWS, ROWS)
        d_spread = (jnp.broadcast_to(d_att[g : g + 1, :].astype(f32), (CR, D)) * mask).astype(bf16)
        q_spread = (jnp.broadcast_to(queries[g : g + 1, :].astype(f32) * SCALE, (CR, D)) * mask).astype(bf16)
        p = shares[g]
        d_p = dot_bt(d_spread, kv[rows, pl.ds(D, D)])
        d_s = (p * (d_p - jnp.sum(p * d_p, -1, keepdims=True))).astype(bf16)
        dkv[rows, pl.ds(D, D)] = dot_at(p.astype(bf16), d_spread).astype(bf16)
        dkv[rows, pl.ds(0, D)] = dot_at(d_s, q_spread).astype(bf16)
        dq = dot(d_s, kv[rows, pl.ds(0, D)]) * mask
        dq_all[g : g + 1, :] = jnp.sum(dq, 0, keepdims=True) * SCALE
    dq_low = dq_all[...].astype(bf16)
    hat_c, _ = normalize(cls[...])
    s_in[:, :D] = dot_at((hat_c * gains[0:1, :]).astype(bf16), dq_low)
    hat, inv = normalize(state[...])
    s_in[:, D:] = dot_at((hat * gains[0:1, :]).astype(bf16), dkv[...])
    d_class = dot_bt(dq_low, win[:, :D])
    delta[...] = dot_bt(dkv[...], win[:, D:])
    for g in range(count):
        one = pl.ds(g * ROWS + CLS, 1)
        delta[one, :] = delta[one, :] + d_class[g : g + 1, :]
    d_state, gain_one = norm_back(hat, inv, gains[0:1, :], delta[...])
    s_gain[0:1, :] = gain_one
    delta[...] = d_state
    for g in range(count):
        one = pl.ds(g * ROWS + CLS, 1)
        delta[one, :] = delta[one, :] + d_mid[g : g + 1, :]
    if packed:
        pack_blocks(me[0], keep, send, [(s_up, 24)], [], 0)


BITS = {"c": 0, "x": 1, "y": 2, "z": 3}
PATHS = (("c", "x", "y", "z"), ("c", "y", "z", "x"), ("c", "z", "x", "y"))
LAYER_ROWS = 288
CHUNK_ROWS = (352, 192, 160)


def pack_blocks(me, keep, send, layered, wide, start=0):
    for path in range(3):
        for place in range(16):
            mask = 0
            for k in range(4):
                mask |= ((place >> (3 - k)) & 1) << BITS[PATHS[path][k]]
            owner = (me & 15) ^ mask
            pieces = []
            for ref, rows in layered:
                at = pl.ds(pl.multiple_of(owner * rows, 8), rows)
                for j in range(ref.shape[1] // D):
                    pieces.append(ref[at, pl.ds(D * j + 128 * path, 128)])
            for other in range(2):
                half = (me >> 4) ^ other
                for ref, rows in wide:
                    at = pl.ds(pl.multiple_of((half * 16 + owner) * rows, 8), rows)
                    pieces.append(ref[at, pl.ds(128 * path, 128)])
            value = jnp.concatenate(pieces, 0).astype(bf16)
            target, at = (keep, place) if place < 8 else (send, place - 8)
            target[path, at, pl.ds(start, value.shape[0]), :] = value


def chunk_shapes(chunk):
    return [jax.ShapeDtypeStruct((3, 8, CHUNK_ROWS[chunk], 128), bf16)] * 2


def layer_one_back(args, net, gains, inverse_count, me):
    count = args[6].shape[0]
    packed = net["fast"]
    weights = (net["arrays"][0], *net["natural"][1:]) if packed else net["arrays"]
    rows = count * ROWS
    slopes = [(D, 3 * D), (D, D), (D, FF), (FF, D), (PROTOS, D)]
    out_shape = [
        jax.ShapeDtypeStruct((rows, D), f32),
        jax.ShapeDtypeStruct((8, D), f32),
        jax.ShapeDtypeStruct((8, 128), f32),
    ]
    scratch = [pltpu.VMEM((rows, 2 * D), bf16), pltpu.VMEM((CR, D), f32)]
    if packed:
        out_shape += chunk_shapes(0)
        scratch += [pltpu.VMEM(shape, f32) for shape in ((D, FF), (FF, D))]
    else:
        out_shape += [jax.ShapeDtypeStruct(shape, f32) for shape in slopes]
    scalar = [pl.BlockSpec(memory_space=pltpu.SMEM)] if packed else []
    return pl.pallas_call(
        lambda *refs: class_back_kernel(packed, count, inverse_count, *refs),
        in_specs=[whole()] * 12 + scalar + [whole()] * (1 + len(weights)),
        out_specs=[whole()] * len(out_shape),
        out_shape=out_shape,
        scratch_shapes=scratch,
        compiler_params=pltpu.CompilerParams(vmem_limit_bytes=megabytes(LIMITS[2])),
        cost_estimate=cost(13),
        name="layer_one_back",
    )(*args, *([me] if packed else []), gains, *weights)


def mlp_back_kernel(packed, *refs):
    delta, mid, gains, ups, downs = refs[:5]
    w1 = layer_views((ups,), True, 0)[2] if packed else ups.at[pl.ds(0, D)]
    w2 = downs.at[pl.ds(0, FF)]
    if packed:
        me, d_mid, s_gain, keep, send, s_up, s_down = refs[5:]
    else:
        d_mid, s_gain, s_up, s_down = refs[5:]
    d = delta[...]
    d_low = d.astype(bf16)
    hat, inv = normalize(mid[...])
    normed = (hat * gains[1:2, :]).astype(bf16)
    d_normed = None
    for j in range(FF // WIDE):
        cols = pl.ds(WIDE * j, WIDE)
        act, slope = gelu_parts(dot(normed, w1[:, cols]), True)
        s_down[cols, :] = dot_at(act.astype(bf16), d_low)
        d_exp = (dot_bt(d_low, w2[cols, :]) * slope).astype(bf16)
        s_up[:, cols] = dot_at(normed, d_exp)
        part = dot_bt(d_exp, w1[:, cols])
        d_normed = part if d_normed is None else d_normed + part
    back, gain = norm_back(hat, inv, gains[1:2, :], d_normed)
    s_gain[...] = jnp.zeros((8, D), f32)
    s_gain[0:1, :] = gain
    d_mid[...] = d + back
    if packed:
        pack_blocks(me[0], keep, send, [(s_up, 24), (s_down, 96)], [])


def backward_shapes(packed, slopes, chunk):
    if packed:
        return chunk_shapes(chunk), [pltpu.VMEM(shape, f32) for shape in slopes]
    return [jax.ShapeDtypeStruct(shape, f32) for shape in slopes], []


def layer_zero_mlp_back(delta, mid, net, gains, me):
    packed = net["fast"]
    weights = (net["arrays"][0], net["natural"][0]) if packed else net["arrays"][2:4]
    slopes, scratch = backward_shapes(packed, [(D, FF), (FF, D)], 1)
    scalar = [pl.BlockSpec(memory_space=pltpu.SMEM)] if packed else []
    return pl.pallas_call(
        lambda *refs: mlp_back_kernel(packed, *refs),
        in_specs=[whole()] * 5 + scalar,
        out_specs=[whole()] * (2 + len(slopes)),
        out_shape=[jax.ShapeDtypeStruct(delta.shape, f32), jax.ShapeDtypeStruct((8, D), f32)] + slopes,
        scratch_shapes=scratch,
        compiler_params=pltpu.CompilerParams(vmem_limit_bytes=megabytes(LIMITS[3])),
        cost_estimate=cost(12),
        name="layer_zero_mlp_back",
    )(delta, mid, gains, *weights, *([me] if packed else []))


def attention_back_kernel(count, d_mid, mix, share, att, wo, s_out, dmix, d_att):
    d_low = d_mid[...].astype(bf16)
    s_out[...] = dot_at(att[...], d_low)
    d_att[...] = dot_bt(d_low, wo[...]).astype(bf16)
    masks = half_masks()
    for g in range(count):
        rows = pl.ds(g * ROWS, ROWS)
        for pair in range(HEADS // 2):
            lanes = [pl.ds(D * part + 128 * pair, 128) for part in range(3)]
            query = mix[rows, lanes[0]] * jnp.asarray(SCALE, bf16)
            keys = mix[rows, lanes[1]] * jnp.asarray(SCALE, bf16)
            values = mix[rows, lanes[2]]
            upstream = d_att[rows, lanes[0]]
            dq = dk = dv = None
            for half in range(2):
                p = share[g, 2 * pair + half]
                up = upstream * masks[half]
                d_p = dot_bt(values, up)
                p_wide = p.astype(f32)
                weighted = p_wide * d_p
                d_s = (weighted - p_wide * jnp.sum(weighted, 0, keepdims=True)).astype(bf16)
                parts = (
                    dot_at(d_s, keys * masks[half]),
                    dot(d_s, query * masks[half]),
                    dot(p, up),
                )
                dq, dk, dv = parts if dq is None else (dq + parts[0], dk + parts[1], dv + parts[2])
            dmix[rows, lanes[0]] = dq.astype(bf16)
            dmix[rows, lanes[1]] = dk.astype(bf16)
            dmix[rows, lanes[2]] = dv.astype(bf16)


def layer_zero_attention_back(d_mid, mix, share, att, net):
    packed = net["packed"]
    count, rows = share.shape[0], d_mid.shape[0]

    def kernel(d_mid, mix, share, att, weight, *outs):
        wo = layer_views((weight,), True, 0)[1] if packed else weight.at[pl.ds(0, D)]
        attention_back_kernel(count, d_mid, mix, share, att, wo, *outs)

    return pl.pallas_call(
        kernel,
        in_specs=[whole()] * 5,
        out_specs=[whole()] * 2,
        out_shape=[jax.ShapeDtypeStruct((D, D), f32), jax.ShapeDtypeStruct((rows, 3 * D), bf16)],
        scratch_shapes=[pltpu.VMEM((rows, D), bf16)],
        compiler_params=pltpu.CompilerParams(vmem_limit_bytes=megabytes(LIMITS[4])),
        cost_estimate=cost(10),
        name="layer_zero_attention_back",
    )(d_mid, mix, share, att, net["arrays"][0 if packed else 1])


def input_back_kernel(packed, *refs):
    (d_mid, state, dmix, pats, s_out, mixes, gains, gain_two, gain_one) = refs[:9]
    if packed:
        me, keep, send, s_in, s_patch, s_vector = refs[9:]
        win = layer_views((mixes,), True, 0)[0]
    else:
        s_in, s_patch, s_vector = refs[9:]
        win = mixes.at[pl.ds(0, D)]
    hat, inv = normalize(state[...])
    normed = (hat * gains[0:1, :]).astype(bf16)
    s_in[...] = dot_at(normed, dmix[...])
    back, gain = norm_back(hat, inv, gains[0:1, :], dot_bt(dmix[...], win[...]))
    d_state = d_mid[...] + back
    table = patch = None
    groups, per = pats.shape[:2]
    for g in range(groups * per):
        one = d_state[g * ROWS : (g + 1) * ROWS]
        part = dot_at(pats[g // per, g % per], one[:PATCHES].astype(bf16))
        table = one if table is None else table + one
        patch = part if patch is None else patch + part
    s_patch[...] = patch
    s_vector[0:ROWS, :] = table
    s_vector[ROWS:, :] = jnp.zeros((VECTORS - ROWS, D), f32)
    s_vector[ROWS : ROWS + 1, :] = gain
    s_vector[ROWS + 1 : ROWS + 2, :] = gain_two[0:1, :]
    s_vector[ROWS + 2 : ROWS + 5, :] = gain_one[0:3, :]
    if packed:
        pack_blocks(me[0], keep, send, [(s_in, 24), (s_out, 24)], [(s_patch, 24), (s_vector, 8)])


def layer_zero_input_back(d_mid, state, dmix, patches, s_out, net, gains, gain_two, gain_one, me):
    packed = net["fast"]
    slopes, scratch = backward_shapes(packed, [(D, 3 * D), (PATCH_DIM, D), (VECTORS, D)], 2)
    scalar = [pl.BlockSpec(memory_space=pltpu.SMEM)] if packed else []
    return pl.pallas_call(
        lambda *refs: input_back_kernel(packed, *refs),
        in_specs=[whole()] * 9 + scalar,
        out_specs=[whole()] * len(slopes),
        out_shape=slopes,
        scratch_shapes=scratch,
        compiler_params=pltpu.CompilerParams(vmem_limit_bytes=megabytes(LIMITS[6])),
        cost_estimate=cost(6),
        name="layer_zero_input_back",
    )(d_mid, state, dmix, patches, s_out, net["arrays"][0], gains, gain_two, gain_one, *([me] if packed else []))


VECTORS = 256


NAMES = ("mix", "out", "up", "down", "patch", "protos")
WIDTHS = {"up": FF, "down": FF, "patch": D, "mix": 3 * D, "out": D, "protos": D, "rest": 128}
PLACE = {}
COLUMNS = 0
for _key in WIDTHS:
    PLACE[_key] = COLUMNS
    COLUMNS += WIDTHS[_key]


def pack_pieces(values):
    pieces = {name: values[name] for name in ("mix", "out", "up", "patch")}
    r = values["patch"].shape[0]
    down, protos = values["down"], values["protos"]
    pieces["down"] = jnp.concatenate([down[r * j : r * (j + 1)] for j in range(4)], 1)
    pieces["protos"] = protos[:r]
    pieces["rest"] = jnp.concatenate([protos[r:, 128 * j : 128 * (j + 1)] for j in range(3)], 0)
    return pieces


def pack_kernel(*refs):
    for net in range(2):
        out = refs[12 + net]
        values = {name: ref[...].astype(f32) for name, ref in zip(NAMES, refs[6 * net : 6 * net + 6])}
        for name, piece in pack_pieces(values).items():
            out[:, pl.ds(PLACE[name], WIDTHS[name])] = piece.astype(bf16)


THIRDS = ((0, 1792), (1792, 3584), (3584, 5504))


def chain_gather(mine):
    got = swap(mine, 4)
    arrays = [jnp.stack([mine[:, a:b], got[:, a:b]]) for a, b in THIRDS]
    for stage in (1, 2, 3):
        got = [swap(arrays[path], BITS[PATHS[path][stage]]) for path in range(3)]
        arrays = [jnp.concatenate([a, g], 0) for a, g in zip(arrays, got)]
    return arrays, [swap(a, 0) for a in arrays]


CHIPS_A_STEP = 4


def unpack_kernel(me, *refs):
    ins, outs = refs[: 6 * CHIPS_A_STEP], dict(zip(NAMES, refs[6 * CHIPS_A_STEP :]))
    first_core = (me[0] & 1) == 0
    pieces = {name: [] for name in NAMES}
    for chip in range(CHIPS_A_STEP):
        mine, got = ins[6 * chip : 6 * chip + 3], ins[6 * chip + 3 : 6 * chip + 6]
        own = jnp.concatenate([ref[0].astype(f32) for ref in mine], 1)
        other = jnp.concatenate([ref[0].astype(f32) for ref in got], 1)
        for rows in (jnp.where(first_core, own, other), jnp.where(first_core, other, own)):
            for name in ("mix", "out", "up", "patch"):
                pieces[name].append(rows[:, PLACE[name] : PLACE[name] + WIDTHS[name]])
            for j in range(4):
                pieces["down"].append(rows[:, PLACE["down"] + D * j : PLACE["down"] + D * (j + 1)])
            rest = rows[:, PLACE["rest"] :]
            pieces["protos"].append(rows[:, PLACE["protos"] : PLACE["protos"] + D])
            pieces["protos"].append(jnp.concatenate([rest[8 * j : 8 * (j + 1)] for j in range(3)], 1))
    for name in NAMES:
        outs[name][...] = jnp.concatenate(pieces[name], 0).astype(bf16)


def unpack_weights(arrays, got, me):
    def index(chip, path):
        def at(i, me_ref):
            other = (CHIPS_A_STEP * i + chip) ^ (me_ref[0] >> 1)
            place = (other >> 3) & 1
            for k in range(3):
                place = place + (((other >> (BITS[PATHS[path][k + 1]] - 1)) & 1) << (k + 1))
            return place, 0, 0

        return at

    in_specs, operands = [], []
    for chip in range(CHIPS_A_STEP):
        for source in (arrays, got):
            for path in range(3):
                in_specs.append(pl.BlockSpec((1,) + source[path].shape[1:], index(chip, path)))
                operands.append(source[path])
    shapes = ((2 * D, 3 * D), (2 * D, D), (2 * D, FF), (2 * FF, D), (PATCH_DIM, D), (PROTOS, D))
    steps = 16 // CHIPS_A_STEP
    return pl.pallas_call(
        unpack_kernel,
        grid_spec=pltpu.PrefetchScalarGridSpec(
            num_scalar_prefetch=1,
            grid=(steps,),
            in_specs=in_specs,
            out_specs=[pl.BlockSpec((a // steps, b), lambda i, me_ref: (i, 0)) for a, b in shapes],
        ),
        out_shape=[jax.ShapeDtypeStruct(shape, bf16) for shape in shapes],
        compiler_params=pltpu.CompilerParams(dimension_semantics=("arbitrary",), vmem_limit_bytes=megabytes(LIMITS[5])),
        cost_estimate=cost(9),
        name="unpack_weights",
    )(me, *operands)


def natural_net(mix, out, up, down, patch, protos, fast):
    return {"packed": False, "fast": fast, "arrays": (mix, out, up, down, patch, protos)}


def gathered_net(full):
    return {"packed": True, "fast": True, "arrays": (full,)}


def plain_net(full, n):
    r = full.shape[0] // n
    part = lambda name: full[:, PLACE[name] : PLACE[name] + WIDTHS[name]]
    down = part("down").reshape(n, r, 4, D).transpose(0, 2, 1, 3).reshape(2 * FF, D)
    rest = part("rest").reshape(n, 3, r // 3, 128).transpose(0, 2, 1, 3).reshape(n, r // 3, D)
    protos = jnp.concatenate([part("protos").reshape(n, r, D), rest], 1).reshape(PROTOS, D)
    return natural_net(part("mix"), part("out"), part("up"), down, part("patch"), protos, False)


def gather_networks(student, teacher, me, n):
    gather = lambda rows: lax.all_gather(rows, "dp", axis=0, tiled=True)
    r = student[0].shape[0]
    if n != 32:
        nets = []
        for shards in (student, teacher):
            pieces = pack_pieces(dict(zip(NAMES, shards)))
            nets.append(plain_net(gather(jnp.concatenate([pieces[name].astype(bf16) for name in WIDTHS], 1)), n))
        return nets
    student_rows, teacher_rows = pl.pallas_call(
        pack_kernel,
        in_specs=[whole()] * 12,
        out_specs=[whole()] * 2,
        out_shape=[jax.ShapeDtypeStruct((r, COLUMNS), bf16)] * 2,
        cost_estimate=cost(2),
        name="pack_weights",
    )(*student, *teacher)
    full = gather(student_rows)
    arrays, got = chain_gather(teacher_rows)
    return gathered_net(full), natural_net(*unpack_weights(arrays, got, me), True)


def swap(value, bit):
    size = lax.axis_size("dp")
    return lax.ppermute(value, "dp", [(i, i ^ (1 << bit)) for i in range(size)])


def after(value, other):
    value, other = lax.optimization_barrier((value, other))
    return value, other


def core_stage(keep, send, other=None):
    got = swap(send, 0)
    if other is not None:
        keep, other = after(keep, other)
    total = (keep.astype(f32) + got.astype(f32)).astype(bf16)
    return total if other is None else (total, other)


def halves(total):
    return [(total[path, :4], total[path, 4:]) for path in range(3)]


def axis_stage(stage, arrays, other=None):
    got = [swap(arrays[path][1], BITS[PATHS[path][stage]]) for path in range(3)]
    kept = [keep for keep, _ in arrays]
    if other is not None:
        kept, other = after(kept, other)
    total = [kept[path].astype(f32) + got[path].astype(f32) for path in range(3)]
    if stage == 3:
        return jnp.concatenate(total, 0)
    half = total[0].shape[0] // 2
    total = [t.astype(bf16) for t in total]
    arrays = [(t[:half], t[half:]) for t in total]
    return arrays if other is None else (arrays, other)


def last_stage(one, zero, me):
    upper = (me[0] >> 4) == 1
    keep = jnp.concatenate([jnp.where(upper, one[:, :288], zero[:, :288]), one[:, 288:320], zero[:, 288:320]], 1)
    send = jnp.concatenate([jnp.where(upper, zero[:, :288], one[:, :288]), one[:, 320:], zero[:, 320:]], 1)
    return keep, swap(send.astype(bf16), 4)


def square_sum(value):
    return jnp.sum(jnp.sum(value * value, -1, keepdims=True), 0, keepdims=True)


def three_parts(value):
    high = value.astype(bf16).astype(f32)
    middle = (value - high).astype(bf16).astype(f32)
    return high, middle, value - high - middle


def collect_kernel(*refs):
    (keep, got, report) = refs[:3]
    (mix, out, up, down, patch, protos, line) = refs[3:]
    vectors = []
    for path in range(3):
        a = keep[path] + got[path].astype(f32)
        lanes = pl.ds(128 * path, 128)
        for j in range(3):
            mix[:, pl.ds(D * j + 128 * path, 128)] = a[24 * j : 24 * (j + 1)]
        out[:, lanes] = a[72:96]
        for j in range(4):
            up[:, pl.ds(D * j + 128 * path, 128)] = a[96 + 24 * j : 120 + 24 * j]
        down[:, lanes] = a[192:288]
        protos[:, lanes] = a[288:320]
        patch[:, lanes] = a[320:344]
        vectors.append(a[344:352])
    write_line(line, (mix, out, up, down, patch, protos), jnp.concatenate(vectors, 1), report)


def write_line(line, slopes, vectors, report):
    squares = square_sum(vectors)
    for ref in slopes:
        squares = squares + square_sum(ref[...])
    cross = report[0:1, 0:1]
    rows = vectors.shape[0]
    lane = lax.broadcasted_iota(jnp.int32, (rows, 128), 1)
    row = lax.broadcasted_iota(jnp.int32, (rows, 128), 0)
    tail = jnp.zeros((rows, 128), f32)
    for i, part in enumerate(three_parts(squares) + three_parts(cross)):
        tail = jnp.where(jnp.logical_and(lane == i, row == 0), part, tail)
    full = jnp.concatenate([vectors, tail], 1).astype(bf16)
    for d in range(line.shape[0]):
        line[d] = full


RATES = (matrix_rate,) * 5 + (table_rate,) * 2


def update_kernel(rows, *refs):
    (fixes, report, arrived), refs = refs[:3], refs[3:]
    slopes, masters, firsts, seconds = refs[:6], refs[6:13], refs[13:20], refs[20:27]
    news, moments, squares, scalars, vector = refs[27:34], refs[34:41], refs[41:48], refs[48:50], refs[50]
    tail = jnp.zeros((1, 128), f32)
    for d in range(arrived.shape[0]):
        tail = tail + arrived[d, 0:1, pl.ds(D, 128)].astype(f32)
    lane = lax.broadcasted_iota(jnp.int32, (1, 128), 1)
    norm = jnp.sqrt(jnp.sum(jnp.where(lane < 3, tail, 0.0), -1, keepdims=True))
    cross = jnp.sum(jnp.where(jnp.logical_and(lane >= 3, lane < 6), tail, 0.0), -1, keepdims=True)
    loss = cross + report[0:1, 1:2]
    scalars[0][...] = loss
    scalars[1][...] = norm
    factor = jnp.minimum(1.0, clip_limit / (norm + 1e-06))
    per_device = arrived.shape[1]
    table = jnp.concatenate([arrived[d, :, pl.ds(0, D)].astype(f32) for d in range(arrived.shape[0])], 0)
    vector[0:1, :] = table[CLS : CLS + 1]
    vector[1:SEQ, :] = table[:PATCHES]
    vector[SEQ:VROWS, :] = table[ROWS : ROWS + 5]
    scale_one, scale_two = 1.0 / fixes[0], 1.0 / fixes[1]
    order = (0, 1, 2, 3, 4, None, 5)
    for i in range(7):
        slope = vector if order[i] is None else slopes[order[i]]
        clipped = slope[...] * factor
        moment = beta_one * firsts[i][...] + (1.0 - beta_one) * clipped
        square = beta_two * seconds[i][...] + (1.0 - beta_two) * clipped * clipped
        stepped = (moment * scale_one) / (jnp.sqrt(square * scale_two) + adam_floor)
        weight = masters[i][...]
        news[i][...] = weight - RATES[i] * (stepped + decay_rate * weight)
        moments[i][...] = moment
        squares[i][...] = square


def update_rows(slopes, arrived, report, masters, firsts, seconds, fixes):
    shapes = [jax.ShapeDtypeStruct(w.shape, f32) for w in masters]
    out_shape = shapes * 3 + [jax.ShapeDtypeStruct((1, 1), f32)] * 2
    return pl.pallas_call(
        lambda *refs: update_kernel(None, *refs),
        in_specs=[pl.BlockSpec(memory_space=pltpu.SMEM)] + [whole()] * 29,
        out_specs=[whole()] * len(out_shape),
        out_shape=out_shape,
        scratch_shapes=[pltpu.VMEM((VROWS, D), f32)],
        compiler_params=pltpu.CompilerParams(vmem_limit_bytes=megabytes(LIMITS[5])),
        cost_estimate=cost(4),
        name="update_rows",
    )(fixes, report, arrived, *slopes, *masters, *firsts, *seconds)


def update_plain(slopes, arrived, report, masters, firsts, seconds, fixes):
    tail = jnp.sum(arrived[:, 0, D:].astype(f32), 0)
    table = arrived[:, :, :D].astype(f32).reshape(-1, D)
    vector = jnp.concatenate([table[CLS : CLS + 1], table[:PATCHES], table[ROWS : ROWS + 5]], 0)
    norm = jnp.sqrt(tail[0] + tail[1] + tail[2])
    loss = tail[3] + tail[4] + tail[5] + report[0, 1]
    factor = jnp.minimum(1.0, clip_limit / (norm + 1e-06))
    slopes = list(slopes[:5]) + [vector, slopes[5]]
    news, moments, squares = ([], [], [])
    for weight, first, second, slope, rate in zip(masters, firsts, seconds, slopes, RATES):
        clipped = slope * factor
        moment = beta_one * first + (1.0 - beta_one) * clipped
        square = beta_two * second + (1.0 - beta_two) * clipped * clipped
        stepped = moment / fixes[0] / (jnp.sqrt(square / fixes[1]) + adam_floor)
        news.append(weight - rate * (stepped + decay_rate * weight))
        moments.append(moment)
        squares.append(square)
    return (*news, *moments, *squares, loss[None, None], norm[None, None])


def collect(keep, got, report, n, r):
    shapes = [(r, 3 * D), (r, D), (r, FF), (4 * r, D), (r, D), (4 * r // 3, D)]
    out_shape = [jax.ShapeDtypeStruct(shape, f32) for shape in shapes] + [jax.ShapeDtypeStruct((n, VECTORS // n, 512), bf16)]
    *slopes, line = pl.pallas_call(
        collect_kernel,
        in_specs=[whole()] * 3,
        out_specs=[whole()] * len(out_shape),
        out_shape=out_shape,
        compiler_params=pltpu.CompilerParams(vmem_limit_bytes=megabytes(LIMITS[5])),
        cost_estimate=cost(3),
        name="collect_gradients",
    )(keep, got, report)
    return slopes, line


def collect_plain(one, mlp, rest, report, n):
    mix1, out1, up1, down1, protos = one
    up0, down0 = mlp
    mix0, out0, patch, vectors = rest
    scatter = lambda *v: lax.psum_scatter(jnp.concatenate(v, 0), "dp", scatter_dimension=0, tiled=True)
    slopes = [scatter(mix0, mix1), scatter(out0, out1), scatter(up0, up1), scatter(down0, down1), scatter(patch), scatter(protos)]
    vectors = scatter(vectors)
    squares = sum(jnp.sum(s * s) for s in slopes) + jnp.sum(vectors * vectors)
    tail = jnp.stack(three_parts(squares) + three_parts(report[0, 0]))
    tail = jnp.zeros((vectors.shape[0], 128), f32).at[0, :6].set(tail)
    line = jnp.concatenate([vectors, tail], 1).astype(bf16)
    return slopes, jnp.broadcast_to(line[None], (n,) + line.shape)


def local(
    attention_in, attention_out, hidden_in, hidden_out, patch_weight, vector_rows, prototypes,
    first_attention_in, first_attention_out, first_hidden_in, first_hidden_out, first_patch_weight, first_vector_rows, first_prototypes,
    second_attention_in, second_attention_out, second_hidden_in, second_hidden_out, second_patch_weight, second_vector_rows, second_prototypes,
    teacher_attention_in, teacher_attention_out, teacher_hidden_in, teacher_hidden_out, teacher_patch_weight, teacher_vector_rows, teacher_prototypes,
    anchor_patches, target_patches, patch_keep, step_count,
):
    n = lax.axis_size("dp")
    me = lax.axis_index("dp").astype(jnp.int32)[None]
    groups, per = anchor_patches.shape[:2]
    count = groups * per
    inverse_count = 1.0 / (count * n)
    masters = (attention_in, attention_out, hidden_in, hidden_out, patch_weight, vector_rows, prototypes)
    firsts = (first_attention_in, first_attention_out, first_hidden_in, first_hidden_out, first_patch_weight, first_vector_rows, first_prototypes)
    seconds = (second_attention_in, second_attention_out, second_hidden_in, second_hidden_out, second_patch_weight, second_vector_rows, second_prototypes)
    student, teacher = gather_networks(
        (attention_in, attention_out, hidden_in, hidden_out, patch_weight, prototypes),
        (teacher_attention_in, teacher_attention_out, teacher_hidden_in, teacher_hidden_out, teacher_patch_weight, teacher_prototypes),
        me,
        n,
    )

    def table_of(rows):
        return jnp.concatenate([rows[1:SEQ], rows[0:1], jnp.zeros((ROWS - SEQ, D), f32)], 0)

    def gains_of(rows):
        zeros = jnp.zeros((5, D), f32)
        first = jnp.concatenate([rows[SEQ : SEQ + 2], jnp.zeros((6, D), f32)], 0)
        second = jnp.concatenate([rows[SEQ + 2 : SEQ + 5], zeros], 0)
        return first, second

    keep = patch_keep.reshape(count, PATCHES)
    bias = jnp.where(keep == 1, 0.0, -1000000000.0).astype(f32)
    ends = jnp.where(jnp.arange(ROWS - PATCHES) == 0, 0.0, -1000000000.0).astype(f32)
    ends = jnp.broadcast_to(ends, (count, ROWS - PATCHES))
    bias = jnp.concatenate([bias, ends], 1)[:, None]
    plain = jnp.concatenate([jnp.zeros((count, PATCHES), f32), ends], 1)[:, None]
    gains0, gains1 = gains_of(vector_rows)
    teacher_rows = teacher_vector_rows.astype(f32)
    teacher_gains0, teacher_gains1 = gains_of(teacher_rows)
    counter = step_count.astype(f32)
    fixes = jnp.stack([1.0 - beta_one**counter, 1.0 - beta_two**counter])

    (targets,) = forward(target_patches, table_of(teacher_rows), plain, teacher, teacher_gains0, teacher_gains1, False, n)
    if student["fast"]:
        targets, bias = lax.optimization_barrier((targets, bias))
    state1, state0, mix, share, att, mid, logs, sums, kv, queries, shares, att_c, mid_c, expanded, last, cls, *natural = forward(
        anchor_patches, table_of(vector_rows), bias, student, gains0, gains1, True, n)
    student["natural"] = natural
    mean_sum = lax.all_to_all(sums, "dp", 0, 0, tiled=True)
    delta, gain_one, report, *one = layer_one_back(
        (logs, targets, mean_sum, state1, kv, queries, shares, att_c, mid_c, expanded, last, cls), student, gains1, inverse_count, me)
    d_mid, gain_two, *mlp = layer_zero_mlp_back(delta, mid, student, gains0, me)
    if student["fast"]:
        one, d_mid = core_stage(*one, d_mid)
    out0, dmix = layer_zero_attention_back(d_mid, mix, share, att, student)
    if student["fast"]:
        one, dmix = axis_stage(1, halves(one), dmix)
        mlp, dmix = core_stage(*mlp, dmix)
    rest = layer_zero_input_back(d_mid, state0, dmix, anchor_patches, out0, student, gains0, gain_two, gain_one, me)
    if student["fast"]:
        one, rest = axis_stage(2, one, rest)
        mlp, rest = axis_stage(1, halves(mlp), rest)
        rest = axis_stage(1, halves(core_stage(*rest)))
        zero = [tuple(jnp.concatenate([c[:, :96], b, c[:, 96:]], 1) for b, c in zip(bs, cs)) for bs, cs in zip(mlp, rest)]
        zero, one = lax.optimization_barrier((zero, one))
        keep, got = last_stage(axis_stage(3, one), axis_stage(3, axis_stage(2, zero)), me)
        slopes, line = collect(keep, got, report, n, attention_in.shape[0])
        update = update_rows
    else:
        mix0, patch0, vectors = rest
        slopes, line = collect_plain(one, mlp, (mix0, out0, patch0, vectors), report, n)
        update = update_plain
    arrived = lax.all_to_all(line, "dp", 0, 0, tiled=True)
    *states, loss, norm = update(slopes, arrived, report, masters, firsts, seconds, fixes)
    return (loss[0, 0], norm[0, 0], *states)


def solution(mesh):
    rows, same, images = P("dp", None), P(), P(None, "dp", None, None)
    weights = (rows,) * 5 + (same, rows)
    return jax.shard_map(
        local,
        mesh=mesh,
        in_specs=weights * 4 + (images, images, P(None, "dp", None), same),
        out_specs=(same, same) + weights * 3,
        check_vma=False,
    )
```

```python
import jax
import jax.numpy as jnp
from jax import lax
from jax.experimental import pallas as pl
from jax.experimental.pallas import tpu as pltpu
from jax.sharding import PartitionSpec as P

D = 384
HEADS = 6
HEAD_DIM = 64
FF = 1536
PATCHES = 196
PATCH_DIM = 768
PROTOS = 1024
SEQ = 197
VROWS = 202
ROWS = 208
CLS = 196
WIDE = 512
CR = 16
SCALE = HEAD_DIM ** (-0.5)

student_softness = 0.04
teacher_sharpness = 0.02
clip_limit = 0.01
matrix_rate = 0.05
table_rate = 0.4
decay_rate = 0.05
beta_one = 0.9
beta_two = 0.999
adam_floor = 1e-08

f32 = jnp.float32
bf16 = jnp.bfloat16
GELU_C = 0.7978845608028654
GELU_A = 0.044715


def dot(a, b):
    return lax.dot_general(a, b, (((1,), (0,)), ((), ())), preferred_element_type=f32)


def dot_bt(a, b):
    return lax.dot_general(a, b, (((1,), (1,)), ((), ())), preferred_element_type=f32)


def dot_at(a, b):
    return lax.dot_general(a, b, (((0,), (0,)), ((), ())), preferred_element_type=f32)


def normalize(x):
    centre = x - jnp.sum(x, -1, keepdims=True) * (1.0 / D)
    spread = jnp.sum(centre * centre, -1, keepdims=True) * (1.0 / D)
    inverse = lax.rsqrt(spread + 1e-06)
    return centre * inverse, inverse


def norm_back(hat, inverse, gain, upstream):
    gain_slope = jnp.sum(upstream * hat, 0, keepdims=True)
    scaled = upstream * gain
    mean_one = jnp.sum(scaled, -1, keepdims=True) * (1.0 / D)
    mean_two = jnp.sum(scaled * hat, -1, keepdims=True) * (1.0 / D)
    return inverse * (scaled - mean_one - hat * mean_two), gain_slope


def gelu_parts(x, slope):
    square = x * x
    t = jnp.tanh(x * (GELU_C + (GELU_C * GELU_A) * square))
    half = 0.5 + 0.5 * t
    act = x * half
    if not slope:
        return act, None
    inner = GELU_C + (3.0 * GELU_C * GELU_A) * square
    return act, half + act * (1.0 - t) * inner


def half_masks():
    lane = lax.broadcasted_iota(jnp.int32, (1, 128), 1)
    first = jnp.where(lane < HEAD_DIM, 1.0, 0.0)
    return first.astype(bf16), (1.0 - first).astype(bf16)


def spot_masks():
    lane = lax.broadcasted_iota(jnp.int32, (1, 128), 1)
    return jnp.where(lane == HEAD_DIM, 1.0, 0.0).astype(bf16), jnp.where(lane == 0, 1.0, 0.0).astype(bf16)


def head_mask():
    row = lax.broadcasted_iota(jnp.int32, (CR, D), 0)
    lane = lax.broadcasted_iota(jnp.int32, (CR, D), 1)
    low = row * HEAD_DIM
    return jnp.where(jnp.logical_and(lane >= low, lane < low + HEAD_DIM), 1.0, 0.0)


def natural_down(ref, natural):
    for pair in range(8):
        rows = ref[pl.ds(48 * pair, 48), :].astype(f32)
        pieces = [rows[24 * b : 24 * (b + 1), D * j : D * (j + 1)] for b in range(2) for j in range(4)]
        natural[pl.ds(192 * pair, 192), :] = jnp.concatenate(pieces, 0).astype(bf16)


def natural_protos(ref, rest, natural):
    for pair in range(16):
        rows = ref[pl.ds(48 * pair, 48), :].astype(f32)
        tail = rest[pl.ds(48 * pair, 48), :].astype(f32)
        pieces = []
        for b in range(2):
            pieces.append(rows[24 * b : 24 * (b + 1)])
            pieces.append(jnp.concatenate([tail[24 * b + 8 * j : 24 * b + 8 * (j + 1)] for j in range(3)], 1))
        natural[pl.ds(64 * pair, 64), :] = jnp.concatenate(pieces, 0).astype(bf16)


def layer_views(weights, packed, layer):
    if packed:
        (full,) = weights
        at = lambda name: full.at[pl.ds(D * layer, D), pl.ds(PLACE[name], WIDTHS[name])]
        return tuple(at(name) for name in ("mix", "out", "up", "down"))
    mix, out, up, down = weights[:4]
    rows = pl.ds(D * layer, D)
    return mix.at[rows], out.at[rows], up.at[rows], down.at[pl.ds(FF * layer, FF)]


def forward_kernel(save, packed, count, *refs):
    (pats, tab, bias_all, key_bias_all, gains, gains_one), refs = refs[:6], refs[6:]
    weights, refs = refs[: 1 if packed else 6], refs[1 if packed else 6 :]
    group = count
    per = pats.shape[1]
    if save:
        out, first, mix, share, att, mid = refs[:6]
        class_refs, naturals = refs[6:16], refs[16:]
    else:
        share = mid = None
        (target, first, mix, att, kv, att_c, cls, out) = refs[:8]
        class_refs = (target, kv, att_c, cls)
    win, wo, w1, w2 = layer_views(weights, packed, 0)
    if packed:
        down, down_one, protos = naturals
        wp = weights[0].at[:, pl.ds(PLACE["patch"], D)]
        natural_down(w2, down)
    else:
        wp, down = weights[4], w2
    table = tab[...]
    for g in range(group):
        embedded = dot(pats[g // per, g % per], wp[...])
        first[pl.ds(g * ROWS, PATCHES), :] = embedded + table[:PATCHES]
        first[pl.ds(g * ROWS + PATCHES, ROWS - PATCHES), :] = table[PATCHES:]
    state = first[...]
    hat, _ = normalize(state)
    normed = (hat * gains[0:1, :]).astype(bf16)
    mix[...] = dot(normed, win[...]).astype(bf16)
    masks, spots = half_masks(), spot_masks()

    for g in range(group):
        rows = pl.ds(g * ROWS, ROWS)
        key_bias = key_bias_all[g]
        for pair in range(HEADS // 2):
            query = mix[rows, pl.ds(128 * pair, 128)] * jnp.asarray(SCALE, bf16)
            keys = mix[rows, pl.ds(D + 128 * pair, 128)]
            values = mix[rows, pl.ds(2 * D + 128 * pair, 128)]
            total = None
            for half in range(2):
                scores = dot_bt(keys * masks[half] + key_bias * spots[half], query * masks[half] + spots[half])
                e = jnp.exp(scores - jnp.max(scores, 0, keepdims=True))
                p = (e * (1.0 / jnp.sum(e, 0, keepdims=True))).astype(bf16)
                if save:
                    share[g, 2 * pair + half] = p
                o = dot_at(p, values * masks[half])
                total = o if total is None else total + o
            att[rows, pl.ds(128 * pair, 128)] = total.astype(bf16)
    middle = first[...] + dot(att[...], wo[...])
    if save:
        mid[...] = middle
    hat, _ = normalize(middle)
    normed = (hat * gains[1:2, :]).astype(bf16)
    result = middle
    for j in range(FF // WIDE):
        cols = pl.ds(WIDE * j, WIDE)
        a, _ = gelu_parts(dot(normed, w1[:, cols]), False)
        result = result + dot(a.astype(bf16), down[cols, :])
    out[...] = result
    win, wo, w1, w2 = layer_views(weights, packed, 1)
    if packed:
        natural_down(w2, down_one)
        natural_protos(weights[0].at[:, pl.ds(PLACE["protos"], D)], weights[0].at[:, pl.ds(PLACE["rest"], 128)], protos)
        late = (win, wo, w1, down_one, protos)
    else:
        late = (win, wo, w1, w2, weights[5])
    class_forward(save, count, out, bias_all, late, gains_one, class_refs)


def class_forward(student, count, state, bias, weights, gains, refs):
    win, wo, w1, w2, protos = weights
    if student:
        (logs, sums, kv, queries, shares, att, mid_c, expanded_out, last, cls) = refs
    else:
        (target, kv, att, cls) = refs
    hat, _ = normalize(state[...])
    normed = (hat * gains[0:1, :]).astype(bf16)
    kv[...] = dot(normed, win[:, D:]).astype(bf16)
    cls[...] = jnp.zeros((CR, D), f32)
    for g in range(count):
        cls[g : g + 1, :] = state[pl.ds(g * ROWS + CLS, 1), :]
    class_state = cls[...]
    hat, _ = normalize(class_state)
    query = dot((hat * gains[0:1, :]).astype(bf16), win[:, :D]).astype(bf16)
    if student:
        queries[...] = query
    mask = head_mask()
    for g in range(count):
        rows = pl.ds(g * ROWS, ROWS)
        spread = (jnp.broadcast_to(query[g : g + 1, :].astype(f32) * SCALE, (CR, D)) * mask).astype(bf16)
        scores = dot_bt(spread, kv[rows, pl.ds(0, D)]) + bias[g]
        e = jnp.exp(scores - jnp.max(scores, -1, keepdims=True))
        p = e * (1.0 / jnp.sum(e, -1, keepdims=True))
        if student:
            shares[g] = p
        o = dot(p.astype(bf16), kv[rows, pl.ds(D, D)])
        att[g : g + 1, :] = jnp.sum(o * mask, 0, keepdims=True)
    att[count:, :] = jnp.zeros((CR - count, D), f32)
    middle = class_state + dot(att[...].astype(bf16), wo[...])
    hat, _ = normalize(middle)
    expanded = dot((hat * gains[1:2, :]).astype(bf16), w1[...])
    act, _ = gelu_parts(expanded, False)
    result = middle + dot(act.astype(bf16), w2[...])
    if student:
        mid_c[...] = middle
        expanded_out[...] = expanded
        last[...] = result
    hat, _ = normalize(result)
    unit, _ = unit_parts(hat * gains[2:3, :])
    proto_unit, _ = unit_parts(protos[...].astype(f32))
    raw = dot_bt(unit.astype(bf16), proto_unit.astype(bf16))
    logits = raw * (1.0 / (student_softness if student else teacher_sharpness))
    logits = logits - jnp.max(logits, -1, keepdims=True)
    e = jnp.exp(logits)
    total = jnp.sum(e, -1, keepdims=True)
    if student:
        log_share = logits - jnp.log(total)
        logs[...] = log_share
        share = jnp.exp(log_share)
        row = lax.broadcasted_iota(jnp.int32, (CR, PROTOS), 0)
        per = count // 2
        lines = []
        for m in range(2):
            inside = jnp.logical_and(row >= m * per, row < (m + 1) * per)
            line = jnp.sum(jnp.where(inside, share, 0.0), 0, keepdims=True)
            lines += [line[:, 128 * k : 128 * (k + 1)] for k in range(PROTOS // 128)]
        lines = jnp.concatenate(lines, 0)
        for d in range(sums.shape[0]):
            sums[d] = lines.astype(bf16)
    else:
        target[...] = e / total


def forward(patches, table, bias, net, gains, gains_one, save, n):
    groups, group = patches.shape[:2]
    count = groups * group
    rows = count * ROWS
    packed = net["packed"]
    if save:
        out_shape = [
            jax.ShapeDtypeStruct((rows, D), f32),
            jax.ShapeDtypeStruct((rows, D), f32),
            jax.ShapeDtypeStruct((rows, 3 * D), bf16),
            jax.ShapeDtypeStruct((count, HEADS, ROWS, ROWS), bf16),
            jax.ShapeDtypeStruct((rows, D), bf16),
            jax.ShapeDtypeStruct((rows, D), f32),
            jax.ShapeDtypeStruct((CR, PROTOS), f32),
            jax.ShapeDtypeStruct((n, 16, 128), bf16),
            jax.ShapeDtypeStruct((rows, 2 * D), bf16),
            jax.ShapeDtypeStruct((CR, D), bf16),
            jax.ShapeDtypeStruct((count, CR, ROWS), f32),
            jax.ShapeDtypeStruct((CR, D), f32),
            jax.ShapeDtypeStruct((CR, D), f32),
            jax.ShapeDtypeStruct((CR, FF), f32),
            jax.ShapeDtypeStruct((CR, D), f32),
            jax.ShapeDtypeStruct((CR, D), f32),
        ]
        scratch = []
    else:
        out_shape = [jax.ShapeDtypeStruct((CR, PROTOS), f32)]
        scratch = [
            pltpu.VMEM((rows, D), f32),
            pltpu.VMEM((rows, 3 * D), bf16),
            pltpu.VMEM((rows, D), bf16),
            pltpu.VMEM((rows, 2 * D), bf16),
            pltpu.VMEM((CR, D), f32),
            pltpu.VMEM((CR, D), f32),
            pltpu.VMEM((rows, D), f32),
        ]
    if packed:
        out_shape += [jax.ShapeDtypeStruct(shape, bf16) for shape in ((FF, D), (FF, D), (PROTOS, D))]
    key_bias = jnp.broadcast_to(bias.reshape(count, ROWS, 1).astype(bf16), (count, ROWS, 128))
    operands = (patches, table, bias, key_bias, gains, gains_one, *net["arrays"])
    return pl.pallas_call(
        lambda *refs: forward_kernel(save, packed, count, *refs),
        in_specs=[whole()] * len(operands),
        out_specs=[whole()] * len(out_shape),
        out_shape=out_shape,
        scratch_shapes=scratch,
        compiler_params=pltpu.CompilerParams(vmem_limit_bytes=megabytes(LIMITS[0 if save else 1])),
        cost_estimate=cost(30),
        name="student_forward" if save else "teacher_forward",
    )(*operands)


LIMITS = [14, 18, 18, 18, 18, 10, 18]


def megabytes(count):
    return count * 1024 * 1024


def cost(micros):
    return pl.CostEstimate(flops=int(micros * 1e9), transcendentals=0, bytes_accessed=int(micros * 3e6))


def unit_parts(v):
    inverse = lax.rsqrt(jnp.sum(v * v, -1, keepdims=True) + 1e-06)
    return v * inverse, inverse


def whole():
    return pl.BlockSpec(memory_space=pltpu.VMEM)


def class_back_kernel(packed, count, inverse_count, *refs):
    (logs, target, mean_sum, state, kv, queries, shares, att, mid_c, expanded, last, cls) = refs[:12]
    if packed:
        (me, gains, full, w2, protos), refs = refs[12:17], refs[17:]
        (delta, s_gain, report, keep, send, dkv, dq_all, s_up, s_down) = refs
        s_proto, s_in, s_out = s_down.at[pl.ds(0, PROTOS)], s_up.at[:, pl.ds(0, 3 * D)], s_up.at[:, pl.ds(3 * D, D)]
        win, wo, w1, _ = layer_views((full,), True, 1)
    else:
        gains, weights = refs[12], refs[13:19]
        (delta, s_gain, report, s_in, s_out, s_up, s_down, s_proto, dkv, dq_all) = refs[19:]
        (win, wo, w1, w2), protos = layer_views(weights, False, 1), weights[5]
    mask = head_mask()
    row = lax.broadcasted_iota(jnp.int32, (CR, 1), 0)
    live = row < count
    log_share = logs[...]
    share = jnp.exp(log_share)
    targets = target[...]
    total = mean_sum[0].astype(f32)
    for device in range(1, mean_sum.shape[0]):
        total = total + mean_sum[device].astype(f32)
    lines = [jnp.concatenate([total[8 * m + k : 8 * m + k + 1] for k in range(PROTOS // 128)], 1) for m in range(2)]
    mean_share = jnp.concatenate(lines, 0) * (2.0 * inverse_count)
    log_mean = jnp.log(mean_share)
    cross = -jnp.sum(jnp.where(live, targets * log_share, 0.0), -1, keepdims=True)
    cross = jnp.sum(cross, 0, keepdims=True) * inverse_count
    entropy = jnp.sum(jnp.sum(mean_share * log_mean, -1, keepdims=True), 0, keepdims=True) * 0.5
    lane = lax.broadcasted_iota(jnp.int32, (8, 128), 1)
    report[...] = jnp.where(lane == 0, cross, jnp.where(lane == 1, entropy, 0.0))
    log_row = jnp.where(row < count // 2, log_mean[0:1, :], log_mean[1:2, :])
    slope = share - targets + share * (log_row - jnp.sum(share * log_row, -1, keepdims=True))
    slope = jnp.where(live, slope * (inverse_count / student_softness), 0.0).astype(bf16)
    hat_f, inv_f = normalize(last[...])
    summary = hat_f * gains[2:3, :]
    unit, inv_u = unit_parts(summary)
    proto = protos[...].astype(f32)
    proto_unit, inv_p = unit_parts(proto)
    d_unit = dot(slope, proto_unit.astype(bf16))
    d_proto = dot_at(slope, unit.astype(bf16))
    s_proto[...] = inv_p * (d_proto - proto_unit * jnp.sum(proto_unit * d_proto, -1, keepdims=True))
    if packed:
        pack_blocks(me[0], keep, send, [], [(s_proto, 32)], 288)
    d_summary = inv_u * (d_unit - unit * jnp.sum(unit * d_unit, -1, keepdims=True))
    d, gain_f = norm_back(hat_f, inv_f, gains[2:3, :], d_summary)
    s_gain[...] = jnp.zeros((8, D), f32)
    s_gain[2:3, :] = gain_f
    d_low = d.astype(bf16)
    act, gslope = gelu_parts(expanded[...], True)
    s_down[...] = dot_at(act.astype(bf16), d_low)
    d_exp = (dot_bt(d_low, w2[...]) * gslope).astype(bf16)
    if packed:
        pack_blocks(me[0], keep, send, [(s_down, 96)], [], 192)
    hat_m, inv_m = normalize(mid_c[...])
    s_up[...] = dot_at((hat_m * gains[1:2, :]).astype(bf16), d_exp)
    d_mid, gain_two = norm_back(hat_m, inv_m, gains[1:2, :], dot_bt(d_exp, w1[...]))
    s_gain[1:2, :] = gain_two
    if packed:
        pack_blocks(me[0], keep, send, [(s_up, 24)], [], 96)
    d_mid = d + d_mid
    d_mid_low = d_mid.astype(bf16)
    s_out[...] = dot_at(att[...].astype(bf16), d_mid_low)
    d_att = dot_bt(d_mid_low, wo[...]).astype(bf16)
    dq_all[...] = jnp.zeros((CR, D), f32)
    for g in range(count):
        rows = pl.ds(g * ROWS, ROWS)
        d_spread = (jnp.broadcast_to(d_att[g : g + 1, :].astype(f32), (CR, D)) * mask).astype(bf16)
        q_spread = (jnp.broadcast_to(queries[g : g + 1, :].astype(f32) * SCALE, (CR, D)) * mask).astype(bf16)
        p = shares[g]
        d_p = dot_bt(d_spread, kv[rows, pl.ds(D, D)])
        d_s = (p * (d_p - jnp.sum(p * d_p, -1, keepdims=True))).astype(bf16)
        dkv[rows, pl.ds(D, D)] = dot_at(p.astype(bf16), d_spread).astype(bf16)
        dkv[rows, pl.ds(0, D)] = dot_at(d_s, q_spread).astype(bf16)
        dq = dot(d_s, kv[rows, pl.ds(0, D)]) * mask
        dq_all[g : g + 1, :] = jnp.sum(dq, 0, keepdims=True) * SCALE
    dq_low = dq_all[...].astype(bf16)
    hat_c, _ = normalize(cls[...])
    s_in[:, :D] = dot_at((hat_c * gains[0:1, :]).astype(bf16), dq_low)
    hat, inv = normalize(state[...])
    s_in[:, D:] = dot_at((hat * gains[0:1, :]).astype(bf16), dkv[...])
    d_class = dot_bt(dq_low, win[:, :D])
    delta[...] = dot_bt(dkv[...], win[:, D:])
    for g in range(count):
        one = pl.ds(g * ROWS + CLS, 1)
        delta[one, :] = delta[one, :] + d_class[g : g + 1, :]
    d_state, gain_one = norm_back(hat, inv, gains[0:1, :], delta[...])
    s_gain[0:1, :] = gain_one
    delta[...] = d_state
    for g in range(count):
        one = pl.ds(g * ROWS + CLS, 1)
        delta[one, :] = delta[one, :] + d_mid[g : g + 1, :]
    if packed:
        pack_blocks(me[0], keep, send, [(s_up, 24)], [], 0)


BITS = {"c": 0, "x": 1, "y": 2, "z": 3}
PATHS = (("c", "x", "y", "z"), ("c", "y", "z", "x"), ("c", "z", "x", "y"))
LAYER_ROWS = 288
CHUNK_ROWS = (352, 192, 160)


def pack_blocks(me, keep, send, layered, wide, start=0):
    for path in range(3):
        for place in range(16):
            mask = 0
            for k in range(4):
                mask |= ((place >> (3 - k)) & 1) << BITS[PATHS[path][k]]
            owner = (me & 15) ^ mask
            pieces = []
            for ref, rows in layered:
                at = pl.ds(pl.multiple_of(owner * rows, 8), rows)
                for j in range(ref.shape[1] // D):
                    pieces.append(ref[at, pl.ds(D * j + 128 * path, 128)])
            for other in range(2):
                half = (me >> 4) ^ other
                for ref, rows in wide:
                    at = pl.ds(pl.multiple_of((half * 16 + owner) * rows, 8), rows)
                    pieces.append(ref[at, pl.ds(128 * path, 128)])
            value = jnp.concatenate(pieces, 0).astype(bf16)
            target, at = (keep, place) if place < 8 else (send, place - 8)
            target[path, at, pl.ds(start, value.shape[0]), :] = value


def chunk_shapes(chunk):
    return [jax.ShapeDtypeStruct((3, 8, CHUNK_ROWS[chunk], 128), bf16)] * 2


def layer_one_back(args, net, gains, inverse_count, me):
    count = args[6].shape[0]
    packed = net["fast"]
    weights = (net["arrays"][0], *net["natural"][1:]) if packed else net["arrays"]
    rows = count * ROWS
    slopes = [(D, 3 * D), (D, D), (D, FF), (FF, D), (PROTOS, D)]
    out_shape = [
        jax.ShapeDtypeStruct((rows, D), f32),
        jax.ShapeDtypeStruct((8, D), f32),
        jax.ShapeDtypeStruct((8, 128), f32),
    ]
    scratch = [pltpu.VMEM((rows, 2 * D), bf16), pltpu.VMEM((CR, D), f32)]
    if packed:
        out_shape += chunk_shapes(0)
        scratch += [pltpu.VMEM(shape, f32) for shape in ((D, FF), (FF, D))]
    else:
        out_shape += [jax.ShapeDtypeStruct(shape, f32) for shape in slopes]
    scalar = [pl.BlockSpec(memory_space=pltpu.SMEM)] if packed else []
    return pl.pallas_call(
        lambda *refs: class_back_kernel(packed, count, inverse_count, *refs),
        in_specs=[whole()] * 12 + scalar + [whole()] * (1 + len(weights)),
        out_specs=[whole()] * len(out_shape),
        out_shape=out_shape,
        scratch_shapes=scratch,
        compiler_params=pltpu.CompilerParams(vmem_limit_bytes=megabytes(LIMITS[2])),
        cost_estimate=cost(13),
        name="layer_one_back",
    )(*args, *([me] if packed else []), gains, *weights)


def mlp_back_kernel(packed, *refs):
    delta, mid, gains, ups, downs = refs[:5]
    w1 = layer_views((ups,), True, 0)[2] if packed else ups.at[pl.ds(0, D)]
    w2 = downs.at[pl.ds(0, FF)]
    if packed:
        me, d_mid, s_gain, keep, send, s_up, s_down = refs[5:]
    else:
        d_mid, s_gain, s_up, s_down = refs[5:]
    d = delta[...]
    d_low = d.astype(bf16)
    hat, inv = normalize(mid[...])
    normed = (hat * gains[1:2, :]).astype(bf16)
    d_normed = None
    for j in range(FF // WIDE):
        cols = pl.ds(WIDE * j, WIDE)
        act, slope = gelu_parts(dot(normed, w1[:, cols]), True)
        s_down[cols, :] = dot_at(act.astype(bf16), d_low)
        d_exp = (dot_bt(d_low, w2[cols, :]) * slope).astype(bf16)
        s_up[:, cols] = dot_at(normed, d_exp)
        part = dot_bt(d_exp, w1[:, cols])
        d_normed = part if d_normed is None else d_normed + part
    back, gain = norm_back(hat, inv, gains[1:2, :], d_normed)
    s_gain[...] = jnp.zeros((8, D), f32)
    s_gain[0:1, :] = gain
    d_mid[...] = d + back
    if packed:
        pack_blocks(me[0], keep, send, [(s_up, 24), (s_down, 96)], [])


def backward_shapes(packed, slopes, chunk):
    if packed:
        return chunk_shapes(chunk), [pltpu.VMEM(shape, f32) for shape in slopes]
    return [jax.ShapeDtypeStruct(shape, f32) for shape in slopes], []


def layer_zero_mlp_back(delta, mid, net, gains, me):
    packed = net["fast"]
    weights = (net["arrays"][0], net["natural"][0]) if packed else net["arrays"][2:4]
    slopes, scratch = backward_shapes(packed, [(D, FF), (FF, D)], 1)
    scalar = [pl.BlockSpec(memory_space=pltpu.SMEM)] if packed else []
    return pl.pallas_call(
        lambda *refs: mlp_back_kernel(packed, *refs),
        in_specs=[whole()] * 5 + scalar,
        out_specs=[whole()] * (2 + len(slopes)),
        out_shape=[jax.ShapeDtypeStruct(delta.shape, f32), jax.ShapeDtypeStruct((8, D), f32)] + slopes,
        scratch_shapes=scratch,
        compiler_params=pltpu.CompilerParams(vmem_limit_bytes=megabytes(LIMITS[3])),
        cost_estimate=cost(12),
        name="layer_zero_mlp_back",
    )(delta, mid, gains, *weights, *([me] if packed else []))


def attention_back_kernel(count, d_mid, mix, share, att, wo, s_out, dmix, d_att):
    d_low = d_mid[...].astype(bf16)
    s_out[...] = dot_at(att[...], d_low)
    d_att[...] = dot_bt(d_low, wo[...]).astype(bf16)
    masks = half_masks()
    for g in range(count):
        rows = pl.ds(g * ROWS, ROWS)
        for pair in range(HEADS // 2):
            lanes = [pl.ds(D * part + 128 * pair, 128) for part in range(3)]
            query = mix[rows, lanes[0]] * jnp.asarray(SCALE, bf16)
            keys = mix[rows, lanes[1]] * jnp.asarray(SCALE, bf16)
            values = mix[rows, lanes[2]]
            upstream = d_att[rows, lanes[0]]
            dq = dk = dv = None
            for half in range(2):
                p = share[g, 2 * pair + half]
                up = upstream * masks[half]
                d_p = dot_bt(values, up)
                p_wide = p.astype(f32)
                weighted = p_wide * d_p
                d_s = (weighted - p_wide * jnp.sum(weighted, 0, keepdims=True)).astype(bf16)
                parts = (
                    dot_at(d_s, keys * masks[half]),
                    dot(d_s, query * masks[half]),
                    dot(p, up),
                )
                dq, dk, dv = parts if dq is None else (dq + parts[0], dk + parts[1], dv + parts[2])
            dmix[rows, lanes[0]] = dq.astype(bf16)
            dmix[rows, lanes[1]] = dk.astype(bf16)
            dmix[rows, lanes[2]] = dv.astype(bf16)


def layer_zero_attention_back(d_mid, mix, share, att, net):
    packed = net["packed"]
    count, rows = share.shape[0], d_mid.shape[0]

    def kernel(d_mid, mix, share, att, weight, *outs):
        wo = layer_views((weight,), True, 0)[1] if packed else weight.at[pl.ds(0, D)]
        attention_back_kernel(count, d_mid, mix, share, att, wo, *outs)

    return pl.pallas_call(
        kernel,
        in_specs=[whole()] * 5,
        out_specs=[whole()] * 2,
        out_shape=[jax.ShapeDtypeStruct((D, D), f32), jax.ShapeDtypeStruct((rows, 3 * D), bf16)],
        scratch_shapes=[pltpu.VMEM((rows, D), bf16)],
        compiler_params=pltpu.CompilerParams(vmem_limit_bytes=megabytes(LIMITS[4])),
        cost_estimate=cost(10),
        name="layer_zero_attention_back",
    )(d_mid, mix, share, att, net["arrays"][0 if packed else 1])


def input_back_kernel(packed, *refs):
    (d_mid, state, dmix, pats, s_out, mixes, gains, gain_two, gain_one) = refs[:9]
    if packed:
        me, keep, send, s_in, s_patch, s_vector = refs[9:]
        win = layer_views((mixes,), True, 0)[0]
    else:
        s_in, s_patch, s_vector = refs[9:]
        win = mixes.at[pl.ds(0, D)]
    hat, inv = normalize(state[...])
    normed = (hat * gains[0:1, :]).astype(bf16)
    s_in[...] = dot_at(normed, dmix[...])
    back, gain = norm_back(hat, inv, gains[0:1, :], dot_bt(dmix[...], win[...]))
    d_state = d_mid[...] + back
    table = patch = None
    groups, per = pats.shape[:2]
    for g in range(groups * per):
        one = d_state[g * ROWS : (g + 1) * ROWS]
        part = dot_at(pats[g // per, g % per], one[:PATCHES].astype(bf16))
        table = one if table is None else table + one
        patch = part if patch is None else patch + part
    s_patch[...] = patch
    s_vector[0:ROWS, :] = table
    s_vector[ROWS:, :] = jnp.zeros((VECTORS - ROWS, D), f32)
    s_vector[ROWS : ROWS + 1, :] = gain
    s_vector[ROWS + 1 : ROWS + 2, :] = gain_two[0:1, :]
    s_vector[ROWS + 2 : ROWS + 5, :] = gain_one[0:3, :]
    if packed:
        pack_blocks(me[0], keep, send, [(s_in, 24), (s_out, 24)], [(s_patch, 24), (s_vector, 8)])


def layer_zero_input_back(d_mid, state, dmix, patches, s_out, net, gains, gain_two, gain_one, me):
    packed = net["fast"]
    slopes, scratch = backward_shapes(packed, [(D, 3 * D), (PATCH_DIM, D), (VECTORS, D)], 2)
    scalar = [pl.BlockSpec(memory_space=pltpu.SMEM)] if packed else []
    return pl.pallas_call(
        lambda *refs: input_back_kernel(packed, *refs),
        in_specs=[whole()] * 9 + scalar,
        out_specs=[whole()] * len(slopes),
        out_shape=slopes,
        scratch_shapes=scratch,
        compiler_params=pltpu.CompilerParams(vmem_limit_bytes=megabytes(LIMITS[6])),
        cost_estimate=cost(6),
        name="layer_zero_input_back",
    )(d_mid, state, dmix, patches, s_out, net["arrays"][0], gains, gain_two, gain_one, *([me] if packed else []))


VECTORS = 256


NAMES = ("mix", "out", "up", "down", "patch", "protos")
WIDTHS = {"up": FF, "down": FF, "patch": D, "mix": 3 * D, "out": D, "protos": D, "rest": 128}
PLACE = {}
COLUMNS = 0
for _key in WIDTHS:
    PLACE[_key] = COLUMNS
    COLUMNS += WIDTHS[_key]


def pack_pieces(values):
    pieces = {name: values[name] for name in ("mix", "out", "up", "patch")}
    r = values["patch"].shape[0]
    down, protos = values["down"], values["protos"]
    pieces["down"] = jnp.concatenate([down[r * j : r * (j + 1)] for j in range(4)], 1)
    pieces["protos"] = protos[:r]
    pieces["rest"] = jnp.concatenate([protos[r:, 128 * j : 128 * (j + 1)] for j in range(3)], 0)
    return pieces


def pack_kernel(*refs):
    for net in range(2):
        out = refs[12 + net]
        values = {name: ref[...].astype(f32) for name, ref in zip(NAMES, refs[6 * net : 6 * net + 6])}
        for name, piece in pack_pieces(values).items():
            out[:, pl.ds(PLACE[name], WIDTHS[name])] = piece.astype(bf16)


THIRDS = ((0, 1792), (1792, 3584), (3584, 5504))


def chain_gather(mine):
    got = swap(mine, 4)
    arrays = [jnp.stack([mine[:, a:b], got[:, a:b]]) for a, b in THIRDS]
    for stage in (1, 2, 3):
        got = [swap(arrays[path], BITS[PATHS[path][stage]]) for path in range(3)]
        arrays = [jnp.concatenate([a, g], 0) for a, g in zip(arrays, got)]
    return arrays, [swap(a, 0) for a in arrays]


CHIPS_A_STEP = 4


def unpack_kernel(me, *refs):
    ins, outs = refs[: 6 * CHIPS_A_STEP], dict(zip(NAMES, refs[6 * CHIPS_A_STEP :]))
    first_core = (me[0] & 1) == 0
    pieces = {name: [] for name in NAMES}
    for chip in range(CHIPS_A_STEP):
        mine, got = ins[6 * chip : 6 * chip + 3], ins[6 * chip + 3 : 6 * chip + 6]
        own = jnp.concatenate([ref[0].astype(f32) for ref in mine], 1)
        other = jnp.concatenate([ref[0].astype(f32) for ref in got], 1)
        for rows in (jnp.where(first_core, own, other), jnp.where(first_core, other, own)):
            for name in ("mix", "out", "up", "patch"):
                pieces[name].append(rows[:, PLACE[name] : PLACE[name] + WIDTHS[name]])
            for j in range(4):
                pieces["down"].append(rows[:, PLACE["down"] + D * j : PLACE["down"] + D * (j + 1)])
            rest = rows[:, PLACE["rest"] :]
            pieces["protos"].append(rows[:, PLACE["protos"] : PLACE["protos"] + D])
            pieces["protos"].append(jnp.concatenate([rest[8 * j : 8 * (j + 1)] for j in range(3)], 1))
    for name in NAMES:
        outs[name][...] = jnp.concatenate(pieces[name], 0).astype(bf16)


def unpack_weights(arrays, got, me):
    def index(chip, path):
        def at(i, me_ref):
            other = (CHIPS_A_STEP * i + chip) ^ (me_ref[0] >> 1)
            place = (other >> 3) & 1
            for k in range(3):
                place = place + (((other >> (BITS[PATHS[path][k + 1]] - 1)) & 1) << (k + 1))
            return place, 0, 0

        return at

    in_specs, operands = [], []
    for chip in range(CHIPS_A_STEP):
        for source in (arrays, got):
            for path in range(3):
                in_specs.append(pl.BlockSpec((1,) + source[path].shape[1:], index(chip, path)))
                operands.append(source[path])
    shapes = ((2 * D, 3 * D), (2 * D, D), (2 * D, FF), (2 * FF, D), (PATCH_DIM, D), (PROTOS, D))
    steps = 16 // CHIPS_A_STEP
    return pl.pallas_call(
        unpack_kernel,
        grid_spec=pltpu.PrefetchScalarGridSpec(
            num_scalar_prefetch=1,
            grid=(steps,),
            in_specs=in_specs,
            out_specs=[pl.BlockSpec((a // steps, b), lambda i, me_ref: (i, 0)) for a, b in shapes],
        ),
        out_shape=[jax.ShapeDtypeStruct(shape, bf16) for shape in shapes],
        compiler_params=pltpu.CompilerParams(dimension_semantics=("arbitrary",), vmem_limit_bytes=megabytes(LIMITS[5])),
        cost_estimate=cost(9),
        name="unpack_weights",
    )(me, *operands)


def natural_net(mix, out, up, down, patch, protos, fast):
    return {"packed": False, "fast": fast, "arrays": (mix, out, up, down, patch, protos)}


def gathered_net(full):
    return {"packed": True, "fast": True, "arrays": (full,)}


def plain_net(full, n):
    r = full.shape[0] // n
    part = lambda name: full[:, PLACE[name] : PLACE[name] + WIDTHS[name]]
    down = part("down").reshape(n, r, 4, D).transpose(0, 2, 1, 3).reshape(2 * FF, D)
    rest = part("rest").reshape(n, 3, r // 3, 128).transpose(0, 2, 1, 3).reshape(n, r // 3, D)
    protos = jnp.concatenate([part("protos").reshape(n, r, D), rest], 1).reshape(PROTOS, D)
    return natural_net(part("mix"), part("out"), part("up"), down, part("patch"), protos, False)


def gather_networks(student, teacher, me, n):
    gather = lambda rows: lax.all_gather(rows, "dp", axis=0, tiled=True)
    r = student[0].shape[0]
    if n != 32:
        nets = []
        for shards in (student, teacher):
            pieces = pack_pieces(dict(zip(NAMES, shards)))
            nets.append(plain_net(gather(jnp.concatenate([pieces[name].astype(bf16) for name in WIDTHS], 1)), n))
        return nets
    student_rows, teacher_rows = pl.pallas_call(
        pack_kernel,
        in_specs=[whole()] * 12,
        out_specs=[whole()] * 2,
        out_shape=[jax.ShapeDtypeStruct((r, COLUMNS), bf16)] * 2,
        cost_estimate=cost(2),
        name="pack_weights",
    )(*student, *teacher)
    full = gather(student_rows)
    arrays, got = chain_gather(teacher_rows)
    return gathered_net(full), natural_net(*unpack_weights(arrays, got, me), True)


def swap(value, bit):
    size = lax.axis_size("dp")
    return lax.ppermute(value, "dp", [(i, i ^ (1 << bit)) for i in range(size)])


def after(value, other):
    value, other = lax.optimization_barrier((value, other))
    return value, other


def core_stage(keep, send, other=None):
    got = swap(send, 0)
    if other is not None:
        keep, other = after(keep, other)
    total = (keep.astype(f32) + got.astype(f32)).astype(bf16)
    return total if other is None else (total, other)


def halves(total):
    return [(total[path, :4], total[path, 4:]) for path in range(3)]


def axis_stage(stage, arrays, other=None):
    got = [swap(arrays[path][1], BITS[PATHS[path][stage]]) for path in range(3)]
    kept = [keep for keep, _ in arrays]
    if other is not None:
        kept, other = after(kept, other)
    total = [kept[path].astype(f32) + got[path].astype(f32) for path in range(3)]
    if stage == 3:
        return jnp.concatenate(total, 0)
    half = total[0].shape[0] // 2
    total = [t.astype(bf16) for t in total]
    arrays = [(t[:half], t[half:]) for t in total]
    return arrays if other is None else (arrays, other)


def last_stage(one, zero, me):
    upper = (me[0] >> 4) == 1
    keep = jnp.concatenate([jnp.where(upper, one[:, :288], zero[:, :288]), one[:, 288:320], zero[:, 288:320]], 1)
    send = jnp.concatenate([jnp.where(upper, zero[:, :288], one[:, :288]), one[:, 320:], zero[:, 320:]], 1)
    return keep, swap(send.astype(bf16), 4)


def square_sum(value):
    return jnp.sum(jnp.sum(value * value, -1, keepdims=True), 0, keepdims=True)


def three_parts(value):
    high = value.astype(bf16).astype(f32)
    middle = (value - high).astype(bf16).astype(f32)
    return high, middle, value - high - middle


def collect_kernel(*refs):
    (keep, got, report) = refs[:3]
    (mix, out, up, down, patch, protos, line) = refs[3:]
    vectors = []
    for path in range(3):
        a = keep[path] + got[path].astype(f32)
        lanes = pl.ds(128 * path, 128)
        for j in range(3):
            mix[:, pl.ds(D * j + 128 * path, 128)] = a[24 * j : 24 * (j + 1)]
        out[:, lanes] = a[72:96]
        for j in range(4):
            up[:, pl.ds(D * j + 128 * path, 128)] = a[96 + 24 * j : 120 + 24 * j]
        down[:, lanes] = a[192:288]
        protos[:, lanes] = a[288:320]
        patch[:, lanes] = a[320:344]
        vectors.append(a[344:352])
    write_line(line, (mix, out, up, down, patch, protos), jnp.concatenate(vectors, 1), report)


def write_line(line, slopes, vectors, report):
    squares = square_sum(vectors)
    for ref in slopes:
        squares = squares + square_sum(ref[...])
    cross = report[0:1, 0:1]
    rows = vectors.shape[0]
    lane = lax.broadcasted_iota(jnp.int32, (rows, 128), 1)
    row = lax.broadcasted_iota(jnp.int32, (rows, 128), 0)
    tail = jnp.zeros((rows, 128), f32)
    for i, part in enumerate(three_parts(squares) + three_parts(cross)):
        tail = jnp.where(jnp.logical_and(lane == i, row == 0), part, tail)
    full = jnp.concatenate([vectors, tail], 1).astype(bf16)
    for d in range(line.shape[0]):
        line[d] = full


RATES = (matrix_rate,) * 5 + (table_rate,) * 2


def update_kernel(rows, *refs):
    (fixes, report, arrived), refs = refs[:3], refs[3:]
    slopes, masters, firsts, seconds = refs[:6], refs[6:13], refs[13:20], refs[20:27]
    news, moments, squares, scalars, vector = refs[27:34], refs[34:41], refs[41:48], refs[48:50], refs[50]
    tail = jnp.zeros((1, 128), f32)
    for d in range(arrived.shape[0]):
        tail = tail + arrived[d, 0:1, pl.ds(D, 128)].astype(f32)
    lane = lax.broadcasted_iota(jnp.int32, (1, 128), 1)
    norm = jnp.sqrt(jnp.sum(jnp.where(lane < 3, tail, 0.0), -1, keepdims=True))
    cross = jnp.sum(jnp.where(jnp.logical_and(lane >= 3, lane < 6), tail, 0.0), -1, keepdims=True)
    loss = cross + report[0:1, 1:2]
    scalars[0][...] = loss
    scalars[1][...] = norm
    factor = jnp.minimum(1.0, clip_limit / (norm + 1e-06))
    per_device = arrived.shape[1]
    table = jnp.concatenate([arrived[d, :, pl.ds(0, D)].astype(f32) for d in range(arrived.shape[0])], 0)
    vector[0:1, :] = table[CLS : CLS + 1]
    vector[1:SEQ, :] = table[:PATCHES]
    vector[SEQ:VROWS, :] = table[ROWS : ROWS + 5]
    scale_one, scale_two = 1.0 / fixes[0], 1.0 / fixes[1]
    order = (0, 1, 2, 3, 4, None, 5)
    for i in range(7):
        slope = vector if order[i] is None else slopes[order[i]]
        clipped = slope[...] * factor
        moment = beta_one * firsts[i][...] + (1.0 - beta_one) * clipped
        square = beta_two * seconds[i][...] + (1.0 - beta_two) * clipped * clipped
        stepped = (moment * scale_one) / (jnp.sqrt(square * scale_two) + adam_floor)
        weight = masters[i][...]
        news[i][...] = weight - RATES[i] * (stepped + decay_rate * weight)
        moments[i][...] = moment
        squares[i][...] = square


def update_rows(slopes, arrived, report, masters, firsts, seconds, fixes):
    shapes = [jax.ShapeDtypeStruct(w.shape, f32) for w in masters]
    out_shape = shapes * 3 + [jax.ShapeDtypeStruct((1, 1), f32)] * 2
    return pl.pallas_call(
        lambda *refs: update_kernel(None, *refs),
        in_specs=[pl.BlockSpec(memory_space=pltpu.SMEM)] + [whole()] * 29,
        out_specs=[whole()] * len(out_shape),
        out_shape=out_shape,
        scratch_shapes=[pltpu.VMEM((VROWS, D), f32)],
        compiler_params=pltpu.CompilerParams(vmem_limit_bytes=megabytes(LIMITS[5])),
        cost_estimate=cost(4),
        name="update_rows",
    )(fixes, report, arrived, *slopes, *masters, *firsts, *seconds)


def update_plain(slopes, arrived, report, masters, firsts, seconds, fixes):
    tail = jnp.sum(arrived[:, 0, D:].astype(f32), 0)
    table = arrived[:, :, :D].astype(f32).reshape(-1, D)
    vector = jnp.concatenate([table[CLS : CLS + 1], table[:PATCHES], table[ROWS : ROWS + 5]], 0)
    norm = jnp.sqrt(tail[0] + tail[1] + tail[2])
    loss = tail[3] + tail[4] + tail[5] + report[0, 1]
    factor = jnp.minimum(1.0, clip_limit / (norm + 1e-06))
    slopes = list(slopes[:5]) + [vector, slopes[5]]
    news, moments, squares = ([], [], [])
    for weight, first, second, slope, rate in zip(masters, firsts, seconds, slopes, RATES):
        clipped = slope * factor
        moment = beta_one * first + (1.0 - beta_one) * clipped
        square = beta_two * second + (1.0 - beta_two) * clipped * clipped
        stepped = moment / fixes[0] / (jnp.sqrt(square / fixes[1]) + adam_floor)
        news.append(weight - rate * (stepped + decay_rate * weight))
        moments.append(moment)
        squares.append(square)
    return (*news, *moments, *squares, loss[None, None], norm[None, None])


def collect(keep, got, report, n, r):
    shapes = [(r, 3 * D), (r, D), (r, FF), (4 * r, D), (r, D), (4 * r // 3, D)]
    out_shape = [jax.ShapeDtypeStruct(shape, f32) for shape in shapes] + [jax.ShapeDtypeStruct((n, VECTORS // n, 512), bf16)]
    *slopes, line = pl.pallas_call(
        collect_kernel,
        in_specs=[whole()] * 3,
        out_specs=[whole()] * len(out_shape),
        out_shape=out_shape,
        compiler_params=pltpu.CompilerParams(vmem_limit_bytes=megabytes(LIMITS[5])),
        cost_estimate=cost(3),
        name="collect_gradients",
    )(keep, got, report)
    return slopes, line


def collect_plain(one, mlp, rest, report, n):
    mix1, out1, up1, down1, protos = one
    up0, down0 = mlp
    mix0, out0, patch, vectors = rest
    scatter = lambda *v: lax.psum_scatter(jnp.concatenate(v, 0), "dp", scatter_dimension=0, tiled=True)
    slopes = [scatter(mix0, mix1), scatter(out0, out1), scatter(up0, up1), scatter(down0, down1), scatter(patch), scatter(protos)]
    vectors = scatter(vectors)
    squares = sum(jnp.sum(s * s) for s in slopes) + jnp.sum(vectors * vectors)
    tail = jnp.stack(three_parts(squares) + three_parts(report[0, 0]))
    tail = jnp.zeros((vectors.shape[0], 128), f32).at[0, :6].set(tail)
    line = jnp.concatenate([vectors, tail], 1).astype(bf16)
    return slopes, jnp.broadcast_to(line[None], (n,) + line.shape)


def local(
    attention_in, attention_out, hidden_in, hidden_out, patch_weight, vector_rows, prototypes,
    first_attention_in, first_attention_out, first_hidden_in, first_hidden_out, first_patch_weight, first_vector_rows, first_prototypes,
    second_attention_in, second_attention_out, second_hidden_in, second_hidden_out, second_patch_weight, second_vector_rows, second_prototypes,
    teacher_attention_in, teacher_attention_out, teacher_hidden_in, teacher_hidden_out, teacher_patch_weight, teacher_vector_rows, teacher_prototypes,
    anchor_patches, target_patches, patch_keep, step_count,
):
    n = lax.axis_size("dp")
    me = lax.axis_index("dp").astype(jnp.int32)[None]
    groups, per = anchor_patches.shape[:2]
    count = groups * per
    inverse_count = 1.0 / (count * n)
    masters = (attention_in, attention_out, hidden_in, hidden_out, patch_weight, vector_rows, prototypes)
    firsts = (first_attention_in, first_attention_out, first_hidden_in, first_hidden_out, first_patch_weight, first_vector_rows, first_prototypes)
    seconds = (second_attention_in, second_attention_out, second_hidden_in, second_hidden_out, second_patch_weight, second_vector_rows, second_prototypes)
    student, teacher = gather_networks(
        (attention_in, attention_out, hidden_in, hidden_out, patch_weight, prototypes),
        (teacher_attention_in, teacher_attention_out, teacher_hidden_in, teacher_hidden_out, teacher_patch_weight, teacher_prototypes),
        me,
        n,
    )

    def table_of(rows):
        return jnp.concatenate([rows[1:SEQ], rows[0:1], jnp.zeros((ROWS - SEQ, D), f32)], 0)

    def gains_of(rows):
        zeros = jnp.zeros((5, D), f32)
        first = jnp.concatenate([rows[SEQ : SEQ + 2], jnp.zeros((6, D), f32)], 0)
        second = jnp.concatenate([rows[SEQ + 2 : SEQ + 5], zeros], 0)
        return first, second

    keep = patch_keep.reshape(count, PATCHES)
    bias = jnp.where(keep == 1, 0.0, -1000000000.0).astype(f32)
    ends = jnp.where(jnp.arange(ROWS - PATCHES) == 0, 0.0, -1000000000.0).astype(f32)
    ends = jnp.broadcast_to(ends, (count, ROWS - PATCHES))
    bias = jnp.concatenate([bias, ends], 1)[:, None]
    plain = jnp.concatenate([jnp.zeros((count, PATCHES), f32), ends], 1)[:, None]
    gains0, gains1 = gains_of(vector_rows)
    teacher_rows = teacher_vector_rows.astype(f32)
    teacher_gains0, teacher_gains1 = gains_of(teacher_rows)
    counter = step_count.astype(f32)
    fixes = jnp.stack([1.0 - beta_one**counter, 1.0 - beta_two**counter])

    (targets,) = forward(target_patches, table_of(teacher_rows), plain, teacher, teacher_gains0, teacher_gains1, False, n)
    if student["fast"]:
        targets, bias = lax.optimization_barrier((targets, bias))
    state1, state0, mix, share, att, mid, logs, sums, kv, queries, shares, att_c, mid_c, expanded, last, cls, *natural = forward(
        anchor_patches, table_of(vector_rows), bias, student, gains0, gains1, True, n)
    student["natural"] = natural
    mean_sum = lax.all_to_all(sums, "dp", 0, 0, tiled=True)
    delta, gain_one, report, *one = layer_one_back(
        (logs, targets, mean_sum, state1, kv, queries, shares, att_c, mid_c, expanded, last, cls), student, gains1, inverse_count, me)
    d_mid, gain_two, *mlp = layer_zero_mlp_back(delta, mid, student, gains0, me)
    if student["fast"]:
        one, d_mid = core_stage(*one, d_mid)
    out0, dmix = layer_zero_attention_back(d_mid, mix, share, att, student)
    if student["fast"]:
        one, dmix = axis_stage(1, halves(one), dmix)
        mlp, dmix = core_stage(*mlp, dmix)
    rest = layer_zero_input_back(d_mid, state0, dmix, anchor_patches, out0, student, gains0, gain_two, gain_one, me)
    if student["fast"]:
        one, rest = axis_stage(2, one, rest)
        mlp, rest = axis_stage(1, halves(mlp), rest)
        rest = axis_stage(1, halves(core_stage(*rest)))
        zero = [tuple(jnp.concatenate([c[:, :96], b, c[:, 96:]], 1) for b, c in zip(bs, cs)) for bs, cs in zip(mlp, rest)]
        zero, one = lax.optimization_barrier((zero, one))
        keep, got = last_stage(axis_stage(3, one), axis_stage(3, axis_stage(2, zero)), me)
        slopes, line = collect(keep, got, report, n, attention_in.shape[0])
        update = update_rows
    else:
        mix0, patch0, vectors = rest
        slopes, line = collect_plain(one, mlp, (mix0, out0, patch0, vectors), report, n)
        update = update_plain
    arrived = lax.all_to_all(line, "dp", 0, 0, tiled=True)
    *states, loss, norm = update(slopes, arrived, report, masters, firsts, seconds, fixes)
    return (loss[0, 0], norm[0, 0], *states)


def solution(mesh):
    rows, same, images = P("dp", None), P(), P(None, "dp", None, None)
    weights = (rows,) * 5 + (same, rows)
    return jax.shard_map(
        local,
        mesh=mesh,
        in_specs=weights * 4 + (images, images, P(None, "dp", None), same),
        out_specs=(same, same) + weights * 3,
        check_vma=False,
    )
```

```python
import jax
import jax.numpy as jnp
from jax import lax
from jax.experimental import pallas as pl
from jax.experimental.pallas import tpu as pltpu
from jax.sharding import PartitionSpec as P

D = 384
HEADS = 6
HEAD_DIM = 64
FF = 1536
PATCHES = 196
PATCH_DIM = 768
PROTOS = 1024
SEQ = 197
VROWS = 202
ROWS = 208
CLS = 196
WIDE = 512
CR = 16
SCALE = HEAD_DIM ** (-0.5)

student_softness = 0.04
teacher_sharpness = 0.02
clip_limit = 0.01
matrix_rate = 0.05
table_rate = 0.4
decay_rate = 0.05
beta_one = 0.9
beta_two = 0.999
adam_floor = 1e-08

f32 = jnp.float32
bf16 = jnp.bfloat16
GELU_C = 0.7978845608028654
GELU_A = 0.044715


def dot(a, b):
    return lax.dot_general(a, b, (((1,), (0,)), ((), ())), preferred_element_type=f32)


def dot_bt(a, b):
    return lax.dot_general(a, b, (((1,), (1,)), ((), ())), preferred_element_type=f32)


def dot_at(a, b):
    return lax.dot_general(a, b, (((0,), (0,)), ((), ())), preferred_element_type=f32)


def normalize(x):
    centre = x - jnp.sum(x, -1, keepdims=True) * (1.0 / D)
    spread = jnp.sum(centre * centre, -1, keepdims=True) * (1.0 / D)
    inverse = lax.rsqrt(spread + 1e-06)
    return centre * inverse, inverse


def norm_back(hat, inverse, gain, upstream):
    gain_slope = jnp.sum(upstream * hat, 0, keepdims=True)
    scaled = upstream * gain
    mean_one = jnp.sum(scaled, -1, keepdims=True) * (1.0 / D)
    mean_two = jnp.sum(scaled * hat, -1, keepdims=True) * (1.0 / D)
    return inverse * (scaled - mean_one - hat * mean_two), gain_slope


def gelu_parts(x, slope):
    square = x * x
    t = jnp.tanh(x * (GELU_C + (GELU_C * GELU_A) * square))
    half = 0.5 + 0.5 * t
    act = x * half
    if not slope:
        return act, None
    inner = GELU_C + (3.0 * GELU_C * GELU_A) * square
    return act, half + act * (1.0 - t) * inner


def half_masks():
    lane = lax.broadcasted_iota(jnp.int32, (1, 128), 1)
    first = jnp.where(lane < HEAD_DIM, 1.0, 0.0)
    return first.astype(bf16), (1.0 - first).astype(bf16)


def spot_masks():
    lane = lax.broadcasted_iota(jnp.int32, (1, 128), 1)
    return jnp.where(lane == HEAD_DIM, 1.0, 0.0).astype(bf16), jnp.where(lane == 0, 1.0, 0.0).astype(bf16)


def head_mask():
    row = lax.broadcasted_iota(jnp.int32, (CR, D), 0)
    lane = lax.broadcasted_iota(jnp.int32, (CR, D), 1)
    low = row * HEAD_DIM
    return jnp.where(jnp.logical_and(lane >= low, lane < low + HEAD_DIM), 1.0, 0.0)


def natural_down(ref, natural):
    for pair in range(8):
        rows = ref[pl.ds(48 * pair, 48), :].astype(f32)
        pieces = [rows[24 * b : 24 * (b + 1), D * j : D * (j + 1)] for b in range(2) for j in range(4)]
        natural[pl.ds(192 * pair, 192), :] = jnp.concatenate(pieces, 0).astype(bf16)


def natural_protos(ref, rest, natural):
    for pair in range(16):
        rows = ref[pl.ds(48 * pair, 48), :].astype(f32)
        tail = rest[pl.ds(48 * pair, 48), :].astype(f32)
        pieces = []
        for b in range(2):
            pieces.append(rows[24 * b : 24 * (b + 1)])
            pieces.append(jnp.concatenate([tail[24 * b + 8 * j : 24 * b + 8 * (j + 1)] for j in range(3)], 1))
        natural[pl.ds(64 * pair, 64), :] = jnp.concatenate(pieces, 0).astype(bf16)


def layer_views(weights, packed, layer):
    if packed:
        (full,) = weights
        at = lambda name: full.at[pl.ds(D * layer, D), pl.ds(PLACE[name], WIDTHS[name])]
        return tuple(at(name) for name in ("mix", "out", "up", "down"))
    mix, out, up, down = weights[:4]
    rows = pl.ds(D * layer, D)
    return mix.at[rows], out.at[rows], up.at[rows], down.at[pl.ds(FF * layer, FF)]


def forward_kernel(save, packed, count, *refs):
    (pats, tab, bias_all, key_bias_all, gains, gains_one), refs = refs[:6], refs[6:]
    weights, refs = refs[: 1 if packed else 6], refs[1 if packed else 6 :]
    group = count
    per = pats.shape[1]
    if save:
        out, first, mix, share, att, mid = refs[:6]
        class_refs, naturals = refs[6:16], refs[16:]
    else:
        share = mid = None
        (target, first, mix, att, kv, att_c, cls, out) = refs[:8]
        class_refs = (target, kv, att_c, cls)
    win, wo, w1, w2 = layer_views(weights, packed, 0)
    if packed:
        down, down_one, protos = naturals
        wp = weights[0].at[:, pl.ds(PLACE["patch"], D)]
        natural_down(w2, down)
    else:
        wp, down = weights[4], w2
    table = tab[...]
    for g in range(group):
        embedded = dot(pats[g // per, g % per], wp[...])
        first[pl.ds(g * ROWS, PATCHES), :] = embedded + table[:PATCHES]
        first[pl.ds(g * ROWS + PATCHES, ROWS - PATCHES), :] = table[PATCHES:]
    state = first[...]
    hat, _ = normalize(state)
    normed = (hat * gains[0:1, :]).astype(bf16)
    mix[...] = dot(normed, win[...]).astype(bf16)
    masks, spots = half_masks(), spot_masks()

    for g in range(group):
        rows = pl.ds(g * ROWS, ROWS)
        key_bias = key_bias_all[g]
        for pair in range(HEADS // 2):
            query = mix[rows, pl.ds(128 * pair, 128)] * jnp.asarray(SCALE, bf16)
            keys = mix[rows, pl.ds(D + 128 * pair, 128)]
            values = mix[rows, pl.ds(2 * D + 128 * pair, 128)]
            total = None
            for half in range(2):
                scores = dot_bt(keys * masks[half] + key_bias * spots[half], query * masks[half] + spots[half])
                e = jnp.exp(scores - jnp.max(scores, 0, keepdims=True))
                p = (e * (1.0 / jnp.sum(e, 0, keepdims=True))).astype(bf16)
                if save:
                    share[g, 2 * pair + half] = p
                o = dot_at(p, values * masks[half])
                total = o if total is None else total + o
            att[rows, pl.ds(128 * pair, 128)] = total.astype(bf16)
    middle = first[...] + dot(att[...], wo[...])
    if save:
        mid[...] = middle
    hat, _ = normalize(middle)
    normed = (hat * gains[1:2, :]).astype(bf16)
    result = middle
    for j in range(FF // WIDE):
        cols = pl.ds(WIDE * j, WIDE)
        a, _ = gelu_parts(dot(normed, w1[:, cols]), False)
        result = result + dot(a.astype(bf16), down[cols, :])
    out[...] = result
    win, wo, w1, w2 = layer_views(weights, packed, 1)
    if packed:
        natural_down(w2, down_one)
        natural_protos(weights[0].at[:, pl.ds(PLACE["protos"], D)], weights[0].at[:, pl.ds(PLACE["rest"], 128)], protos)
        late = (win, wo, w1, down_one, protos)
    else:
        late = (win, wo, w1, w2, weights[5])
    class_forward(save, count, out, bias_all, late, gains_one, class_refs)


def class_forward(student, count, state, bias, weights, gains, refs):
    win, wo, w1, w2, protos = weights
    if student:
        (logs, sums, kv, queries, shares, att, mid_c, expanded_out, last, cls) = refs
    else:
        (target, kv, att, cls) = refs
    hat, _ = normalize(state[...])
    normed = (hat * gains[0:1, :]).astype(bf16)
    kv[...] = dot(normed, win[:, D:]).astype(bf16)
    cls[...] = jnp.zeros((CR, D), f32)
    for g in range(count):
        cls[g : g + 1, :] = state[pl.ds(g * ROWS + CLS, 1), :]
    class_state = cls[...]
    hat, _ = normalize(class_state)
    query = dot((hat * gains[0:1, :]).astype(bf16), win[:, :D]).astype(bf16)
    if student:
        queries[...] = query
    mask = head_mask()
    for g in range(count):
        rows = pl.ds(g * ROWS, ROWS)
        spread = (jnp.broadcast_to(query[g : g + 1, :].astype(f32) * SCALE, (CR, D)) * mask).astype(bf16)
        scores = dot_bt(spread, kv[rows, pl.ds(0, D)]) + bias[g]
        e = jnp.exp(scores - jnp.max(scores, -1, keepdims=True))
        p = e * (1.0 / jnp.sum(e, -1, keepdims=True))
        if student:
            shares[g] = p
        o = dot(p.astype(bf16), kv[rows, pl.ds(D, D)])
        att[g : g + 1, :] = jnp.sum(o * mask, 0, keepdims=True)
    att[count:, :] = jnp.zeros((CR - count, D), f32)
    middle = class_state + dot(att[...].astype(bf16), wo[...])
    hat, _ = normalize(middle)
    expanded = dot((hat * gains[1:2, :]).astype(bf16), w1[...])
    act, _ = gelu_parts(expanded, False)
    result = middle + dot(act.astype(bf16), w2[...])
    if student:
        mid_c[...] = middle
        expanded_out[...] = expanded
        last[...] = result
    hat, _ = normalize(result)
    unit, _ = unit_parts(hat * gains[2:3, :])
    proto_unit, _ = unit_parts(protos[...].astype(f32))
    raw = dot_bt(unit.astype(bf16), proto_unit.astype(bf16))
    logits = raw * (1.0 / (student_softness if student else teacher_sharpness))
    logits = logits - jnp.max(logits, -1, keepdims=True)
    e = jnp.exp(logits)
    total = jnp.sum(e, -1, keepdims=True)
    if student:
        log_share = logits - jnp.log(total)
        logs[...] = log_share
        share = jnp.exp(log_share)
        row = lax.broadcasted_iota(jnp.int32, (CR, PROTOS), 0)
        per = count // 2
        lines = []
        for m in range(2):
            inside = jnp.logical_and(row >= m * per, row < (m + 1) * per)
            line = jnp.sum(jnp.where(inside, share, 0.0), 0, keepdims=True)
            lines += [line[:, 128 * k : 128 * (k + 1)] for k in range(PROTOS // 128)]
        lines = jnp.concatenate(lines, 0)
        for d in range(sums.shape[0]):
            sums[d] = lines.astype(bf16)
    else:
        target[...] = e / total


def forward(patches, table, bias, net, gains, gains_one, save, n):
    groups, group = patches.shape[:2]
    count = groups * group
    rows = count * ROWS
    packed = net["packed"]
    if save:
        out_shape = [
            jax.ShapeDtypeStruct((rows, D), f32),
            jax.ShapeDtypeStruct((rows, D), f32),
            jax.ShapeDtypeStruct((rows, 3 * D), bf16),
            jax.ShapeDtypeStruct((count, HEADS, ROWS, ROWS), bf16),
            jax.ShapeDtypeStruct((rows, D), bf16),
            jax.ShapeDtypeStruct((rows, D), f32),
            jax.ShapeDtypeStruct((CR, PROTOS), f32),
            jax.ShapeDtypeStruct((n, 16, 128), bf16),
            jax.ShapeDtypeStruct((rows, 2 * D), bf16),
            jax.ShapeDtypeStruct((CR, D), bf16),
            jax.ShapeDtypeStruct((count, CR, ROWS), f32),
            jax.ShapeDtypeStruct((CR, D), f32),
            jax.ShapeDtypeStruct((CR, D), f32),
            jax.ShapeDtypeStruct((CR, FF), f32),
            jax.ShapeDtypeStruct((CR, D), f32),
            jax.ShapeDtypeStruct((CR, D), f32),
        ]
        scratch = []
    else:
        out_shape = [jax.ShapeDtypeStruct((CR, PROTOS), f32)]
        scratch = [
            pltpu.VMEM((rows, D), f32),
            pltpu.VMEM((rows, 3 * D), bf16),
            pltpu.VMEM((rows, D), bf16),
            pltpu.VMEM((rows, 2 * D), bf16),
            pltpu.VMEM((CR, D), f32),
            pltpu.VMEM((CR, D), f32),
            pltpu.VMEM((rows, D), f32),
        ]
    if packed:
        out_shape += [jax.ShapeDtypeStruct(shape, bf16) for shape in ((FF, D), (FF, D), (PROTOS, D))]
    key_bias = jnp.broadcast_to(bias.reshape(count, ROWS, 1).astype(bf16), (count, ROWS, 128))
    operands = (patches, table, bias, key_bias, gains, gains_one, *net["arrays"])
    return pl.pallas_call(
        lambda *refs: forward_kernel(save, packed, count, *refs),
        in_specs=[whole()] * len(operands),
        out_specs=[whole()] * len(out_shape),
        out_shape=out_shape,
        scratch_shapes=scratch,
        compiler_params=pltpu.CompilerParams(vmem_limit_bytes=megabytes(LIMITS[0 if save else 1])),
        cost_estimate=cost(30),
        name="student_forward" if save else "teacher_forward",
    )(*operands)


LIMITS = [14, 18, 18, 18, 18, 10, 18]


def megabytes(count):
    return count * 1024 * 1024


def cost(micros):
    return pl.CostEstimate(flops=int(micros * 1e9), transcendentals=0, bytes_accessed=int(micros * 3e6))


def unit_parts(v):
    inverse = lax.rsqrt(jnp.sum(v * v, -1, keepdims=True) + 1e-06)
    return v * inverse, inverse


def whole():
    return pl.BlockSpec(memory_space=pltpu.VMEM)


def class_back_kernel(packed, count, inverse_count, *refs):
    (logs, target, mean_sum, state, kv, queries, shares, att, mid_c, expanded, last, cls) = refs[:12]
    if packed:
        (me, gains, full, w2, protos), refs = refs[12:17], refs[17:]
        (delta, s_gain, report, keep, send, dkv, dq_all, s_up, s_down) = refs
        s_proto, s_in, s_out = s_down.at[pl.ds(0, PROTOS)], s_up.at[:, pl.ds(0, 3 * D)], s_up.at[:, pl.ds(3 * D, D)]
        win, wo, w1, _ = layer_views((full,), True, 1)
    else:
        gains, weights = refs[12], refs[13:19]
        (delta, s_gain, report, s_in, s_out, s_up, s_down, s_proto, dkv, dq_all) = refs[19:]
        (win, wo, w1, w2), protos = layer_views(weights, False, 1), weights[5]
    mask = head_mask()
    row = lax.broadcasted_iota(jnp.int32, (CR, 1), 0)
    live = row < count
    log_share = logs[...]
    share = jnp.exp(log_share)
    targets = target[...]
    total = mean_sum[0].astype(f32)
    for device in range(1, mean_sum.shape[0]):
        total = total + mean_sum[device].astype(f32)
    lines = [jnp.concatenate([total[8 * m + k : 8 * m + k + 1] for k in range(PROTOS // 128)], 1) for m in range(2)]
    mean_share = jnp.concatenate(lines, 0) * (2.0 * inverse_count)
    log_mean = jnp.log(mean_share)
    cross = -jnp.sum(jnp.where(live, targets * log_share, 0.0), -1, keepdims=True)
    cross = jnp.sum(cross, 0, keepdims=True) * inverse_count
    entropy = jnp.sum(jnp.sum(mean_share * log_mean, -1, keepdims=True), 0, keepdims=True) * 0.5
    lane = lax.broadcasted_iota(jnp.int32, (8, 128), 1)
    report[...] = jnp.where(lane == 0, cross, jnp.where(lane == 1, entropy, 0.0))
    log_row = jnp.where(row < count // 2, log_mean[0:1, :], log_mean[1:2, :])
    slope = share - targets + share * (log_row - jnp.sum(share * log_row, -1, keepdims=True))
    slope = jnp.where(live, slope * (inverse_count / student_softness), 0.0).astype(bf16)
    hat_f, inv_f = normalize(last[...])
    summary = hat_f * gains[2:3, :]
    unit, inv_u = unit_parts(summary)
    proto = protos[...].astype(f32)
    proto_unit, inv_p = unit_parts(proto)
    d_unit = dot(slope, proto_unit.astype(bf16))
    d_proto = dot_at(slope, unit.astype(bf16))
    s_proto[...] = inv_p * (d_proto - proto_unit * jnp.sum(proto_unit * d_proto, -1, keepdims=True))
    if packed:
        pack_blocks(me[0], keep, send, [], [(s_proto, 32)], 288)
    d_summary = inv_u * (d_unit - unit * jnp.sum(unit * d_unit, -1, keepdims=True))
    d, gain_f = norm_back(hat_f, inv_f, gains[2:3, :], d_summary)
    s_gain[...] = jnp.zeros((8, D), f32)
    s_gain[2:3, :] = gain_f
    d_low = d.astype(bf16)
    act, gslope = gelu_parts(expanded[...], True)
    s_down[...] = dot_at(act.astype(bf16), d_low)
    d_exp = (dot_bt(d_low, w2[...]) * gslope).astype(bf16)
    if packed:
        pack_blocks(me[0], keep, send, [(s_down, 96)], [], 192)
    hat_m, inv_m = normalize(mid_c[...])
    s_up[...] = dot_at((hat_m * gains[1:2, :]).astype(bf16), d_exp)
    d_mid, gain_two = norm_back(hat_m, inv_m, gains[1:2, :], dot_bt(d_exp, w1[...]))
    s_gain[1:2, :] = gain_two
    if packed:
        pack_blocks(me[0], keep, send, [(s_up, 24)], [], 96)
    d_mid = d + d_mid
    d_mid_low = d_mid.astype(bf16)
    s_out[...] = dot_at(att[...].astype(bf16), d_mid_low)
    d_att = dot_bt(d_mid_low, wo[...]).astype(bf16)
    dq_all[...] = jnp.zeros((CR, D), f32)
    for g in range(count):
        rows = pl.ds(g * ROWS, ROWS)
        d_spread = (jnp.broadcast_to(d_att[g : g + 1, :].astype(f32), (CR, D)) * mask).astype(bf16)
        q_spread = (jnp.broadcast_to(queries[g : g + 1, :].astype(f32) * SCALE, (CR, D)) * mask).astype(bf16)
        p = shares[g]
        d_p = dot_bt(d_spread, kv[rows, pl.ds(D, D)])
        d_s = (p * (d_p - jnp.sum(p * d_p, -1, keepdims=True))).astype(bf16)
        dkv[rows, pl.ds(D, D)] = dot_at(p.astype(bf16), d_spread).astype(bf16)
        dkv[rows, pl.ds(0, D)] = dot_at(d_s, q_spread).astype(bf16)
        dq = dot(d_s, kv[rows, pl.ds(0, D)]) * mask
        dq_all[g : g + 1, :] = jnp.sum(dq, 0, keepdims=True) * SCALE
    dq_low = dq_all[...].astype(bf16)
    hat_c, _ = normalize(cls[...])
    s_in[:, :D] = dot_at((hat_c * gains[0:1, :]).astype(bf16), dq_low)
    hat, inv = normalize(state[...])
    s_in[:, D:] = dot_at((hat * gains[0:1, :]).astype(bf16), dkv[...])
    d_class = dot_bt(dq_low, win[:, :D])
    delta[...] = dot_bt(dkv[...], win[:, D:])
    for g in range(count):
        one = pl.ds(g * ROWS + CLS, 1)
        delta[one, :] = delta[one, :] + d_class[g : g + 1, :]
    d_state, gain_one = norm_back(hat, inv, gains[0:1, :], delta[...])
    s_gain[0:1, :] = gain_one
    delta[...] = d_state
    for g in range(count):
        one = pl.ds(g * ROWS + CLS, 1)
        delta[one, :] = delta[one, :] + d_mid[g : g + 1, :]
    if packed:
        pack_blocks(me[0], keep, send, [(s_up, 24)], [], 0)


BITS = {"c": 0, "x": 1, "y": 2, "z": 3}
PATHS = (("c", "x", "y", "z"), ("c", "y", "z", "x"), ("c", "z", "x", "y"))
LAYER_ROWS = 288
CHUNK_ROWS = (352, 192, 160)


def pack_blocks(me, keep, send, layered, wide, start=0):
    for path in range(3):
        for place in range(16):
            mask = 0
            for k in range(4):
                mask |= ((place >> (3 - k)) & 1) << BITS[PATHS[path][k]]
            owner = (me & 15) ^ mask
            pieces = []
            for ref, rows in layered:
                at = pl.ds(pl.multiple_of(owner * rows, 8), rows)
                for j in range(ref.shape[1] // D):
                    pieces.append(ref[at, pl.ds(D * j + 128 * path, 128)])
            for other in range(2):
                half = (me >> 4) ^ other
                for ref, rows in wide:
                    at = pl.ds(pl.multiple_of((half * 16 + owner) * rows, 8), rows)
                    pieces.append(ref[at, pl.ds(128 * path, 128)])
            value = jnp.concatenate(pieces, 0).astype(bf16)
            target, at = (keep, place) if place < 8 else (send, place - 8)
            target[path, at, pl.ds(start, value.shape[0]), :] = value


def chunk_shapes(chunk):
    return [jax.ShapeDtypeStruct((3, 8, CHUNK_ROWS[chunk], 128), bf16)] * 2


def layer_one_back(args, net, gains, inverse_count, me):
    count = args[6].shape[0]
    packed = net["fast"]
    weights = (net["arrays"][0], *net["natural"][1:]) if packed else net["arrays"]
    rows = count * ROWS
    slopes = [(D, 3 * D), (D, D), (D, FF), (FF, D), (PROTOS, D)]
    out_shape = [
        jax.ShapeDtypeStruct((rows, D), f32),
        jax.ShapeDtypeStruct((8, D), f32),
        jax.ShapeDtypeStruct((8, 128), f32),
    ]
    scratch = [pltpu.VMEM((rows, 2 * D), bf16), pltpu.VMEM((CR, D), f32)]
    if packed:
        out_shape += chunk_shapes(0)
        scratch += [pltpu.VMEM(shape, f32) for shape in ((D, FF), (FF, D))]
    else:
        out_shape += [jax.ShapeDtypeStruct(shape, f32) for shape in slopes]
    scalar = [pl.BlockSpec(memory_space=pltpu.SMEM)] if packed else []
    return pl.pallas_call(
        lambda *refs: class_back_kernel(packed, count, inverse_count, *refs),
        in_specs=[whole()] * 12 + scalar + [whole()] * (1 + len(weights)),
        out_specs=[whole()] * len(out_shape),
        out_shape=out_shape,
        scratch_shapes=scratch,
        compiler_params=pltpu.CompilerParams(vmem_limit_bytes=megabytes(LIMITS[2])),
        cost_estimate=cost(13),
        name="layer_one_back",
    )(*args, *([me] if packed else []), gains, *weights)


def mlp_back_kernel(packed, *refs):
    delta, mid, gains, ups, downs = refs[:5]
    w1 = layer_views((ups,), True, 0)[2] if packed else ups.at[pl.ds(0, D)]
    w2 = downs.at[pl.ds(0, FF)]
    if packed:
        me, d_mid, s_gain, keep, send, s_up, s_down = refs[5:]
    else:
        d_mid, s_gain, s_up, s_down = refs[5:]
    d = delta[...]
    d_low = d.astype(bf16)
    hat, inv = normalize(mid[...])
    normed = (hat * gains[1:2, :]).astype(bf16)
    d_normed = None
    for j in range(FF // WIDE):
        cols = pl.ds(WIDE * j, WIDE)
        act, slope = gelu_parts(dot(normed, w1[:, cols]), True)
        s_down[cols, :] = dot_at(act.astype(bf16), d_low)
        d_exp = (dot_bt(d_low, w2[cols, :]) * slope).astype(bf16)
        s_up[:, cols] = dot_at(normed, d_exp)
        part = dot_bt(d_exp, w1[:, cols])
        d_normed = part if d_normed is None else d_normed + part
    back, gain = norm_back(hat, inv, gains[1:2, :], d_normed)
    s_gain[...] = jnp.zeros((8, D), f32)
    s_gain[0:1, :] = gain
    d_mid[...] = d + back
    if packed:
        pack_blocks(me[0], keep, send, [(s_up, 24), (s_down, 96)], [])


def backward_shapes(packed, slopes, chunk):
    if packed:
        return chunk_shapes(chunk), [pltpu.VMEM(shape, f32) for shape in slopes]
    return [jax.ShapeDtypeStruct(shape, f32) for shape in slopes], []


def layer_zero_mlp_back(delta, mid, net, gains, me):
    packed = net["fast"]
    weights = (net["arrays"][0], net["natural"][0]) if packed else net["arrays"][2:4]
    slopes, scratch = backward_shapes(packed, [(D, FF), (FF, D)], 1)
    scalar = [pl.BlockSpec(memory_space=pltpu.SMEM)] if packed else []
    return pl.pallas_call(
        lambda *refs: mlp_back_kernel(packed, *refs),
        in_specs=[whole()] * 5 + scalar,
        out_specs=[whole()] * (2 + len(slopes)),
        out_shape=[jax.ShapeDtypeStruct(delta.shape, f32), jax.ShapeDtypeStruct((8, D), f32)] + slopes,
        scratch_shapes=scratch,
        compiler_params=pltpu.CompilerParams(vmem_limit_bytes=megabytes(LIMITS[3])),
        cost_estimate=cost(12),
        name="layer_zero_mlp_back",
    )(delta, mid, gains, *weights, *([me] if packed else []))


def attention_back_kernel(count, d_mid, mix, share, att, wo, s_out, dmix, d_att):
    d_low = d_mid[...].astype(bf16)
    s_out[...] = dot_at(att[...], d_low)
    d_att[...] = dot_bt(d_low, wo[...]).astype(bf16)
    masks = half_masks()
    for g in range(count):
        rows = pl.ds(g * ROWS, ROWS)
        for pair in range(HEADS // 2):
            lanes = [pl.ds(D * part + 128 * pair, 128) for part in range(3)]
            query = mix[rows, lanes[0]] * jnp.asarray(SCALE, bf16)
            keys = mix[rows, lanes[1]] * jnp.asarray(SCALE, bf16)
            values = mix[rows, lanes[2]]
            upstream = d_att[rows, lanes[0]]
            dq = dk = dv = None
            for half in range(2):
                p = share[g, 2 * pair + half]
                up = upstream * masks[half]
                d_p = dot_bt(values, up)
                p_wide = p.astype(f32)
                weighted = p_wide * d_p
                d_s = (weighted - p_wide * jnp.sum(weighted, 0, keepdims=True)).astype(bf16)
                parts = (
                    dot_at(d_s, keys * masks[half]),
                    dot(d_s, query * masks[half]),
                    dot(p, up),
                )
                dq, dk, dv = parts if dq is None else (dq + parts[0], dk + parts[1], dv + parts[2])
            dmix[rows, lanes[0]] = dq.astype(bf16)
            dmix[rows, lanes[1]] = dk.astype(bf16)
            dmix[rows, lanes[2]] = dv.astype(bf16)


def layer_zero_attention_back(d_mid, mix, share, att, net):
    packed = net["packed"]
    count, rows = share.shape[0], d_mid.shape[0]

    def kernel(d_mid, mix, share, att, weight, *outs):
        wo = layer_views((weight,), True, 0)[1] if packed else weight.at[pl.ds(0, D)]
        attention_back_kernel(count, d_mid, mix, share, att, wo, *outs)

    return pl.pallas_call(
        kernel,
        in_specs=[whole()] * 5,
        out_specs=[whole()] * 2,
        out_shape=[jax.ShapeDtypeStruct((D, D), f32), jax.ShapeDtypeStruct((rows, 3 * D), bf16)],
        scratch_shapes=[pltpu.VMEM((rows, D), bf16)],
        compiler_params=pltpu.CompilerParams(vmem_limit_bytes=megabytes(LIMITS[4])),
        cost_estimate=cost(10),
        name="layer_zero_attention_back",
    )(d_mid, mix, share, att, net["arrays"][0 if packed else 1])


def input_back_kernel(packed, *refs):
    (d_mid, state, dmix, pats, s_out, mixes, gains, gain_two, gain_one) = refs[:9]
    if packed:
        me, keep, send, s_in, s_patch, s_vector = refs[9:]
        win = layer_views((mixes,), True, 0)[0]
    else:
        s_in, s_patch, s_vector = refs[9:]
        win = mixes.at[pl.ds(0, D)]
    hat, inv = normalize(state[...])
    normed = (hat * gains[0:1, :]).astype(bf16)
    s_in[...] = dot_at(normed, dmix[...])
    back, gain = norm_back(hat, inv, gains[0:1, :], dot_bt(dmix[...], win[...]))
    d_state = d_mid[...] + back
    table = patch = None
    groups, per = pats.shape[:2]
    for g in range(groups * per):
        one = d_state[g * ROWS : (g + 1) * ROWS]
        part = dot_at(pats[g // per, g % per], one[:PATCHES].astype(bf16))
        table = one if table is None else table + one
        patch = part if patch is None else patch + part
    s_patch[...] = patch
    s_vector[0:ROWS, :] = table
    s_vector[ROWS:, :] = jnp.zeros((VECTORS - ROWS, D), f32)
    s_vector[ROWS : ROWS + 1, :] = gain
    s_vector[ROWS + 1 : ROWS + 2, :] = gain_two[0:1, :]
    s_vector[ROWS + 2 : ROWS + 5, :] = gain_one[0:3, :]
    if packed:
        pack_blocks(me[0], keep, send, [(s_in, 24), (s_out, 24)], [(s_patch, 24), (s_vector, 8)])


def layer_zero_input_back(d_mid, state, dmix, patches, s_out, net, gains, gain_two, gain_one, me):
    packed = net["fast"]
    slopes, scratch = backward_shapes(packed, [(D, 3 * D), (PATCH_DIM, D), (VECTORS, D)], 2)
    scalar = [pl.BlockSpec(memory_space=pltpu.SMEM)] if packed else []
    return pl.pallas_call(
        lambda *refs: input_back_kernel(packed, *refs),
        in_specs=[whole()] * 9 + scalar,
        out_specs=[whole()] * len(slopes),
        out_shape=slopes,
        scratch_shapes=scratch,
        compiler_params=pltpu.CompilerParams(vmem_limit_bytes=megabytes(LIMITS[6])),
        cost_estimate=cost(6),
        name="layer_zero_input_back",
    )(d_mid, state, dmix, patches, s_out, net["arrays"][0], gains, gain_two, gain_one, *([me] if packed else []))


VECTORS = 256


NAMES = ("mix", "out", "up", "down", "patch", "protos")
WIDTHS = {"up": FF, "down": FF, "patch": D, "mix": 3 * D, "out": D, "protos": D, "rest": 128}
PLACE = {}
COLUMNS = 0
for _key in WIDTHS:
    PLACE[_key] = COLUMNS
    COLUMNS += WIDTHS[_key]


def pack_pieces(values):
    pieces = {name: values[name] for name in ("mix", "out", "up", "patch")}
    r = values["patch"].shape[0]
    down, protos = values["down"], values["protos"]
    pieces["down"] = jnp.concatenate([down[r * j : r * (j + 1)] for j in range(4)], 1)
    pieces["protos"] = protos[:r]
    pieces["rest"] = jnp.concatenate([protos[r:, 128 * j : 128 * (j + 1)] for j in range(3)], 0)
    return pieces


def pack_kernel(*refs):
    for net in range(2):
        out = refs[12 + net]
        values = {name: ref[...].astype(f32) for name, ref in zip(NAMES, refs[6 * net : 6 * net + 6])}
        for name, piece in pack_pieces(values).items():
            out[:, pl.ds(PLACE[name], WIDTHS[name])] = piece.astype(bf16)


THIRDS = ((0, 1792), (1792, 3584), (3584, 5504))


def chain_gather(mine):
    got = swap(mine, 4)
    arrays = [jnp.stack([mine[:, a:b], got[:, a:b]]) for a, b in THIRDS]
    for stage in (1, 2, 3):
        got = [swap(arrays[path], BITS[PATHS[path][stage]]) for path in range(3)]
        arrays = [jnp.concatenate([a, g], 0) for a, g in zip(arrays, got)]
    return arrays, [swap(a, 0) for a in arrays]


CHIPS_A_STEP = 4


def unpack_kernel(me, *refs):
    ins, outs = refs[: 6 * CHIPS_A_STEP], dict(zip(NAMES, refs[6 * CHIPS_A_STEP :]))
    first_core = (me[0] & 1) == 0
    pieces = {name: [] for name in NAMES}
    for chip in range(CHIPS_A_STEP):
        mine, got = ins[6 * chip : 6 * chip + 3], ins[6 * chip + 3 : 6 * chip + 6]
        own = jnp.concatenate([ref[0].astype(f32) for ref in mine], 1)
        other = jnp.concatenate([ref[0].astype(f32) for ref in got], 1)
        for rows in (jnp.where(first_core, own, other), jnp.where(first_core, other, own)):
            for name in ("mix", "out", "up", "patch"):
                pieces[name].append(rows[:, PLACE[name] : PLACE[name] + WIDTHS[name]])
            for j in range(4):
                pieces["down"].append(rows[:, PLACE["down"] + D * j : PLACE["down"] + D * (j + 1)])
            rest = rows[:, PLACE["rest"] :]
            pieces["protos"].append(rows[:, PLACE["protos"] : PLACE["protos"] + D])
            pieces["protos"].append(jnp.concatenate([rest[8 * j : 8 * (j + 1)] for j in range(3)], 1))
    for name in NAMES:
        outs[name][...] = jnp.concatenate(pieces[name], 0).astype(bf16)


def unpack_weights(arrays, got, me):
    def index(chip, path):
        def at(i, me_ref):
            other = (CHIPS_A_STEP * i + chip) ^ (me_ref[0] >> 1)
            place = (other >> 3) & 1
            for k in range(3):
                place = place + (((other >> (BITS[PATHS[path][k + 1]] - 1)) & 1) << (k + 1))
            return place, 0, 0

        return at

    in_specs, operands = [], []
    for chip in range(CHIPS_A_STEP):
        for source in (arrays, got):
            for path in range(3):
                in_specs.append(pl.BlockSpec((1,) + source[path].shape[1:], index(chip, path)))
                operands.append(source[path])
    shapes = ((2 * D, 3 * D), (2 * D, D), (2 * D, FF), (2 * FF, D), (PATCH_DIM, D), (PROTOS, D))
    steps = 16 // CHIPS_A_STEP
    return pl.pallas_call(
        unpack_kernel,
        grid_spec=pltpu.PrefetchScalarGridSpec(
            num_scalar_prefetch=1,
            grid=(steps,),
            in_specs=in_specs,
            out_specs=[pl.BlockSpec((a // steps, b), lambda i, me_ref: (i, 0)) for a, b in shapes],
        ),
        out_shape=[jax.ShapeDtypeStruct(shape, bf16) for shape in shapes],
        compiler_params=pltpu.CompilerParams(dimension_semantics=("arbitrary",), vmem_limit_bytes=megabytes(LIMITS[5])),
        cost_estimate=cost(9),
        name="unpack_weights",
    )(me, *operands)


def natural_net(mix, out, up, down, patch, protos, fast):
    return {"packed": False, "fast": fast, "arrays": (mix, out, up, down, patch, protos)}


def gathered_net(full):
    return {"packed": True, "fast": True, "arrays": (full,)}


def plain_net(full, n):
    r = full.shape[0] // n
    part = lambda name: full[:, PLACE[name] : PLACE[name] + WIDTHS[name]]
    down = part("down").reshape(n, r, 4, D).transpose(0, 2, 1, 3).reshape(2 * FF, D)
    rest = part("rest").reshape(n, 3, r // 3, 128).transpose(0, 2, 1, 3).reshape(n, r // 3, D)
    protos = jnp.concatenate([part("protos").reshape(n, r, D), rest], 1).reshape(PROTOS, D)
    return natural_net(part("mix"), part("out"), part("up"), down, part("patch"), protos, False)


def gather_networks(student, teacher, me, n):
    gather = lambda rows: lax.all_gather(rows, "dp", axis=0, tiled=True)
    r = student[0].shape[0]
    if n != 32:
        nets = []
        for shards in (student, teacher):
            pieces = pack_pieces(dict(zip(NAMES, shards)))
            nets.append(plain_net(gather(jnp.concatenate([pieces[name].astype(bf16) for name in WIDTHS], 1)), n))
        return nets
    student_rows, teacher_rows = pl.pallas_call(
        pack_kernel,
        in_specs=[whole()] * 12,
        out_specs=[whole()] * 2,
        out_shape=[jax.ShapeDtypeStruct((r, COLUMNS), bf16)] * 2,
        cost_estimate=cost(2),
        name="pack_weights",
    )(*student, *teacher)
    full = gather(student_rows)
    arrays, got = chain_gather(teacher_rows)
    return gathered_net(full), natural_net(*unpack_weights(arrays, got, me), True)


def swap(value, bit):
    size = lax.axis_size("dp")
    return lax.ppermute(value, "dp", [(i, i ^ (1 << bit)) for i in range(size)])


def after(value, other):
    value, other = lax.optimization_barrier((value, other))
    return value, other


def core_stage(keep, send, other=None):
    got = swap(send, 0)
    if other is not None:
        keep, other = after(keep, other)
    total = (keep.astype(f32) + got.astype(f32)).astype(bf16)
    return total if other is None else (total, other)


def halves(total):
    return [(total[path, :4], total[path, 4:]) for path in range(3)]


def axis_stage(stage, arrays, other=None):
    got = [swap(arrays[path][1], BITS[PATHS[path][stage]]) for path in range(3)]
    kept = [keep for keep, _ in arrays]
    if other is not None:
        kept, other = after(kept, other)
    total = [kept[path].astype(f32) + got[path].astype(f32) for path in range(3)]
    if stage == 3:
        return jnp.concatenate(total, 0)
    half = total[0].shape[0] // 2
    total = [t.astype(bf16) for t in total]
    arrays = [(t[:half], t[half:]) for t in total]
    return arrays if other is None else (arrays, other)


def last_stage(one, zero, me):
    upper = (me[0] >> 4) == 1
    keep = jnp.concatenate([jnp.where(upper, one[:, :288], zero[:, :288]), one[:, 288:320], zero[:, 288:320]], 1)
    send = jnp.concatenate([jnp.where(upper, zero[:, :288], one[:, :288]), one[:, 320:], zero[:, 320:]], 1)
    return keep, swap(send.astype(bf16), 4)


def square_sum(value):
    return jnp.sum(jnp.sum(value * value, -1, keepdims=True), 0, keepdims=True)


def three_parts(value):
    high = value.astype(bf16).astype(f32)
    middle = (value - high).astype(bf16).astype(f32)
    return high, middle, value - high - middle


def collect_kernel(*refs):
    (keep, got, report) = refs[:3]
    (mix, out, up, down, patch, protos, line) = refs[3:]
    vectors = []
    for path in range(3):
        a = keep[path] + got[path].astype(f32)
        lanes = pl.ds(128 * path, 128)
        for j in range(3):
            mix[:, pl.ds(D * j + 128 * path, 128)] = a[24 * j : 24 * (j + 1)]
        out[:, lanes] = a[72:96]
        for j in range(4):
            up[:, pl.ds(D * j + 128 * path, 128)] = a[96 + 24 * j : 120 + 24 * j]
        down[:, lanes] = a[192:288]
        protos[:, lanes] = a[288:320]
        patch[:, lanes] = a[320:344]
        vectors.append(a[344:352])
    write_line(line, (mix, out, up, down, patch, protos), jnp.concatenate(vectors, 1), report)


def write_line(line, slopes, vectors, report):
    squares = square_sum(vectors)
    for ref in slopes:
        squares = squares + square_sum(ref[...])
    cross = report[0:1, 0:1]
    rows = vectors.shape[0]
    lane = lax.broadcasted_iota(jnp.int32, (rows, 128), 1)
    row = lax.broadcasted_iota(jnp.int32, (rows, 128), 0)
    tail = jnp.zeros((rows, 128), f32)
    for i, part in enumerate(three_parts(squares) + three_parts(cross)):
        tail = jnp.where(jnp.logical_and(lane == i, row == 0), part, tail)
    full = jnp.concatenate([vectors, tail], 1).astype(bf16)
    for d in range(line.shape[0]):
        line[d] = full


RATES = (matrix_rate,) * 5 + (table_rate,) * 2


def update_kernel(rows, *refs):
    (fixes, report, arrived), refs = refs[:3], refs[3:]
    slopes, masters, firsts, seconds = refs[:6], refs[6:13], refs[13:20], refs[20:27]
    news, moments, squares, scalars, vector = refs[27:34], refs[34:41], refs[41:48], refs[48:50], refs[50]
    tail = jnp.zeros((1, 128), f32)
    for d in range(arrived.shape[0]):
        tail = tail + arrived[d, 0:1, pl.ds(D, 128)].astype(f32)
    lane = lax.broadcasted_iota(jnp.int32, (1, 128), 1)
    norm = jnp.sqrt(jnp.sum(jnp.where(lane < 3, tail, 0.0), -1, keepdims=True))
    cross = jnp.sum(jnp.where(jnp.logical_and(lane >= 3, lane < 6), tail, 0.0), -1, keepdims=True)
    loss = cross + report[0:1, 1:2]
    scalars[0][...] = loss
    scalars[1][...] = norm
    factor = jnp.minimum(1.0, clip_limit / (norm + 1e-06))
    per_device = arrived.shape[1]
    table = jnp.concatenate([arrived[d, :, pl.ds(0, D)].astype(f32) for d in range(arrived.shape[0])], 0)
    vector[0:1, :] = table[CLS : CLS + 1]
    vector[1:SEQ, :] = table[:PATCHES]
    vector[SEQ:VROWS, :] = table[ROWS : ROWS + 5]
    scale_one, scale_two = 1.0 / fixes[0], 1.0 / fixes[1]
    order = (0, 1, 2, 3, 4, None, 5)
    for i in range(7):
        slope = vector if order[i] is None else slopes[order[i]]
        clipped = slope[...] * factor
        moment = beta_one * firsts[i][...] + (1.0 - beta_one) * clipped
        square = beta_two * seconds[i][...] + (1.0 - beta_two) * clipped * clipped
        stepped = (moment * scale_one) / (jnp.sqrt(square * scale_two) + adam_floor)
        weight = masters[i][...]
        news[i][...] = weight - RATES[i] * (stepped + decay_rate * weight)
        moments[i][...] = moment
        squares[i][...] = square


def update_rows(slopes, arrived, report, masters, firsts, seconds, fixes):
    shapes = [jax.ShapeDtypeStruct(w.shape, f32) for w in masters]
    out_shape = shapes * 3 + [jax.ShapeDtypeStruct((1, 1), f32)] * 2
    return pl.pallas_call(
        lambda *refs: update_kernel(None, *refs),
        in_specs=[pl.BlockSpec(memory_space=pltpu.SMEM)] + [whole()] * 29,
        out_specs=[whole()] * len(out_shape),
        out_shape=out_shape,
        scratch_shapes=[pltpu.VMEM((VROWS, D), f32)],
        compiler_params=pltpu.CompilerParams(vmem_limit_bytes=megabytes(LIMITS[5])),
        cost_estimate=cost(4),
        name="update_rows",
    )(fixes, report, arrived, *slopes, *masters, *firsts, *seconds)


def update_plain(slopes, arrived, report, masters, firsts, seconds, fixes):
    tail = jnp.sum(arrived[:, 0, D:].astype(f32), 0)
    table = arrived[:, :, :D].astype(f32).reshape(-1, D)
    vector = jnp.concatenate([table[CLS : CLS + 1], table[:PATCHES], table[ROWS : ROWS + 5]], 0)
    norm = jnp.sqrt(tail[0] + tail[1] + tail[2])
    loss = tail[3] + tail[4] + tail[5] + report[0, 1]
    factor = jnp.minimum(1.0, clip_limit / (norm + 1e-06))
    slopes = list(slopes[:5]) + [vector, slopes[5]]
    news, moments, squares = ([], [], [])
    for weight, first, second, slope, rate in zip(masters, firsts, seconds, slopes, RATES):
        clipped = slope * factor
        moment = beta_one * first + (1.0 - beta_one) * clipped
        square = beta_two * second + (1.0 - beta_two) * clipped * clipped
        stepped = moment / fixes[0] / (jnp.sqrt(square / fixes[1]) + adam_floor)
        news.append(weight - rate * (stepped + decay_rate * weight))
        moments.append(moment)
        squares.append(square)
    return (*news, *moments, *squares, loss[None, None], norm[None, None])


def collect(keep, got, report, n, r):
    shapes = [(r, 3 * D), (r, D), (r, FF), (4 * r, D), (r, D), (4 * r // 3, D)]
    out_shape = [jax.ShapeDtypeStruct(shape, f32) for shape in shapes] + [jax.ShapeDtypeStruct((n, VECTORS // n, 512), bf16)]
    *slopes, line = pl.pallas_call(
        collect_kernel,
        in_specs=[whole()] * 3,
        out_specs=[whole()] * len(out_shape),
        out_shape=out_shape,
        compiler_params=pltpu.CompilerParams(vmem_limit_bytes=megabytes(LIMITS[5])),
        cost_estimate=cost(3),
        name="collect_gradients",
    )(keep, got, report)
    return slopes, line


def collect_plain(one, mlp, rest, report, n):
    mix1, out1, up1, down1, protos = one
    up0, down0 = mlp
    mix0, out0, patch, vectors = rest
    scatter = lambda *v: lax.psum_scatter(jnp.concatenate(v, 0), "dp", scatter_dimension=0, tiled=True)
    slopes = [scatter(mix0, mix1), scatter(out0, out1), scatter(up0, up1), scatter(down0, down1), scatter(patch), scatter(protos)]
    vectors = scatter(vectors)
    squares = sum(jnp.sum(s * s) for s in slopes) + jnp.sum(vectors * vectors)
    tail = jnp.stack(three_parts(squares) + three_parts(report[0, 0]))
    tail = jnp.zeros((vectors.shape[0], 128), f32).at[0, :6].set(tail)
    line = jnp.concatenate([vectors, tail], 1).astype(bf16)
    return slopes, jnp.broadcast_to(line[None], (n,) + line.shape)


def local(
    attention_in, attention_out, hidden_in, hidden_out, patch_weight, vector_rows, prototypes,
    first_attention_in, first_attention_out, first_hidden_in, first_hidden_out, first_patch_weight, first_vector_rows, first_prototypes,
    second_attention_in, second_attention_out, second_hidden_in, second_hidden_out, second_patch_weight, second_vector_rows, second_prototypes,
    teacher_attention_in, teacher_attention_out, teacher_hidden_in, teacher_hidden_out, teacher_patch_weight, teacher_vector_rows, teacher_prototypes,
    anchor_patches, target_patches, patch_keep, step_count,
):
    n = lax.axis_size("dp")
    me = lax.axis_index("dp").astype(jnp.int32)[None]
    groups, per = anchor_patches.shape[:2]
    count = groups * per
    inverse_count = 1.0 / (count * n)
    masters = (attention_in, attention_out, hidden_in, hidden_out, patch_weight, vector_rows, prototypes)
    firsts = (first_attention_in, first_attention_out, first_hidden_in, first_hidden_out, first_patch_weight, first_vector_rows, first_prototypes)
    seconds = (second_attention_in, second_attention_out, second_hidden_in, second_hidden_out, second_patch_weight, second_vector_rows, second_prototypes)
    student, teacher = gather_networks(
        (attention_in, attention_out, hidden_in, hidden_out, patch_weight, prototypes),
        (teacher_attention_in, teacher_attention_out, teacher_hidden_in, teacher_hidden_out, teacher_patch_weight, teacher_prototypes),
        me,
        n,
    )

    def table_of(rows):
        return jnp.concatenate([rows[1:SEQ], rows[0:1], jnp.zeros((ROWS - SEQ, D), f32)], 0)

    def gains_of(rows):
        zeros = jnp.zeros((5, D), f32)
        first = jnp.concatenate([rows[SEQ : SEQ + 2], jnp.zeros((6, D), f32)], 0)
        second = jnp.concatenate([rows[SEQ + 2 : SEQ + 5], zeros], 0)
        return first, second

    keep = patch_keep.reshape(count, PATCHES)
    bias = jnp.where(keep == 1, 0.0, -1000000000.0).astype(f32)
    ends = jnp.where(jnp.arange(ROWS - PATCHES) == 0, 0.0, -1000000000.0).astype(f32)
    ends = jnp.broadcast_to(ends, (count, ROWS - PATCHES))
    bias = jnp.concatenate([bias, ends], 1)[:, None]
    plain = jnp.concatenate([jnp.zeros((count, PATCHES), f32), ends], 1)[:, None]
    gains0, gains1 = gains_of(vector_rows)
    teacher_rows = teacher_vector_rows.astype(f32)
    teacher_gains0, teacher_gains1 = gains_of(teacher_rows)
    counter = step_count.astype(f32)
    fixes = jnp.stack([1.0 - beta_one**counter, 1.0 - beta_two**counter])

    (targets,) = forward(target_patches, table_of(teacher_rows), plain, teacher, teacher_gains0, teacher_gains1, False, n)
    if student["fast"]:
        targets, bias = lax.optimization_barrier((targets, bias))
    state1, state0, mix, share, att, mid, logs, sums, kv, queries, shares, att_c, mid_c, expanded, last, cls, *natural = forward(
        anchor_patches, table_of(vector_rows), bias, student, gains0, gains1, True, n)
    student["natural"] = natural
    mean_sum = lax.all_to_all(sums, "dp", 0, 0, tiled=True)
    delta, gain_one, report, *one = layer_one_back(
        (logs, targets, mean_sum, state1, kv, queries, shares, att_c, mid_c, expanded, last, cls), student, gains1, inverse_count, me)
    d_mid, gain_two, *mlp = layer_zero_mlp_back(delta, mid, student, gains0, me)
    if student["fast"]:
        one, d_mid = core_stage(*one, d_mid)
    out0, dmix = layer_zero_attention_back(d_mid, mix, share, att, student)
    if student["fast"]:
        one, dmix = axis_stage(1, halves(one), dmix)
        mlp, dmix = core_stage(*mlp, dmix)
    rest = layer_zero_input_back(d_mid, state0, dmix, anchor_patches, out0, student, gains0, gain_two, gain_one, me)
    if student["fast"]:
        rest = core_stage(*rest)
        zero = halves(jnp.concatenate([rest[:, :, :96], mlp, rest[:, :, 96:]], 2))
        zero, one = lax.optimization_barrier((zero, one))
        zero, one = axis_stage(1, zero), axis_stage(2, one)
        zero, one = lax.optimization_barrier((zero, one))
        keep, got = last_stage(axis_stage(3, one), axis_stage(3, axis_stage(2, zero)), me)
        slopes, line = collect(keep, got, report, n, attention_in.shape[0])
        update = update_rows
    else:
        mix0, patch0, vectors = rest
        slopes, line = collect_plain(one, mlp, (mix0, out0, patch0, vectors), report, n)
        update = update_plain
    arrived = lax.all_to_all(line, "dp", 0, 0, tiled=True)
    *states, loss, norm = update(slopes, arrived, report, masters, firsts, seconds, fixes)
    return (loss[0, 0], norm[0, 0], *states)


def solution(mesh):
    rows, same, images = P("dp", None), P(), P(None, "dp", None, None)
    weights = (rows,) * 5 + (same, rows)
    return jax.shard_map(
        local,
        mesh=mesh,
        in_specs=weights * 4 + (images, images, P(None, "dp", None), same),
        out_specs=(same, same) + weights * 3,
        check_vma=False,
    )
```
